32 devices in a mesh: dp: 2 (over x), seq: 8 (over z, y), mp: 2 (over core).
Axes of the slice: x: 2, y: 2, z: 4, core: 2. Of those that a mesh axis runs over, the one named last changes fastest.
Arguments:
- inputs: bfloat16 [6144, 1024], P(('dp', 'seq')), may hold values from -6 to 6
- doc_lengths: int32 [2, 2], P('dp'), may hold values from 1 to 3072, as said below
- slopes: float32 [8], P('mp'), as said below
- norm_gain: float32 [2, 1024], replicated, may hold values from 0.25 to 1.75
- norm_bias: float32 [2, 1024], replicated, may hold values from -4 to 4
- w_qkv: bfloat16 [3, 1024, 1024], P(None, None, 'mp'), may hold values from -0.25 to 0.25
- qv_bias: float32 [2, 1024], P(None, 'mp'), may hold values from -4 to 4
- w_out: bfloat16 [1024, 1024], P('mp'), may hold values from -0.75 to 0.75
- w_up: bfloat16 [1024, 4096], P(None, 'mp'), may hold values from -0.1875 to 0.1875
- up_bias: float32 [4096], P('mp'), may hold values from -4 to 4
- w_down: bfloat16 [4096, 1024], P('mp'), may hold values from -0.09375 to 0.09375
- out_bias: float32 [2, 1024], replicated, may hold values from -4 to 4
- cotangent: bfloat16 [6144, 1024], P(('dp', 'seq')), may hold values from -6 to 6
Outputs:
- outputs: bfloat16 [6144, 1024], P(('dp', 'seq'))
- grad_inputs: float32 [6144, 1024], P(('dp', 'seq'))
- grad_norm_gain: float32 [2, 1024], replicated
- grad_norm_bias: float32 [2, 1024], replicated
- grad_qkv: float32 [3, 1024, 1024], P(None, ('dp', 'seq'), 'mp')
- grad_qv_bias: float32 [2, 1024], P(None, 'mp')
- grad_out: float32 [1024, 1024], P('mp', ('dp', 'seq'))
- grad_up: float32 [1024, 4096], P(('dp', 'seq'), 'mp')
- grad_up_bias: float32 [4096], P('mp')
- grad_down: float32 [4096, 1024], P('mp', ('dp', 'seq'))
- grad_out_bias: float32 [2, 1024], replicated
The draws below stay inside these ranges and needn't reach their ends.
Inputs may be any that keep to these rules, and one draw needn't show every extreme that they name: `doc_lengths`: each row holds the lengths of the 2 documents of one block, in order; they sum to 3072, and none is longer than min(4096, 3072). `slopes`: every slope is positive.
All inputs are finite; a program needn't handle non-finite values.
Results may differ from the reference program's by a relative error of at most 0.02.
Values may be sent and summed in bfloat16 or wider, within the bound.
No kernel may reach another device: no remote copies, remote signals or barrier semaphores. Data moves between devices by JAX's collectives and lax.ppermute only.
A program may use at most 256 MiB of HBM per device.

```python
import jax
import jax.numpy as jnp
from jax import lax

D = 1024
H = 8
HD = 128
FF = 4096
TOK_DEV = 384
UNIT = 4096
SPAN = 3072
DOCS = 2
TOKENS = 6144
N_DP = 2


def draw_doc_lengths(key, part):
    key = jax.random.fold_in(key, 11)
    order_key, cut_key = jax.random.split(key)
    whole = min(UNIT, SPAN)
    units = SPAN // whole
    shorts = units // 4
    row_keys = jax.random.split(order_key, N_DP)
    order = jax.vmap(lambda row_key: jax.random.permutation(row_key, units))(row_keys)
    short_unit = order < shorts
    cut = jax.random.randint(cut_key, (N_DP, units), 1, max(TOK_DEV // 2, 2))
    piece = whole // 6
    slot = jnp.arange(6, dtype=jnp.int32)[None, None, :]
    long_slots = jnp.where(slot == 0, whole - cut[:, :, None], jnp.where(slot == 1, cut[:, :, None], 0))
    short_slots = jnp.where(slot == 5, whole - 5 * piece, piece) + jnp.zeros((N_DP, units, 6), jnp.int32)
    slots = jnp.where(short_unit[:, :, None], short_slots, long_slots).reshape(N_DP, units * 6)
    empty = (slots == 0).astype(jnp.int32)
    ranked = jnp.argsort(empty, axis=1, stable=True)
    packed = jnp.take_along_axis(slots, ranked, axis=1)
    return packed[:, :DOCS].astype(jnp.int32)


def draw_slopes(key, part):
    key = jax.random.fold_in(key, 23)
    order_key, fast_key, slow_key = jax.random.split(key, 3)
    order = jax.random.permutation(order_key, H)
    quick = order < H // 2
    reach = min(UNIT, SPAN)
    fast = jnp.exp(jax.random.uniform(fast_key, (H,), jnp.float32, jnp.log(1.0 / 32.0), jnp.log(1.0 / 12.0)))
    slow = jnp.exp(jax.random.uniform(slow_key, (H,), jnp.float32, jnp.log(0.25 / reach), jnp.log(2.0 / reach)))
    return jnp.where(quick, fast, slow).astype(jnp.float32)


def block_levels(own_key, extent, shards, smallest, top_value):
    level = 1.0
    for dim, parts in shards:
        steps = jax.random.uniform(jax.random.fold_in(jax.random.fold_in(own_key, 6), dim), (parts,), jnp.float32, smallest / len(shards), top_value / len(shards))
        level = level * jnp.repeat(jnp.exp(steps), extent[dim] // parts).reshape((-1,) + (1,) * (len(extent) - 1 - dim))
    return level


def scatter_about(key, extent, scale, bound, cuts=(), held_as=jnp.bfloat16):
    values = scale * jax.random.normal(key, extent, jnp.float32)
    if cuts:
        values = values * block_levels(key, extent, cuts, -0.22, 0.18)
    return jnp.clip(values, -bound, bound).astype(held_as)


def setup_inputs(seed: int = 0) -> dict:
    seeds = jax.random.split(jax.random.key(seed), 14)
    return {
        "inputs": scatter_about(seeds[0], (TOKENS, D), 1.0, 6.0, ((0, 16),)),
        "doc_lengths": draw_doc_lengths(jax.random.fold_in(seeds[13], 71), 0),
        "slopes": draw_slopes(jax.random.fold_in(seeds[13], 71), 0),
        "norm_gain": jnp.clip(1.0 + 0.15 * jax.random.normal(seeds[3], (2, D), jnp.float32), 0.25, 1.75),
        "norm_bias": scatter_about(seeds[4], (2, D), 0.3, 4.0, (), jnp.float32),
        "w_qkv": scatter_about(seeds[5], (3, D, D), (D // 2) ** -0.5, 0.25, ((2, 2),)),
        "qv_bias": scatter_about(seeds[6], (2, D), 0.3, 4.0, ((1, 2),), jnp.float32),
        "w_out": scatter_about(seeds[7], (D, D), (D // 16) ** -0.5, 0.75, ((0, 2),)),
        "w_up": scatter_about(seeds[8], (D, FF), D ** -0.5, 0.1875, ((1, 2),)),
        "up_bias": scatter_about(seeds[9], (FF,), 0.3, 4.0, ((0, 2),), jnp.float32),
        "w_down": scatter_about(seeds[10], (FF, D), FF ** -0.5, 0.09375, ((0, 2),)),
        "out_bias": scatter_about(seeds[11], (2, D), 0.3, 4.0, (), jnp.float32),
        "cotangent": scatter_about(seeds[12], (TOKENS, D), 1.0, 6.0, ((0, 16),)),
    }


norm_eps = 1e-05
masked_fill = -1e+30

@jax.custom_vjp
def low(v):
    return lax.optimization_barrier(v.astype(jnp.bfloat16)).astype(jnp.float32)

@jax.custom_vjp
def low_back(v):
    return v

def low_keep(v):
    return (low(v), None)

def low_pass(kept, grad):
    return (grad,)

def back_keep(v):
    return (v, None)

def back_low(kept, grad):
    return (low(grad),)
low.defvjp(low_keep, low_pass)
low_back.defvjp(back_keep, back_low)

def layer_norm(values, scale_row, shift_row):
    centered = values - lax.optimization_barrier(jnp.mean(values, axis=-1, keepdims=True))
    spread = lax.optimization_barrier(jnp.mean(centered * centered, axis=-1, keepdims=True))
    return centered * lax.rsqrt(spread + norm_eps) * scale_row + shift_row

def doc_index(positions, bounds):
    return lax.optimization_barrier(jnp.sum((positions[:, None] >= bounds[None, :]).astype(jnp.int32), axis=1))

def stretch_attention(queries, key_rows, value_rows, lengths, slopes):
    bounds = jnp.cumsum(lengths).astype(jnp.int32)
    key_pos = jnp.arange(SPAN, dtype=jnp.int32)
    key_doc = doc_index(key_pos, bounds)

    def attend_block(row_start):
        query_part = lax.dynamic_slice_in_dim(queries, row_start, TOK_DEV, 0)
        query_pos = row_start + jnp.arange(TOK_DEV, dtype=jnp.int32)
        query_doc = lax.dynamic_slice_in_dim(key_doc, row_start, TOK_DEV, 0)
        scores = jnp.einsum('qhd,khd->hqk', query_part, key_rows, precision=lax.Precision.HIGHEST)
        distance = (query_pos[:, None] - key_pos[None, :]).astype(jnp.float32)
        scores = low_back(scores - slopes[:, None, None] * distance[None, :, :])
        allowed = ((key_pos[None, :] <= query_pos[:, None]) & (key_doc[None, :] == query_doc[:, None]))[None]
        scores = jnp.where(allowed, scores, masked_fill)
        row_top = lax.optimization_barrier(jnp.max(scores, axis=2, keepdims=True))
        weights = jnp.where(allowed, jnp.exp(scores - row_top), 0.0)
        row_total = lax.optimization_barrier(jnp.sum(weights, axis=2))
        summed = jnp.einsum('hqk,khd->qhd', low(weights), value_rows, precision=lax.Precision.HIGHEST)
        return summed / jnp.transpose(row_total)[:, :, None]
    starts = jnp.arange(SPAN // TOK_DEV, dtype=jnp.int32) * TOK_DEV
    blocks = lax.map(jax.checkpoint(attend_block), starts)
    return blocks.reshape(SPAN, H, HD)

def forward(inputs, norm_gain, norm_bias, w_qkv, qv_bias, w_out, w_up, up_bias, w_down, out_bias, doc_lengths, slopes):
    score_scale = HD ** (-0.5)
    normed_one = low(layer_norm(inputs, norm_gain[0], norm_bias[0]))
    projected = jnp.einsum('td,jde->jte', normed_one, w_qkv, precision=lax.Precision.HIGHEST)
    queries = low(low_back((projected[0] + qv_bias[0]) * score_scale))
    key_rows = low(low_back(projected[1]))
    value_rows = low(low_back(projected[2] + qv_bias[1]))
    shaped = (N_DP, SPAN, H, HD)
    attended = lax.map(lambda stretch_parts: stretch_attention(stretch_parts[0], stretch_parts[1], stretch_parts[2], stretch_parts[3], slopes), (queries.reshape(shaped), key_rows.reshape(shaped), value_rows.reshape(shaped), doc_lengths))
    attended = low(low_back(attended.reshape(TOKENS, D)))
    mixed = inputs + low_back(jnp.dot(attended, w_out, precision=lax.Precision.HIGHEST) + out_bias[0])
    normed_two = low(layer_norm(mixed, norm_gain[1], norm_bias[1]))
    hidden = low_back(jnp.dot(normed_two, w_up, precision=lax.Precision.HIGHEST) + up_bias)
    active = low(jax.nn.gelu(hidden))
    return mixed + low_back(jnp.dot(active, w_down, precision=lax.Precision.HIGHEST) + out_bias[1])

def reference(inputs, doc_lengths, slopes, norm_gain, norm_bias, w_qkv, qv_bias, w_out, w_up, up_bias, w_down, out_bias, cotangent):
    floats = (inputs.astype(jnp.float32), norm_gain, norm_bias, w_qkv.astype(jnp.float32), qv_bias, w_out.astype(jnp.float32), w_up.astype(jnp.float32), up_bias, w_down.astype(jnp.float32), out_bias)

    def closed(*params):
        return forward(*params, doc_lengths, slopes)
    result, pullback = jax.vjp(closed, *floats)
    grads = pullback(cotangent.astype(jnp.float32))
    return (result.astype(jnp.bfloat16), grads[0], grads[1], grads[2], grads[3], grads[4], grads[5], grads[6], grads[7], grads[8], grads[9])
```

```python
import functools

import jax
import jax.numpy as jnp
from jax import lax
from jax.experimental import pallas as pl
from jax.experimental.pallas import tpu as pltpu
from jax.sharding import Mesh
from jax.sharding import PartitionSpec as P

D = 1024
HD = 128
BF16 = jnp.bfloat16
F32 = jnp.float32

norm_eps = 1e-05
masked_fill = -1e30

NT = (((1,), (1,)), ((), ()))
NN = (((1,), (0,)), ((), ()))
TN = (((0,), (0,)), ((), ()))


def mm(a, b, dims=NN):
    return lax.dot_general(a, b, dims, preferred_element_type=F32)


def doc_start(docs_ref, position):
    start = jnp.zeros_like(position)
    bound = jnp.int32(0)
    for d in range(docs_ref.shape[1]):
        bound = bound + docs_ref[0, d]
        start = jnp.where(position >= bound, bound, start)
    return start


def natural_order(place_ref, own, others, groups, cols, store):
    me, col = place_ref[0], place_ref[1]
    for k in range(groups):
        z = lax.rem(me + (groups - k), groups)
        store(z, z * cols + col, own[k], True)
        for s in range(1, cols):
            there = lax.rem(col + (cols - s), cols)
            store(z, z * cols + there, others[s - 1][k], False)


def bias_tile(slope, tok):
    rows = lax.broadcasted_iota(jnp.int32, (tok, tok), 0)
    lanes = lax.broadcasted_iota(jnp.int32, (tok, tok), 1)
    return slope * (rows - lanes).astype(F32)


def valid_tile(docs_ref, key_base, query_base, tok):
    keys = key_base + lax.broadcasted_iota(jnp.int32, (tok, tok), 0)
    queries = query_base + lax.broadcasted_iota(jnp.int32, (1, tok), 1)
    return (keys <= queries) & (keys >= doc_start(docs_ref, queries))


def forward_kernel(groups, cols, tok, place_ref, docs_ref, slope_ref, *refs):
    n_other = (cols - 1) * groups
    own = refs[:groups]
    others = [refs[groups + s * groups : groups + (s + 1) * groups] for s in range(cols - 1)]
    refs = refs[groups + n_other :]
    outs, (ot_ref, lse_ref), scratch = refs[:groups], refs[groups : groups + 2], refs[groups + 2 :]
    q_s, k_s, vt_s, bias_s, acc_s = scratch
    me, col = place_ref[0], place_ref[1]
    slope = slope_ref[0]

    def store(z, block, piece, mine):
        if mine:
            q_s[z] = piece[0]
            k_s[block] = piece[1]
            vt_s[block] = piece[2].T
        else:
            k_s[block] = piece[0]
            vt_s[block] = piece[1].T

    natural_order(place_ref, own, others, groups, cols, store)
    bias_s[...] = bias_tile(slope, tok)
    for k in range(groups):
        z = lax.rem(me + k, groups)
        block = z * cols + col
        query = q_s[z]
        first = doc_start(docs_ref, block * tok)
        last = doc_start(docs_ref, block * tok + tok - 1)
        low = first // tok
        mid = jnp.clip((last + tok - 1) // tok, low, block)

        scores = mm(k_s[block], query, NT) + bias_s[...]
        scores = jnp.where(valid_tile(docs_ref, block * tok, block * tok, tok), scores, masked_fill)
        top = jnp.max(scores, axis=0, keepdims=True)
        weights = jnp.exp(scores - top)
        total = jnp.sum(weights, axis=0, keepdims=True)
        acc_s[...] = mm(vt_s[block], weights.astype(BF16))

        def step(kb, state, masked):
            top, total = state
            shift = slope * ((kb - block) * tok).astype(F32)
            scores = mm(k_s[kb], query, NT) + bias_s[...] + shift
            if masked:
                scores = jnp.where(
                    valid_tile(docs_ref, kb * tok, block * tok, tok), scores, masked_fill
                )
            new_top = jnp.maximum(top, jnp.max(scores, axis=0, keepdims=True))
            weights = jnp.exp(scores - new_top)
            rescale = jnp.exp(top - new_top)
            total = total * rescale + jnp.sum(weights, axis=0, keepdims=True)
            acc_s[...] = acc_s[...] * rescale + mm(vt_s[kb], weights.astype(BF16))
            return (new_top, total)

        state = (top, total)
        state = lax.fori_loop(low, mid, functools.partial(step, masked=True), state)
        top, total = lax.fori_loop(mid, block, functools.partial(step, masked=False), state)
        result = acc_s[...] / total
        ot_ref[z] = result
        lse_ref[z] = top + jnp.log(total)
        outs[k][...] = result.T.astype(BF16)


def backward_kernel(groups, cols, tok, place_ref, docs_ref, slope_ref, *refs):
    n_other = (cols - 1) * groups
    own = refs[:groups]
    others = [refs[groups + s * groups : groups + (s + 1) * groups] for s in range(cols - 1)]
    refs = refs[groups + n_other :]
    grads, (ot_ref, lse_ref) = refs[:groups], refs[groups : groups + 2]
    dq_refs = refs[groups + 2 : 2 * groups + 2]
    own_ref = refs[2 * groups + 2]
    refs = refs[2 * groups + 3 :]
    if cols > 1:
        other_ref, refs = refs[0], refs[1:]
    q_s, k_s, v_s, kt_s, do_s, delta_s, bias_s, dk_s, dv_s, dqt_s = refs
    me, col = place_ref[0], place_ref[1]
    slope = slope_ref[0]

    def store(z, block, piece, mine):
        if mine:
            q_s[z] = piece[0]
        key, value = (piece[1], piece[2]) if mine else (piece[0], piece[1])
        k_s[block] = key
        v_s[block] = value
        kt_s[block] = key.T

    natural_order(place_ref, own, others, groups, cols, store)
    for k in range(groups):
        z = lax.rem(me + k, groups)
        grad = grads[k][...]
        do_s[z] = grad
        delta_s[z] = jnp.sum(grad.astype(F32).T * ot_ref[z], axis=0, keepdims=True)
    bias_s[...] = bias_tile(slope, tok)
    dqt_s[...] = jnp.zeros_like(dqt_s)

    def over_keys(kb, carry):
        z_key, col_key = kb // cols, lax.rem(kb, cols)
        first_query = z_key + (col_key > col).astype(jnp.int32)
        dk_s[...] = jnp.zeros_like(dk_s)
        dv_s[...] = jnp.zeros_like(dv_s)

        def tile(z, masked):
            block = z * cols + col
            shift = slope * ((kb - block) * tok).astype(F32)
            query, grad = q_s[z], do_s[z]
            scores = mm(k_s[kb], query, NT) + bias_s[...]
            probs = jnp.exp(scores - (lse_ref[z] - shift))
            if masked:
                probs = jnp.where(valid_tile(docs_ref, kb * tok, block * tok, tok), probs, 0.0)
            dv_s[...] += mm(probs.astype(BF16), grad)
            grad_probs = mm(v_s[kb], grad, NT)
            grad_scores = (probs * (grad_probs - delta_s[z])).astype(BF16)
            dk_s[...] += mm(grad_scores, query)
            dqt_s[z] += mm(kt_s[kb], grad_scores)

        def over_queries(z, carry):
            block = z * cols + col
            first = doc_start(docs_ref, block * tok)
            last = doc_start(docs_ref, block * tok + tok - 1)
            touches = first < (kb + 1) * tok
            masked = (block == kb) | (last > kb * tok)

            @pl.when(touches & masked)
            def _():
                tile(z, True)

            @pl.when(touches & jnp.logical_not(masked))
            def _():
                tile(z, False)

            return carry

        lax.fori_loop(first_query, groups, over_queries, 0)
        k = lax.rem(z_key - me + groups, groups)
        s = lax.rem(col - col_key + cols, cols)

        @pl.when(s == 0)
        def _():
            own_ref[k, 0] = dk_s[...]
            own_ref[k, 1] = dv_s[...]

        if cols > 1:

            @pl.when(s != 0)
            def _():
                other_ref[s - 1, k, 0] = dk_s[...].astype(BF16)
                other_ref[s - 1, k, 1] = dv_s[...].astype(BF16)

        return carry

    lax.fori_loop(0, groups * cols, over_keys, 0)
    for k in range(groups):
        z = lax.rem(me + k, groups)
        dq_refs[k][...] = (dqt_s[z] * (HD**-0.5)).T.astype(BF16)


SMEM = pl.BlockSpec(memory_space=pltpu.SMEM)
VMEM = pl.BlockSpec(memory_space=pltpu.VMEM)
VMEM_BYTES = 60 * 2**20


def attend_forward(place, docs, slope, own, others, groups, cols, tok):
    flat = list(own) + [piece for column in others for piece in column]
    blocks = groups * cols
    out_shape = [jax.ShapeDtypeStruct((tok, HD), BF16)] * groups + [
        jax.ShapeDtypeStruct((groups, HD, tok), F32),
        jax.ShapeDtypeStruct((groups, 1, tok), F32),
    ]
    results = pl.pallas_call(
        functools.partial(forward_kernel, groups, cols, tok),
        out_shape=out_shape,
        in_specs=[SMEM] * 3 + [VMEM] * len(flat),
        out_specs=[VMEM] * len(out_shape),
        scratch_shapes=[
            pltpu.VMEM((groups, tok, HD), BF16),
            pltpu.VMEM((blocks, tok, HD), BF16),
            pltpu.VMEM((blocks, HD, tok), BF16),
            pltpu.VMEM((tok, tok), F32),
            pltpu.VMEM((HD, tok), F32),
        ],
        compiler_params=pltpu.CompilerParams(vmem_limit_bytes=VMEM_BYTES),
        cost_estimate=pl.CostEstimate(
            flops=2 * blocks * groups * tok * tok * HD,
            bytes_accessed=2 * (groups + 2 * blocks) * tok * HD,
            transcendentals=blocks * groups * tok * tok // 2,
        ),
        name="attend_forward",
    )(place, docs, slope, *flat)
    return results[:groups], results[groups], results[groups + 1]


def attend_backward(place, docs, slope, own, others, grads, ot, lse, groups, cols, tok):
    flat = list(own) + [piece for column in others for piece in column]
    blocks = groups * cols
    out_shape = [jax.ShapeDtypeStruct((tok, HD), BF16)] * groups + [
        jax.ShapeDtypeStruct((groups, 2, tok, HD), F32)
    ]
    if cols > 1:
        out_shape.append(jax.ShapeDtypeStruct((cols - 1, groups, 2, tok, HD), BF16))
    results = pl.pallas_call(
        functools.partial(backward_kernel, groups, cols, tok),
        out_shape=out_shape,
        in_specs=[SMEM] * 3 + [VMEM] * (len(flat) + groups + 2),
        out_specs=[VMEM] * len(out_shape),
        scratch_shapes=[
            pltpu.VMEM((groups, tok, HD), BF16),
            pltpu.VMEM((blocks, tok, HD), BF16),
            pltpu.VMEM((blocks, tok, HD), BF16),
            pltpu.VMEM((blocks, HD, tok), BF16),
            pltpu.VMEM((groups, tok, HD), BF16),
            pltpu.VMEM((groups, 1, tok), F32),
            pltpu.VMEM((tok, tok), F32),
            pltpu.VMEM((tok, HD), F32),
            pltpu.VMEM((tok, HD), F32),
            pltpu.VMEM((groups, HD, tok), F32),
        ],
        compiler_params=pltpu.CompilerParams(vmem_limit_bytes=VMEM_BYTES),
        cost_estimate=pl.CostEstimate(
            flops=5 * blocks * groups * tok * tok * HD,
            bytes_accessed=2 * (groups + 4 * blocks) * tok * HD,
            transcendentals=blocks * groups * tok * tok // 2,
        ),
        name="attend_backward",
    )(place, docs, slope, *flat, *grads, ot, lse)
    return results[:groups], results[groups], (results[groups + 1] if cols > 1 else None)


def shift(x, axis, size, k):
    return lax.ppermute(x, axis, [(i, (i + k) % size) for i in range(size)])


def swap_sum(partial):
    low = partial.astype(BF16)
    other = shift(low, "mp", 2, 1)
    return low.astype(F32) + other.astype(F32)


def pair(axis, size, bit):
    return [(i, i ^ bit) for i in range(size)]


def scatter_stages(sizes):
    n_dp, groups, cols = sizes
    stages = []
    for axis, size in (("dp", n_dp), ("sr", cols), ("sg", groups)):
        bit = 1
        while bit < size:
            stages.append((axis, size, bit))
            bit *= 2
    return stages


def scatter_rows(partial_of, sizes):
    n_dp, groups, cols = sizes
    here = {axis: lax.axis_index(axis) for axis in ("dp", "sg", "sr")}
    kept = partial_of(here["dp"])
    if n_dp > 1:
        for k in range(1, n_dp):
            sent = partial_of(lax.rem(here["dp"] + k, n_dp)).astype(BF16)
            kept = kept + shift(sent, "dp", n_dp, k).astype(F32)
    width = kept.shape[1]
    kept = kept.reshape(groups, cols, -1, width)
    dims = {"sg": 0, "sr": 1}
    for axis, size, bit in scatter_stages((1, groups, cols)):
        dim = dims[axis]
        extent = kept.shape
        now = (here[axis] // bit) % 2
        split = extent[:dim] + (extent[dim] // 2, 2) + extent[dim + 1 :]
        view = kept.reshape(split)
        mine = lax.dynamic_index_in_dim(view, now, dim + 1, keepdims=False)
        sent = lax.dynamic_index_in_dim(view, 1 - now, dim + 1, keepdims=False).astype(BF16)
        kept = mine + lax.ppermute(sent, axis, pair(axis, size, bit)).astype(F32)
    return kept.reshape(-1, width)


def sum_all(vector, sizes):
    for axis, size, bit in scatter_stages(sizes):
        vector = vector + lax.ppermute(vector, axis, pair(axis, size, bit))
    return vector


def layer_norm(values, scale_row, shift_row):
    centered = values - jnp.mean(values, axis=-1, keepdims=True)
    spread = jnp.mean(centered * centered, axis=-1, keepdims=True)
    return centered * lax.rsqrt(spread + norm_eps) * scale_row + shift_row


def body(
    sizes,
    inputs,
    doc_lengths,
    slopes,
    norm_gain,
    norm_bias,
    w_qkv,
    qv_bias,
    w_out,
    w_up,
    up_bias,
    w_down,
    out_bias,
    cotangent,
):
    n_dp, groups, cols = sizes
    tok = inputs.shape[0]
    heads = slopes.shape[0]
    width = heads * HD
    me = lax.axis_index("sg")
    col = lax.axis_index("sr")
    place = jnp.stack([me, col]).astype(jnp.int32)
    slope = lax.dynamic_slice_in_dim(slopes, me, 1, 0)
    score_scale = HD ** (-0.5)

    arrive = jnp.remainder(me - jnp.arange(heads), heads)

    input_float = inputs.astype(F32)
    normed_one_f, norm_one_back = jax.vjp(layer_norm, input_float, norm_gain[0], norm_bias[0])
    normed_one = normed_one_f.astype(BF16)
    projected = jnp.einsum(
        "td,jdhe->hjte", normed_one, w_qkv.reshape(3, D, heads, HD), preferred_element_type=F32
    )
    bias_heads = qv_bias.reshape(2, heads, HD).transpose(1, 0, 2)
    bias_three = jnp.stack([bias_heads[:, 0], jnp.zeros_like(bias_heads[:, 0]), bias_heads[:, 1]], 1)
    scale_three = jnp.array([score_scale, 1.0, 1.0], F32)[None, :, None, None]
    three = ((projected + bias_three[:, :, None, :]) * scale_three).astype(BF16)

    own = []
    for k in range(groups):
        piece = lax.dynamic_index_in_dim(three, lax.rem(me + k, groups), 0, keepdims=False)
        own.append(shift(piece, "sg", groups, k) if k else piece)
    others = [[shift(piece[1:], "sr", cols, s) for piece in own] for s in range(1, cols)]
    outs, ot, lse = attend_forward(
        place, doc_lengths, slope, own, others, groups, cols, tok
    )
    back = [shift(outs[k], "sg", groups, k) if k else outs[k] for k in range(groups)]

    def natural(pieces):
        return jnp.take(jnp.stack(pieces), arrive, axis=0).transpose(1, 0, 2).reshape(tok, width)

    attended = natural(back)
    attn_part = mm(attended, w_out)
    mixed = input_float + swap_sum(attn_part) + out_bias[0]
    normed_two_f, norm_two_back = jax.vjp(layer_norm, mixed, norm_gain[1], norm_bias[1])
    normed_two = normed_two_f.astype(BF16)
    hidden = mm(normed_two, w_up) + up_bias
    active_f, gelu_back = jax.vjp(jax.nn.gelu, hidden)
    active = active_f.astype(BF16)
    outputs = (mixed + swap_sum(mm(active, w_down)) + out_bias[1]).astype(BF16)

    grad_low = cotangent
    grad_float = cotangent.astype(F32)
    grad_hidden = gelu_back(mm(grad_low, w_down, NT))[0].astype(BF16)
    grad_mixed, gain_two, shift_two = norm_two_back(swap_sum(mm(grad_hidden, w_up, NT)))
    grad_mid = grad_float + grad_mixed
    grad_mid_low = grad_mid.astype(BF16)
    grad_attended = mm(grad_mid_low, w_out, NT).astype(BF16)
    grads = []
    for k in range(groups):
        head = lax.rem(me - k + heads, heads)
        piece = lax.dynamic_slice_in_dim(grad_attended, head * HD, HD, 1)
        grads.append(shift(piece, "sg", groups, groups - k) if k else piece)

    def rows_of(left, right):
        step = D // n_dp

        def partial_of(index):
            return mm(lax.dynamic_slice_in_dim(left, index * step, step, 1), right, TN)

        return partial_of

    grad_up = scatter_rows(rows_of(normed_two, grad_hidden), sizes)
    grad_down = scatter_rows(rows_of(grad_low, active), sizes).T
    grad_out = scatter_rows(rows_of(grad_mid_low, attended), sizes).T
    small = jnp.concatenate(
        [
            gain_two,
            shift_two,
            jnp.sum(grad_mid_low.astype(F32), axis=0),
            jnp.sum(grad_low.astype(F32), axis=0),
            jnp.sum(grad_hidden.astype(F32), axis=0),
        ]
    )
    small = sum_all(small, sizes)

    dq, dkv, dkv_other = attend_backward(
        place, doc_lengths, slope, own, others, grads, ot, lse, groups, cols, tok
    )
    for s in range(1, cols):
        dkv = dkv + shift(dkv_other[s - 1], "sr", cols, cols - s).astype(F32)
    dkv = dkv.astype(BF16)
    dq_back = [shift(dq[k], "sg", groups, k) if k else dq[k] for k in range(groups)]
    dkv_back = [shift(dkv[k], "sg", groups, k) if k else dkv[k] for k in range(groups)]
    grad_three = jnp.concatenate(
        [natural(dq_back)]
        + [natural([piece[role] for piece in dkv_back]) for role in (0, 1)],
        axis=1,
    )
    w_three = w_qkv.transpose(1, 0, 2).reshape(D, 3 * width)
    grad_input_norm, gain_one, shift_one = norm_one_back(swap_sum(mm(grad_three, w_three, NT)))
    grad_inputs = grad_mid + grad_input_norm
    grad_qkv = scatter_rows(rows_of(normed_one, grad_three), sizes)
    grad_qkv = grad_qkv.reshape(-1, 3, width).transpose(1, 0, 2)
    column_sums = jnp.sum(grad_three.astype(F32), axis=0).reshape(3, width)
    small_two = sum_all(
        jnp.concatenate([gain_one, shift_one, column_sums[0], column_sums[2]]), sizes
    )
    grad_qv_bias = small_two[2 * D :].reshape(2, width)
    return (
        outputs,
        grad_inputs,
        jnp.stack([small_two[:D], small[:D]]),
        jnp.stack([small_two[D : 2 * D], small[D : 2 * D]]),
        grad_qkv,
        grad_qv_bias,
        grad_out,
        grad_up,
        small[4 * D :],
        grad_down,
        jnp.stack([small[2 * D : 3 * D], small[3 * D : 4 * D]]),
    )


def solution(mesh):
    n_dp, n_seq, n_mp = mesh.shape["dp"], mesh.shape["seq"], mesh.shape["mp"]
    groups = 4
    cols = n_seq // groups
    inner = Mesh(mesh.devices.reshape(n_dp, groups, cols, n_mp), ("dp", "sg", "sr", "mp"))
    rows = ("dp", "sg", "sr")
    return jax.shard_map(
        functools.partial(body, (n_dp, groups, cols)),
        mesh=inner,
        in_specs=(
            P(rows, None),
            P("dp", None),
            P("mp"),
            P(),
            P(),
            P(None, None, "mp"),
            P(None, "mp"),
            P("mp", None),
            P(None, "mp"),
            P("mp"),
            P("mp", None),
            P(),
            P(rows, None),
        ),
        out_specs=(
            P(rows, None),
            P(rows, None),
            P(),
            P(),
            P(None, rows, "mp"),
            P(None, "mp"),
            P("mp", rows),
            P(rows, "mp"),
            P("mp"),
            P("mp", rows),
            P(),
        ),
        check_vma=False,
    )
```

```python
import functools
import math

import jax
import jax.numpy as jnp
from jax import lax
from jax.experimental import pallas as pl
from jax.experimental.pallas import tpu as pltpu
from jax.sharding import Mesh
from jax.sharding import PartitionSpec as P

D = 1024
HD = 128
BF16 = jnp.bfloat16
F32 = jnp.float32

norm_eps = 1e-05
masked_fill = -1e30
score_scale = HD ** (-0.5)

NT = (((1,), (1,)), ((), ()))
NN = (((1,), (0,)), ((), ()))
TN = (((0,), (0,)), ((), ()))


def mm(a, b, dims=NN):
    return lax.dot_general(a, b, dims, preferred_element_type=F32)


def doc_start(docs_ref, position):
    start = jnp.zeros_like(position)
    bound = jnp.int32(0)
    for d in range(docs_ref.shape[1]):
        bound = bound + docs_ref[0, d]
        start = jnp.where(position >= bound, bound, start)
    return start


def key_span(docs_ref, kb, z_count, cols, col, tok):
    z_key, col_key = kb // cols, lax.rem(kb, cols)
    first = z_key + (col_key > col).astype(jnp.int32)
    end = jnp.int32(0)
    barred = (col_key == col).astype(jnp.int32)
    for z in range(z_count):
        block = z * cols + col
        end = end + (doc_start(docs_ref, block * tok) < (kb + 1) * tok).astype(jnp.int32)
        late = (doc_start(docs_ref, block * tok + tok - 1) > kb * tok) & (block >= kb)
        barred = barred | late.astype(jnp.int32)
    return first, jnp.maximum(end - first, 0), barred


def column_setup(docs_ref, slope, groups, cols, col, tok, pos_s, start_s, rise_s):
    for z in range(groups):
        lanes = slice(z * tok, (z + 1) * tok)
        at = (z * cols + col) * tok + lax.broadcasted_iota(jnp.int32, (1, tok), 1)
        pos_s[:, lanes] = at
        start_s[:, lanes] = doc_start(docs_ref, at)
    rise_s[...] = slope * lax.broadcasted_iota(jnp.int32, (tok, 128), 0).astype(F32)


def widened(rise, width):
    return jnp.concatenate([rise] * (width // 128), axis=1)


def over_key_blocks(docs_ref, groups, cols, col, tok, run, none=None):
    blocks = groups * cols

    def step(i, carry):
        kb = blocks - 1 - i
        first, count, barred = key_span(docs_ref, kb, groups, cols, col, tok)
        for n in range(1, groups + 1):
            for masked in (True, False):

                @pl.when((count == n) & (barred == int(masked)))
                def _(n=n, masked=masked):
                    run(kb, pl.multiple_of(first * tok, 128), n * tok, masked)

        if none is not None:

            @pl.when(count == 0)
            def _():
                none(kb)

        return carry

    lax.fori_loop(0, blocks, step, 0)


def allowed(kb, at, start, tok, width):
    keys = kb * tok + lax.broadcasted_iota(jnp.int32, (tok, width), 0)
    return (keys <= at) & (keys >= start)


def natural_order(place_ref, n_groups, n_cols, q_refs, kv_refs, other_refs, store_query, store_key):
    me, col = place_ref[0], place_ref[1]
    for x in range(n_groups):
        z = me ^ x
        store_query(z, q_refs[x])
        store_key(z * n_cols + col, kv_refs[x])
        for s in range(1, n_cols):
            store_key(z * n_cols + (col ^ s), other_refs[(s - 1) * n_groups + x])


def block_rows(z, tok):
    return pl.ds(pl.multiple_of(z * tok, 128), tok)


def forward_kernel(groups, cols, tok, n_after, place_ref, docs_ref, slope_ref, *refs):
    n_other = (cols - 1) * groups
    q_refs, refs = refs[:groups], refs[groups:]
    kv_refs, refs = refs[:groups], refs[groups:]
    other_refs, refs = refs[:n_other], refs[n_other + n_after :]
    outs, (ot_ref, lse_ref), scratch = refs[:groups], refs[groups : groups + 2], refs[groups + 2 :]
    q_s, k_s, vt_s, pos_s, start_s, rise_s, top_s, total_s = scratch
    me, col = place_ref[0], place_ref[1]
    slope = slope_ref[me]

    def store_query(z, piece):
        q_s[block_rows(z, tok)] = piece[...]

    def store_key(block, piece):
        k_s[block] = piece[0]
        vt_s[block] = piece[1].T

    natural_order(place_ref, groups, cols, q_refs, kv_refs, other_refs, store_query, store_key)
    column_setup(docs_ref, slope, groups, cols, col, tok, pos_s, start_s, rise_s)
    top_s[...] = jnp.full(top_s.shape, masked_fill, F32)
    total_s[...] = jnp.zeros_like(total_s)
    ot_ref[...] = jnp.zeros_like(ot_ref)

    def run(kb, base, width, masked):
        lanes = pl.ds(base, width)
        at = pos_s[:, lanes]
        row = slope * (kb * tok - at).astype(F32)
        scores = mm(k_s[kb], q_s[lanes], NT) + widened(rise_s[...], width)
        if masked:
            scores = jnp.where(allowed(kb, at, start_s[:, lanes], tok, width), scores, masked_fill)
        top = jnp.maximum(top_s[:, lanes], jnp.max(scores, axis=0, keepdims=True) + row)
        weights = jnp.exp(scores - (top - row))
        rescale = jnp.exp(top_s[:, lanes] - top)
        top_s[:, lanes] = top
        total_s[:, lanes] = total_s[:, lanes] * rescale + jnp.sum(weights, axis=0, keepdims=True)
        ot_ref[:, lanes] = ot_ref[:, lanes] * rescale + mm(vt_s[kb], weights.astype(BF16))

    over_key_blocks(docs_ref, groups, cols, col, tok, run)
    total = total_s[...]
    ot_ref[...] = ot_ref[...] / total
    lse_ref[...] = top_s[...] + jnp.log(total)
    for x in range(groups):
        outs[x][...] = ot_ref[:, block_rows(me ^ x, tok)].T.astype(BF16)


def backward_kernel(groups, cols, tok, n_after, place_ref, docs_ref, slope_ref, *refs):
    n_other = (cols - 1) * groups
    q_refs, refs = refs[:groups], refs[groups:]
    kv_refs, refs = refs[:groups], refs[groups:]
    other_refs, refs = refs[:n_other], refs[n_other:]
    grads, (ot_ref, lse_ref) = refs[:groups], refs[groups : groups + 2]
    refs = refs[groups + 2 + n_after :]
    dq_refs, own_ref, refs = refs[:groups], refs[groups], refs[groups + 1 :]
    if cols > 1:
        other_ref, refs = refs[0], refs[1:]
    q_s, k_s, v_s, kt_s, do_s, pos_s, start_s, rise_s, delta_s, dqt_s = refs
    me, col = place_ref[0], place_ref[1]
    slope = slope_ref[me]

    def store_query(z, piece):
        q_s[block_rows(z, tok)] = piece[...]

    def store_key(block, piece):
        k_s[block] = piece[0]
        v_s[block] = piece[1]
        kt_s[block] = piece[0].T

    natural_order(place_ref, groups, cols, q_refs, kv_refs, other_refs, store_query, store_key)
    column_setup(docs_ref, slope, groups, cols, col, tok, pos_s, start_s, rise_s)
    for x in range(groups):
        rows = block_rows(me ^ x, tok)
        grad = grads[x][...]
        do_s[rows] = grad
        delta_s[:, rows] = jnp.sum(grad.astype(F32).T * ot_ref[:, rows], axis=0, keepdims=True)
    dqt_s[...] = jnp.zeros_like(dqt_s)

    def store(kb, dk, dv):
        x, s = (kb // cols) ^ me, lax.rem(kb, cols) ^ col

        @pl.when(s == 0)
        def _():
            own_ref[x, 0] = dk
            own_ref[x, 1] = dv

        if cols > 1:

            @pl.when(s != 0)
            def _():
                other_ref[s - 1, x, 0] = dk.astype(BF16)
                other_ref[s - 1, x, 1] = dv.astype(BF16)

    def run(kb, base, width, masked):
        lanes = pl.ds(base, width)
        at = pos_s[:, lanes]
        row = slope * (kb * tok - at).astype(F32)
        query, grad = q_s[lanes], do_s[lanes]
        scores = mm(k_s[kb], query, NT) + widened(rise_s[...], width)
        probs = jnp.exp(scores - (lse_ref[:, lanes] - row))
        if masked:
            probs = jnp.where(allowed(kb, at, start_s[:, lanes], tok, width), probs, 0.0)
        dv = mm(probs.astype(BF16), grad)
        grad_scores = (probs * (mm(v_s[kb], grad, NT) - delta_s[:, lanes])).astype(BF16)
        dk = mm(grad_scores, query)
        dqt_s[:, lanes] += mm(kt_s[kb], grad_scores)
        store(kb, dk, dv)

    def none(kb):
        store(kb, jnp.zeros((tok, HD), F32), jnp.zeros((tok, HD), F32))

    over_key_blocks(docs_ref, groups, cols, col, tok, run, none)
    for x in range(groups):
        dq_refs[x][...] = (dqt_s[:, block_rows(me ^ x, tok)] * score_scale).T.astype(BF16)


SMEM = pl.BlockSpec(memory_space=pltpu.SMEM)
VMEM = pl.BlockSpec(memory_space=pltpu.VMEM)
ANY = pl.BlockSpec(memory_space=pl.ANY)
VMEM_BYTES = 60 * 2**20
COST = 1000
HOLD = 20 * 10**9
LEAST_BYTES = 60 * 2**20
gelu_slope = (2.0 / 3.141592653589793) ** 0.5


def call(kernel, name, out_shape, specs, operands, scratch=(), after=(), room=8, flops=0, moved=0, exps=0):
    held = [*operands, *out_shape, *scratch]
    held = sum(math.prod(x.shape) * jnp.dtype(x.dtype).itemsize for x in held)
    limit = max(LEAST_BYTES, min(VMEM_BYTES, held * 9 // 8 + room * 2**20))
    results = pl.pallas_call(
        kernel,
        out_shape=out_shape,
        in_specs=list(specs) + [ANY] * len(after),
        out_specs=[VMEM] * len(out_shape),
        scratch_shapes=list(scratch),
        compiler_params=pltpu.CompilerParams(vmem_limit_bytes=limit),
        cost_estimate=pl.CostEstimate(flops=flops // COST, bytes_accessed=moved // COST, transcendentals=exps // COST),
        name=name,
    )(*operands, *after)
    return list(results)


def attend_forward(place, docs, slope, q, kv, others, groups, cols, tok, after):
    blocks = groups * cols
    operands = (place, docs, slope, *q, *kv, *others)
    out_shape = [jax.ShapeDtypeStruct((tok, HD), BF16)] * groups + [
        jax.ShapeDtypeStruct((HD, groups * tok), F32),
        jax.ShapeDtypeStruct((1, groups * tok), F32),
    ]
    results = call(
        functools.partial(forward_kernel, groups, cols, tok, len(after)),
        "attend_forward",
        out_shape,
        [SMEM] * 3 + [VMEM] * (len(operands) - 3),
        operands,
        [
            pltpu.VMEM((groups * tok, HD), BF16),
            pltpu.VMEM((blocks, tok, HD), BF16),
            pltpu.VMEM((blocks, HD, tok), BF16),
            pltpu.VMEM((1, groups * tok), jnp.int32),
            pltpu.VMEM((1, groups * tok), jnp.int32),
            pltpu.VMEM((tok, 128), F32),
            pltpu.VMEM((1, groups * tok), F32),
            pltpu.VMEM((1, groups * tok), F32),
        ],
        after,
        16,
        2 * blocks * groups * tok * tok * HD,
        2 * (groups + 2 * blocks) * tok * HD,
        blocks * groups * tok * tok // 2,
    )
    return results[:groups], results[groups], results[groups + 1]


def attend_backward(place, docs, slope, q, kv, others, grads, ot, lse, groups, cols, tok, after):
    blocks = groups * cols
    operands = (place, docs, slope, *q, *kv, *others, *grads, ot, lse)
    out_shape = [jax.ShapeDtypeStruct((tok, HD), BF16)] * groups + [
        jax.ShapeDtypeStruct((groups, 2, tok, HD), F32)
    ]
    if cols > 1:
        out_shape.append(jax.ShapeDtypeStruct((cols - 1, groups, 2, tok, HD), BF16))
    results = call(
        functools.partial(backward_kernel, groups, cols, tok, len(after)),
        "attend_backward",
        out_shape,
        [SMEM] * 3 + [VMEM] * (len(operands) - 3),
        operands,
        [
            pltpu.VMEM((groups * tok, HD), BF16),
            pltpu.VMEM((blocks, tok, HD), BF16),
            pltpu.VMEM((blocks, tok, HD), BF16),
            pltpu.VMEM((blocks, HD, tok), BF16),
            pltpu.VMEM((groups * tok, HD), BF16),
            pltpu.VMEM((1, groups * tok), jnp.int32),
            pltpu.VMEM((1, groups * tok), jnp.int32),
            pltpu.VMEM((tok, 128), F32),
            pltpu.VMEM((1, groups * tok), F32),
            pltpu.VMEM((HD, groups * tok), F32),
        ],
        after,
        24,
        14 * 10**9 * COST,
    )
    return results[:groups], results[groups], (results[groups + 1] if cols > 1 else None)


def rows_of(ref, part, size):
    return ref[pl.ds(pl.multiple_of(part * size, 16), size)]


def norm_rows(values):
    mean = jnp.mean(values, axis=-1, keepdims=True)
    centered = values - mean
    spread = jnp.mean(centered * centered, axis=-1, keepdims=True)
    return centered * lax.rsqrt(spread + norm_eps)


def mix_kernel(heads, n_after, place_ref, w_ref, *refs):
    pieces, out_ref, att_ref = refs[:heads], refs[heads + n_after], refs[heads + n_after + 1]
    for x in range(heads):
        head = place_ref[0] ^ x
        att_ref[:, pl.ds(pl.multiple_of(head * HD, HD), HD)] = pieces[x][...]
    out_ref[...] = mm(att_ref[...], w_ref[...]).astype(BF16)


def mix_heads(place, w_out, pieces, after):
    tok, heads = pieces[0].shape[0], len(pieces)
    return call(
        functools.partial(mix_kernel, heads, len(after)),
        "mix_heads",
        [jax.ShapeDtypeStruct((tok, D), BF16), jax.ShapeDtypeStruct((tok, heads * HD), BF16)],
        [SMEM] + [VMEM] * (heads + 1),
        (place, w_out, *pieces),
        after=after,
        flops=2 * tok * D * heads * HD,
        moved=2 * (tok * D + D * heads * HD),
    )


def unproject_kernel(heads, n_after, place_ref, w_ref, *refs):
    dq, dkv = refs[:heads], refs[heads : 2 * heads]
    out_ref, sum_ref, wide_s = refs[2 * heads + n_after :]
    for x in range(heads):
        head = place_ref[0] ^ x
        lanes = pl.ds(pl.multiple_of(head * HD, HD), HD)
        wide_s[0, :, lanes] = dq[x][...]
        wide_s[1, :, lanes] = dkv[x][0]
        wide_s[2, :, lanes] = dkv[x][1]
    total = mm(wide_s[0], w_ref[0], NT)
    for j in (1, 2):
        total = total + mm(wide_s[j], w_ref[j], NT)
    out_ref[...] = total.astype(BF16)
    sum_ref[0:1] = jnp.sum(wide_s[0].astype(F32), axis=0, keepdims=True)
    sum_ref[1:2] = jnp.sum(wide_s[2].astype(F32), axis=0, keepdims=True)


def unproject(place, w_qkv, dq, dkv, after):
    tok, heads = dq[0].shape[0], len(dq)
    return call(
        functools.partial(unproject_kernel, heads, len(after)),
        "unproject",
        [jax.ShapeDtypeStruct((tok, D), BF16), jax.ShapeDtypeStruct((2, heads * HD), F32)],
        [SMEM] + [VMEM] * (2 * heads + 1),
        (place, w_qkv, *dq, *dkv),
        [pltpu.VMEM((3, tok, heads * HD), BF16)],
        after=after,
        flops=6 * tok * D * heads * HD,
        moved=2 * (tok * D + 3 * D * heads * HD),
    )


def project_kernel(heads, place_ref, x_ref, gain_ref, shift_ref, w_ref, bias_ref, *refs):
    normed_ref, half_ref, q_refs, kv_refs = refs[0], refs[1], refs[2 : 2 + heads], refs[2 + heads : -1]
    out_s = refs[-1]
    normed = norm_rows(x_ref[...].astype(F32)) * gain_ref[0:1] + shift_ref[0:1]
    normed = normed.astype(BF16)
    normed_ref[...] = normed
    half_ref[...] = rows_of(normed_ref, place_ref[3], half_ref.shape[0])
    for j in range(3):
        product = mm(normed, w_ref[j])
        if j == 0:
            product = (product + bias_ref[0:1]) * score_scale
        if j == 2:
            product = product + bias_ref[1:2]
        product = product.astype(BF16)
        for h in range(heads):
            out_s[h, j] = product[:, h * HD : (h + 1) * HD]
    for x in range(heads):
        head = place_ref[0] ^ x
        q_refs[x][...] = out_s[head, 0]
        kv_refs[x][...] = out_s[head, 1:3]


def project(place, inputs, gain, shift, w_qkv, qv_bias):
    tok = inputs.shape[0]
    heads = w_qkv.shape[2] // HD
    out_shape = (
        [jax.ShapeDtypeStruct((tok, D), BF16), jax.ShapeDtypeStruct((tok // 2, D), BF16)]
        + [jax.ShapeDtypeStruct((tok, HD), BF16)] * heads
        + [jax.ShapeDtypeStruct((2, tok, HD), BF16)] * heads
    )
    results = call(
        functools.partial(project_kernel, heads),
        "project",
        out_shape,
        [SMEM] + [VMEM] * 5,
        (place, inputs, gain, shift, w_qkv, qv_bias),
        [pltpu.VMEM((heads, 3, tok, HD), BF16)],
    )
    return results[0], results[1], results[2 : 2 + heads], results[2 + heads :]


def middle_kernel(n_after, place_ref, x_ref, part_ref, other_ref, bias_ref, gain_ref, shift_ref, *refs):
    mixed_ref, normed_ref, half_ref = refs[n_after:]
    parts = part_ref[...].astype(F32) + other_ref[...].astype(F32)
    mixed = x_ref[...].astype(F32) + parts + bias_ref[0:1]
    mixed_ref[...] = mixed
    normed_ref[...] = (norm_rows(mixed) * gain_ref[1:2] + shift_ref[1:2]).astype(BF16)
    half_ref[...] = rows_of(normed_ref, place_ref[3], half_ref.shape[0])


def middle(place, inputs, part, other, out_bias, gain, shift, after=()):
    tok = inputs.shape[0]
    return call(
        functools.partial(middle_kernel, len(after)),
        "middle",
        [
            jax.ShapeDtypeStruct((tok, D), F32),
            jax.ShapeDtypeStruct((tok, D), BF16),
            jax.ShapeDtypeStruct((tok // 2, D), BF16),
        ],
        [SMEM] + [VMEM] * 6,
        (place, inputs, part, other, out_bias, gain, shift),
        after=after,
    )


def hidden_kernel(place_ref, normed_ref, half_ref, w_ref, bias_ref, grad_ref, *refs):
    act_sent, grad_sent, act_mine, grad_mine, back_ref, sum_ref = refs
    near, (tok, width) = place_ref[1] % 2, act_mine.shape
    grad_sent[tok:] = half_ref[...]
    total = None
    for act_ref, out_ref, side in ((act_sent, grad_sent, 1 - near), (act_mine, grad_mine, near)):
        cut = pl.ds(pl.multiple_of(side * width, 128), width)
        u = mm(normed_ref[...], w_ref[:, cut]) + bias_ref[:, cut]
        square = u * u
        bend = jnp.tanh(u * (gelu_slope + gelu_slope * 0.044715 * square))
        half = 0.5 + 0.5 * bend
        act_ref[...] = (u * half).astype(BF16)
        lean = u * (0.5 - 0.5 * bend * bend)
        rise = half + lean * (gelu_slope + (3 * 0.044715 * gelu_slope) * square)
        grad = (rise * grad_ref[:, cut]).astype(BF16)
        out_ref[:tok] = grad
        sum_ref[:, cut] = column_sum(grad.astype(F32))
        back = mm(grad, w_ref[:, cut], NT)
        total = back if total is None else total + back
    back_ref[...] = total.astype(BF16)


def hidden_units(place, normed, half, w_up, up_bias, grad_active, after=()):
    tok, total = normed.shape[0], w_up.shape[1]
    assert total // 2 == D
    act_sent, grad_sent, act_mine, grad_mine, back, sums = call(
        hidden_kernel,
        "hidden_units",
        [
            jax.ShapeDtypeStruct((tok, total // 2), BF16),
            jax.ShapeDtypeStruct((tok + tok // 2, total // 2), BF16),
            jax.ShapeDtypeStruct((tok, total // 2), BF16),
            jax.ShapeDtypeStruct((tok, total // 2), BF16),
            jax.ShapeDtypeStruct((tok, D), BF16),
            jax.ShapeDtypeStruct((1, total), F32),
        ],
        [SMEM] + [VMEM] * 5,
        (place, normed, half, w_up, up_bias, grad_active),
        room=16,
    )
    return act_mine, act_sent, grad_mine, grad_sent, back, sums


def column_sum(values):
    return jnp.sum(values, axis=0, keepdims=True)


def norm_back(values, grad, gain):
    mean = jnp.mean(values, axis=-1, keepdims=True)
    centered = values - mean
    scale = lax.rsqrt(jnp.mean(centered * centered, axis=-1, keepdims=True) + norm_eps)
    normed = centered * scale
    inner = grad * gain
    along = jnp.mean(inner * normed, axis=-1, keepdims=True)
    back = scale * (inner - jnp.mean(inner, axis=-1, keepdims=True) - normed * along)
    return back, column_sum(grad * normed), column_sum(grad)


def turn_kernel(heads, n_after, place_ref, mixed_ref, part_ref, other_ref, low_ref, gain_ref, w_ref, *refs):
    mid_ref, low_out_ref, sum_ref = refs[n_after : n_after + 3]
    pieces, head_s = refs[n_after + 3 : -1], refs[-1]
    grad = part_ref[...].astype(F32) + other_ref[...].astype(F32)
    back, gain_sum, shift_sum = norm_back(mixed_ref[...], grad, gain_ref[1:2])
    low_in = low_ref[...].astype(F32)
    mid = low_in + back
    mid_ref[...] = mid
    low = mid.astype(BF16)
    low_out_ref[...] = low
    sum_ref[0:1] = gain_sum
    sum_ref[1:2] = shift_sum
    sum_ref[2:3] = jnp.sum(low.astype(F32), axis=0, keepdims=True)
    sum_ref[3:4] = jnp.sum(low_in, axis=0, keepdims=True)
    product = mm(low, w_ref[...], NT).astype(BF16)
    for h in range(heads):
        head_s[h] = product[:, h * HD : (h + 1) * HD]
    for x in range(heads):
        pieces[x][...] = head_s[place_ref[0] ^ x]


def turn_back(place, mixed, part, other, cotangent, gain, w_out, after=()):
    tok, heads = mixed.shape[0], w_out.shape[0] // HD
    results = call(
        functools.partial(turn_kernel, heads, len(after)),
        "turn_back",
        [
            jax.ShapeDtypeStruct((tok, D), F32),
            jax.ShapeDtypeStruct((tok, D), BF16),
            jax.ShapeDtypeStruct((4, D), F32),
        ]
        + [jax.ShapeDtypeStruct((tok, HD), BF16)] * heads,
        [SMEM] + [VMEM] * 6,
        (place, mixed, part, other, cotangent, gain, w_out),
        [pltpu.VMEM((heads, tok, HD), BF16)],
        after=after,
    )
    return results[0], results[1], results[2], results[3:]


def last_kernel(n_after, x_ref, part_ref, other_ref, mid_ref, gain_ref, sums_ref, units_ref, heads_ref, *refs):
    out_ref, small_ref = refs[n_after:]
    grad = part_ref[...].astype(F32) + other_ref[...].astype(F32)
    back, gain_sum, shift_sum = norm_back(x_ref[...].astype(F32), grad, gain_ref[0:1])
    out_ref[...] = mid_ref[...] + back
    small_ref[0:4] = sums_ref[...]
    small_ref[4:5] = gain_sum
    small_ref[5:6] = shift_sum
    small_ref[6:7, : heads_ref.shape[1]] = heads_ref[0:1]
    small_ref[6:7, heads_ref.shape[1] :] = heads_ref[1:2]
    for k in range(units_ref.shape[1] // D):
        small_ref[7 + k : 8 + k] = units_ref[:, k * D : (k + 1) * D]


def last_rows(inputs, part, other, grad_mid, gain, sums, unit_sums, head_sums, after=()):
    tok = inputs.shape[0]
    return call(
        functools.partial(last_kernel, len(after)),
        "last_rows",
        [
            jax.ShapeDtypeStruct((tok, D), F32),
            jax.ShapeDtypeStruct((7 + unit_sums.shape[1] // D, D), F32),
        ],
        [VMEM] * 8,
        (inputs, part, other, grad_mid, gain, sums, unit_sums, head_sums),
        after=after,
    )


def feed_kernel(n_after, place_ref, mine_ref, sent_ref, w_ref, *refs):
    near, half = place_ref[1] % 2, mine_ref.shape[1]
    total = mm(mine_ref[...], rows_of(w_ref, near, half))
    total = total + mm(sent_ref[...], rows_of(w_ref, 1 - near, half))
    refs[n_after][...] = total.astype(BF16)


def feed(place, mine, sent, w_down, after):
    return call(
        functools.partial(feed_kernel, len(after)),
        "feed",
        [jax.ShapeDtypeStruct((mine.shape[0], D), BF16)],
        [SMEM] + [VMEM] * 3,
        (place, mine, sent, w_down),
        after=after,
    )[0]


def early_kernel(low_ref, w_ref, out_ref):
    out_ref[...] = mm(low_ref[...], w_ref[...], NT)


def early_grad(cotangent, w_down):
    return call(
        early_kernel,
        "early_grad",
        [jax.ShapeDtypeStruct((cotangent.shape[0], w_down.shape[0]), F32)],
        [VMEM] * 2,
        (cotangent, w_down),
    )[0]


def pair_grad_kernel(extra, halves, n_after, place_ref, rows_ref, units_ref, near_ref, *refs):
    near_rows, refs = refs[: 1 + halves], refs[1 + halves :]
    more, refs = refs[: 2 * extra], refs[2 * extra + n_after :]
    sent_ref, kept_ref, rows_s = refs
    dp, mp = place_ref[2], place_ref[3]
    tok, width = units_ref.shape
    if halves:
        half = near_rows[0].shape[0]
        for k in range(2):
            rows_s[pl.ds(pl.multiple_of((mp ^ k) * half, 16), half)] = near_rows[k][...]
    else:
        rows_s = near_rows[0]
    step = sent_ref.shape[0]
    for k, out_ref in ((1, sent_ref), (0, kept_ref)):
        cut = pl.ds(pl.multiple_of((dp ^ k) * step, 128), step)
        total = mm(rows_ref[:, cut], units_ref[...], TN) + mm(rows_s[:, cut], near_ref[:tok], TN)
        out_ref[:, :width] = total.astype(out_ref.dtype)
        if extra:
            out_ref[:, width:] = mm(more[0][:, cut], more[1][...], TN).astype(out_ref.dtype)


def pair_grad(place, rows, near_rows, units, near_units, more, after):
    tok, width = units.shape
    total = width + (more[1].shape[1] if more else 0)
    return call(
        functools.partial(pair_grad_kernel, int(bool(more)), len(near_rows) - 1, len(after)),
        "pair_grad",
        [jax.ShapeDtypeStruct((D // 2, total), BF16), jax.ShapeDtypeStruct((D // 2, total), F32)],
        [SMEM] + [VMEM] * (3 + len(near_rows) + len(more)),
        (place, rows, units, near_units, *near_rows, *more),
        [pltpu.VMEM((tok, D), BF16)],
        after=after,
    )


def head_grad_kernel(groups, n_after, place_ref, *refs):
    own_ref, mine, other = refs[0], refs[1:groups], refs[groups : 2 * groups - 1]
    dq, dkv = refs[2 * groups - 1 : 3 * groups - 1], refs[3 * groups - 1 : 4 * groups - 1]
    sent_ref, kept_ref, rows_s, grads_s = refs[4 * groups - 1 + n_after :]
    dp, mp = place_ref[2], place_ref[3]
    tok = own_ref.shape[0]
    half = tok // 2
    for x in range(groups):
        if x == 0:
            rows_s[0:tok] = own_ref[...]
        else:
            rows_s[pl.ds(pl.multiple_of(x * tok + mp * half, 16), half)] = mine[x - 1][...]
            rows_s[pl.ds(pl.multiple_of(x * tok + (1 - mp) * half, 16), half)] = other[x - 1][...]
        rows = slice(x * tok, (x + 1) * tok)
        grads_s[rows, :HD] = dq[x][...]
        grads_s[rows, HD : 2 * HD] = dkv[x][0]
        grads_s[rows, 2 * HD :] = dkv[x][1]
    step = sent_ref.shape[0]
    for k, out_ref in ((1, sent_ref), (0, kept_ref)):
        cut = pl.ds(pl.multiple_of((dp ^ k) * step, 128), step)
        out_ref[...] = mm(rows_s[:, cut], grads_s[...], TN).astype(out_ref.dtype)


def head_grad(place, own, mine, other, dq, dkv, after):
    tok, groups = own.shape[0], len(dq)
    return call(
        functools.partial(head_grad_kernel, groups, len(after)),
        "head_grad",
        [jax.ShapeDtypeStruct((D // 2, 3 * HD), BF16), jax.ShapeDtypeStruct((D // 2, 3 * HD), F32)],
        [SMEM] + [VMEM] * (4 * groups - 1),
        (place, own, *mine, *other, *dq, *dkv),
        [pltpu.VMEM((groups * tok, D), BF16), pltpu.VMEM((groups * tok, 3 * HD), BF16)],
        after=after,
        flops=2 * groups * tok * D * 3 * HD,
        moved=2 * groups * tok * (D + 3 * HD),
    )


def sum_kernel(groups, n_there, n_after, own_ref, *refs):
    there, outs = refs[:n_there], refs[n_there + n_after :]
    for x in range(groups):
        for j in range(2):
            total = own_ref[x, j]
            for ref in there:
                total = total + ref[0, x, j].astype(F32)
            outs[x][j] = total.astype(BF16)


def sum_columns(own, there, after):
    groups, _, tok, _ = own.shape
    return call(
        functools.partial(sum_kernel, groups, len(there), len(after)),
        "sum_columns",
        [jax.ShapeDtypeStruct((2, tok, HD), BF16)] * groups,
        [VMEM] * (1 + len(there)),
        (own, *there),
        after=after,
        moved=10 * own.size,
    )


def fold_kernel(outer, inner, n_after, now_ref, kept_ref, there_ref, *refs):
    mine_ref, sent_ref = refs[n_after:]
    for o in range(outer):
        for k, ref in ((0, mine_ref), (1, sent_ref)):
            at = pl.ds(pl.multiple_of((2 * o + (now_ref[0] ^ k)) * inner, 16), inner)
            total = kept_ref[at] + there_ref[at].astype(F32)
            ref[o * inner : (o + 1) * inner] = total.astype(ref.dtype)


def fold(now, kept, there, inner, after=()):
    rows, width = kept.shape
    return call(
        functools.partial(fold_kernel, rows // (2 * inner), inner, len(after)),
        "fold",
        [jax.ShapeDtypeStruct((rows // 2, width), F32), jax.ShapeDtypeStruct((rows // 2, width), BF16)],
        [SMEM, VMEM, VMEM],
        (now, kept, there),
        after=after,
        moved=9 * kept.size,
    )


def pass_on(*refs):
    pass


def gate(x, *after, weight=0):
    return pl.pallas_call(
        pass_on,
        out_shape=jax.ShapeDtypeStruct(x.shape, x.dtype),
        in_specs=[ANY] * (1 + len(after)),
        out_specs=ANY,
        input_output_aliases={0: 0},
        cost_estimate=pl.CostEstimate(flops=weight, bytes_accessed=0, transcendentals=0),
        name="gate",
    )(x, *after)


def swap(x, axis, size, bit):
    return lax.ppermute(x, axis, [(i, i ^ bit) for i in range(size)])


def bits(size):
    return [1 << i for i in range(size.bit_length() - 1)]


def sum_over(vector, axes):
    for axis, size in axes:
        for bit in bits(size):
            vector = vector + swap(vector, axis, size, bit)
    return vector


def body(
    sizes,
    inputs,
    doc_lengths,
    slopes,
    norm_gain,
    norm_bias,
    w_qkv,
    qv_bias,
    w_out,
    w_up,
    up_bias,
    w_down,
    out_bias,
    cotangent,
):
    n_dp, groups, cols = sizes
    tok = inputs.shape[0]
    width = slopes.shape[0] * HD
    me, col = lax.axis_index("sg"), lax.axis_index("sr")
    mp, dp, near = lax.axis_index("mp"), lax.axis_index("dp"), lax.axis_index("sr") % 2
    place = jnp.stack([me, col, dp, mp]).astype(jnp.int32)

    def deal(pieces):
        return [pieces[x] if x == 0 else swap(pieces[x], "sg", groups, x) for x in range(groups)]

    def half_rows(x):
        return lax.dynamic_slice_in_dim(x, mp * (tok // 2), tok // 2, 0)

    normed_one, one_half, q, kv = project(place, inputs, norm_gain, norm_bias, w_qkv, qv_bias)
    grad_active = early_grad(cotangent, w_down)
    kv = deal(kv)
    others = [[swap(kv[0], "sr", cols, s)] for s in range(1, cols)]
    turn = (grad_active,)
    for x in range(1, groups):
        kv[x] = gate(kv[x], *turn, *[column[-1] for column in others])
        turn = ()
        for s in range(1, cols):
            others[s - 1].append(swap(kv[x], "sr", cols, s))
    others = [piece for column in others for piece in column]
    q = deal([q[0]] + [gate(piece, kv[groups - 1]) for piece in q[1:]])
    others[-1] = gate(others[-1], weight=5 * HOLD)
    outs, ot, lse = attend_forward(place, doc_lengths, slopes, q, kv, others, groups, cols, tok, [])
    low_near = swap(gate(cotangent, q[1]), "sr", cols, 1)
    low_near = gate(low_near, outs[0], weight=HOLD)
    outs = deal(outs)
    one_half = gate(one_half, outs[groups - 1])
    far = swap(one_half, "sg", groups, 2)
    attn_part, attended = mix_heads(place, w_out, outs, [low_near])
    mixed, normed_two, two_half = middle(
        place,
        inputs,
        attn_part,
        swap(attn_part, "mp", 2, 1),
        out_bias,
        norm_gain,
        norm_bias,
        [],
    )

    half_units = w_up.shape[1] // 2
    active, active_sent, grad_hidden, hidden_sent, back_two, unit_sums = hidden_units(
        place, normed_two, two_half, w_up, up_bias[None], grad_active
    )
    active_near = swap(active_sent, "sr", cols, 1)
    hidden_near = swap(hidden_sent, "sr", cols, 1)
    far = gate(far, back_two, weight=HOLD)
    grad_mid, grad_mid_low, row_sums, pieces = turn_back(
        place,
        mixed,
        back_two,
        swap(back_two, "mp", 2, 1),
        cotangent,
        norm_gain,
        w_out,
        [far],
    )
    grads = deal(pieces)

    down_sent, down_kept = pair_grad(
        place,
        cotangent,
        [low_near],
        active,
        active_near,
        (),
        [pieces[3]],
    )
    down_there = swap(down_sent, "dp", 2, 1)
    far = gate(far, down_sent, *grads[1:])
    last = swap(far, "sg", groups, 1)
    one_half = gate(one_half, far)
    beside = swap(one_half, "sg", groups, 1)
    dq, dkv, dkv_other = attend_backward(
        place,
        doc_lengths,
        slopes,
        q,
        kv,
        others,
        grads,
        ot,
        lse,
        groups,
        cols,
        tok,
        [down_sent, one_half],
    )
    dkv_there = [swap(dkv_other[s - 1 : s], "sr", cols, s) for s in range(1, cols)]
    beside = gate(beside, dq[0], weight=HOLD)
    last = gate(last, dq[0], weight=HOLD)
    hidden_near = gate(hidden_near, dq[0], weight=HOLD)
    dq_mine = [dq[0], gate(dq[1], beside), gate(dq[2], last), gate(dq[3], hidden_near)]
    dq = deal(dq_mine)
    two_near = hidden_near[tok:]
    two_near_mp = swap(two_near, "mp", 2, 1)

    rows_here = D // (2 * groups * cols)
    stages = [("sr", cols, 2 * bit) for bit in bits(cols // 2)]
    stages += [("sg", groups, bit) for bit in bits(groups)]

    def now(axis, bit):
        return ((lax.axis_index(axis) // bit) % 2).astype(jnp.int32).reshape(1)

    def scatter(kept, there, after):
        for k, (axis, size, bit) in enumerate(stages):
            kept, sent = fold(now(axis, bit), kept, there, 2 * rows_here, after[k : k + 1])
            there = gate(swap(sent, axis, size, bit), weight=HOLD)
            yield kept, sent, there

    down_after = [dq_mine[3]]
    down = scatter(down_kept, gate(down_there, weight=HOLD), down_after)
    down_now = next(down)
    up_sent, up_kept = pair_grad(
        place,
        normed_two,
        [two_near, two_near_mp],
        grad_hidden,
        hidden_near,
        (grad_mid_low, attended),
        [down_now[1]],
    )
    dq = [dq[0]] + [gate(piece, up_sent, weight=HOLD) for piece in dq[1:]]
    dkv_there = [gate(piece, up_sent, weight=HOLD) for piece in dkv_there]
    up_sent = gate(up_sent, *dq[1:])
    up_there = gate(swap(up_sent, "dp", 2, 1), weight=HOLD)
    dkv_mine = sum_columns(dkv, dkv_there, [up_sent])
    dkv = deal(dkv_mine)

    down_after += [dkv_mine[0]] * (len(stages) - 1)
    ffn_part = feed(place, active, active_sent, w_down, [dkv_mine[0]])
    for down_now in down:
        pass
    up_after = [down_now[1]]
    up = scatter(up_kept, up_there, up_after)
    up_now = next(up)
    dkv = [dkv[0]] + [gate(piece, up_now[1]) for piece in dkv[1:]]
    back_part, head_sums = unproject(place, w_qkv, dq, dkv, [ffn_part])
    grad_inputs, small = last_rows(
        inputs,
        back_part,
        swap(back_part, "mp", 2, 1),
        grad_mid,
        norm_gain,
        row_sums,
        unit_sums,
        head_sums,
        [],
    )
    rows_mine = [gate(piece, back_part) for piece in (beside, far, last)]
    rows_mp = [swap(piece, "mp", 2, 1) for piece in rows_mine]
    head_sent, head_kept = head_grad(
        place,
        normed_one,
        rows_mine,
        rows_mp,
        dq_mine,
        dkv_mine,
        [small],
    )
    up_after += [head_sent] * (len(stages) - 1)
    for up_now in up:
        pass
    head_there = gate(swap(head_sent, "dp", 2, 1), up_now[1], weight=HOLD)
    ffn_part = gate(ffn_part, up_now[1])
    small = sum_over(small, (("sr", cols), ("dp", n_dp), ("sg", groups)))

    def last_stage(kept, sent, there):
        return (kept + there.astype(F32)).reshape(2, rows_here, -1)

    down = last_stage(*down_now)

    kept = (head_kept + head_there.astype(F32)).reshape(groups, cols // 2, 2 * rows_here, 3 * HD)
    for bit in bits(cols // 2):
        here = now("sr", 2 * bit)[0]
        view = kept.reshape(groups, -1, 2, 2 * rows_here, 3 * HD)
        sent = lax.dynamic_index_in_dim(view, 1 - here, 2, keepdims=False).astype(BF16)
        kept = lax.dynamic_index_in_dim(view, here, 2, keepdims=False)
        kept = kept + swap(sent, "sr", cols, 2 * bit).astype(F32)
    kept = kept.reshape(groups, 2, rows_here, 3 * HD)
    low = kept.astype(BF16)
    outputs = (
        mixed + ffn_part.astype(F32) + swap(ffn_part, "mp", 2, 1).astype(F32) + out_bias[1]
    ).astype(BF16)
    pieces = [lax.dynamic_index_in_dim(low, me ^ x, 0, keepdims=False) for x in range(groups)]
    up = last_stage(*up_now[:2], gate(up_now[2], pieces[1], outputs))
    pieces = deal(pieces)
    pieces[0] = lax.dynamic_index_in_dim(kept, me, 0, keepdims=False)
    heads_all = jnp.concatenate(
        [
            sum(jnp.where((me ^ x) == h, pieces[x].astype(F32), 0.0) for x in range(groups))
            for h in range(groups)
        ],
        2,
    )

    def with_near(x):
        sent = lax.dynamic_index_in_dim(x, 1 - near, 0, keepdims=False).astype(BF16)
        mine = lax.dynamic_index_in_dim(x, near, 0, keepdims=False)
        return mine, swap(sent, "sr", cols, 1).astype(F32)

    def units_in_order(mine, there):
        return jnp.where(
            near == 0, jnp.concatenate([mine, there], 1), jnp.concatenate([there, mine], 1)
        )

    grad_down = units_in_order(*with_near(down)).T
    mine, there = with_near(up)
    grad_up = units_in_order(mine[:, :half_units], there[:, :half_units])
    grad_out = (mine + there)[:, half_units:].T
    mine, there = with_near(heads_all)
    grad_qkv = (mine + there).reshape(rows_here, groups, 3, HD).transpose(2, 0, 1, 3)
    grad_qkv = grad_qkv.reshape(3, rows_here, width)

    return (
        outputs,
        grad_inputs,
        jnp.concatenate([small[4:5], small[0:1]]),
        jnp.concatenate([small[5:6], small[1:2]]),
        grad_qkv,
        small[6].reshape(2, width),
        grad_out,
        grad_up,
        small[7:].reshape(-1),
        grad_down,
        small[2:4],
    )


def solution(mesh):
    n_dp, n_seq, n_mp = mesh.shape["dp"], mesh.shape["seq"], mesh.shape["mp"]
    groups = 4
    cols = n_seq // groups
    inner = Mesh(mesh.devices.reshape(n_dp, groups, cols, n_mp), ("dp", "sg", "sr", "mp"))
    rows = ("dp", "sg", "sr")
    return jax.shard_map(
        functools.partial(body, (n_dp, groups, cols)),
        mesh=inner,
        in_specs=(
            P(rows, None),
            P("dp", None),
            P("mp"),
            P(),
            P(),
            P(None, None, "mp"),
            P(None, "mp"),
            P("mp", None),
            P(None, "mp"),
            P("mp"),
            P("mp", None),
            P(),
            P(rows, None),
        ),
        out_specs=(
            P(rows, None),
            P(rows, None),
            P(),
            P(),
            P(None, rows, "mp"),
            P(None, "mp"),
            P("mp", rows),
            P(rows, "mp"),
            P("mp"),
            P("mp", rows),
            P(),
        ),
        check_vma=False,
    )
```

```python
import functools
import math

import jax
import jax.numpy as jnp
from jax import lax
from jax.experimental import pallas as pl
from jax.experimental.pallas import tpu as pltpu
from jax.sharding import Mesh
from jax.sharding import PartitionSpec as P

D = 1024
HD = 128
BF16 = jnp.bfloat16
F32 = jnp.float32

norm_eps = 1e-05
masked_fill = -1e30
score_scale = HD ** (-0.5)

NT = (((1,), (1,)), ((), ()))
NN = (((1,), (0,)), ((), ()))
TN = (((0,), (0,)), ((), ()))


def mm(a, b, dims=NN):
    return lax.dot_general(a, b, dims, preferred_element_type=F32)


def doc_start(docs_ref, position):
    start = jnp.zeros_like(position)
    bound = jnp.int32(0)
    for d in range(docs_ref.shape[1]):
        bound = bound + docs_ref[0, d]
        start = jnp.where(position >= bound, bound, start)
    return start


def key_span(docs_ref, kb, z_count, cols, col, tok):
    z_key, col_key = kb // cols, lax.rem(kb, cols)
    first = z_key + (col_key > col).astype(jnp.int32)
    end = jnp.int32(0)
    barred = (col_key == col).astype(jnp.int32)
    for z in range(z_count):
        block = z * cols + col
        end = end + (doc_start(docs_ref, block * tok) < (kb + 1) * tok).astype(jnp.int32)
        late = (doc_start(docs_ref, block * tok + tok - 1) > kb * tok) & (block >= kb)
        barred = barred | late.astype(jnp.int32)
    return first, jnp.maximum(end - first, 0), barred


def column_setup(docs_ref, slope, groups, cols, col, tok, pos_s, start_s, rise_s):
    for z in range(groups):
        lanes = slice(z * tok, (z + 1) * tok)
        at = (z * cols + col) * tok + lax.broadcasted_iota(jnp.int32, (1, tok), 1)
        pos_s[:, lanes] = at
        start_s[:, lanes] = doc_start(docs_ref, at)
    rise_s[...] = slope * lax.broadcasted_iota(jnp.int32, (tok, 128), 0).astype(F32)


def widened(rise, width):
    return jnp.concatenate([rise] * (width // 128), axis=1)


def over_key_blocks(docs_ref, groups, cols, col, tok, run, none=None):
    blocks = groups * cols

    def step(i, carry):
        kb = blocks - 1 - i
        first, count, barred = key_span(docs_ref, kb, groups, cols, col, tok)
        for n in range(1, groups + 1):
            for masked in (True, False):

                @pl.when((count == n) & (barred == int(masked)))
                def _(n=n, masked=masked):
                    run(kb, pl.multiple_of(first * tok, 128), n * tok, masked)

        if none is not None:

            @pl.when(count == 0)
            def _():
                none(kb)

        return carry

    lax.fori_loop(0, blocks, step, 0)


def allowed(kb, at, start, tok, width):
    keys = kb * tok + lax.broadcasted_iota(jnp.int32, (tok, width), 0)
    return (keys <= at) & (keys >= start)


def natural_order(place_ref, n_groups, n_cols, q_refs, kv_refs, other_refs, store_query, store_key):
    me, col = place_ref[0], place_ref[1]
    for x in range(n_groups):
        z = me ^ x
        store_query(z, q_refs[x])
        store_key(z * n_cols + col, kv_refs[x])
        for s in range(1, n_cols):
            store_key(z * n_cols + (col ^ s), other_refs[(s - 1) * n_groups + x])


def block_rows(z, tok):
    return pl.ds(pl.multiple_of(z * tok, 128), tok)


def forward_kernel(groups, cols, tok, n_after, place_ref, docs_ref, slope_ref, *refs):
    n_other = (cols - 1) * groups
    q_refs, refs = refs[:groups], refs[groups:]
    kv_refs, refs = refs[:groups], refs[groups:]
    other_refs, refs = refs[:n_other], refs[n_other + n_after :]
    outs, (ot_ref, lse_ref), scratch = refs[:groups], refs[groups : groups + 2], refs[groups + 2 :]
    q_s, k_s, vt_s, pos_s, start_s, rise_s, top_s, total_s = scratch
    me, col = place_ref[0], place_ref[1]
    slope = slope_ref[me]

    def store_query(z, piece):
        q_s[block_rows(z, tok)] = piece[...]

    def store_key(block, piece):
        k_s[block] = piece[0]
        vt_s[block] = piece[1].T

    natural_order(place_ref, groups, cols, q_refs, kv_refs, other_refs, store_query, store_key)
    column_setup(docs_ref, slope, groups, cols, col, tok, pos_s, start_s, rise_s)
    top_s[...] = jnp.full(top_s.shape, masked_fill, F32)
    total_s[...] = jnp.zeros_like(total_s)
    ot_ref[...] = jnp.zeros_like(ot_ref)

    def run(kb, base, width, masked):
        lanes = pl.ds(base, width)
        at = pos_s[:, lanes]
        row = slope * (kb * tok - at).astype(F32)
        scores = mm(k_s[kb], q_s[lanes], NT) + widened(rise_s[...], width)
        if masked:
            scores = jnp.where(allowed(kb, at, start_s[:, lanes], tok, width), scores, masked_fill)
        top = jnp.maximum(top_s[:, lanes], jnp.max(scores, axis=0, keepdims=True) + row)
        weights = jnp.exp(scores - (top - row))
        rescale = jnp.exp(top_s[:, lanes] - top)
        top_s[:, lanes] = top
        total_s[:, lanes] = total_s[:, lanes] * rescale + jnp.sum(weights, axis=0, keepdims=True)
        ot_ref[:, lanes] = ot_ref[:, lanes] * rescale + mm(vt_s[kb], weights.astype(BF16))

    over_key_blocks(docs_ref, groups, cols, col, tok, run)
    total = total_s[...]
    ot_ref[...] = ot_ref[...] / total
    lse_ref[...] = top_s[...] + jnp.log(total)
    for x in range(groups):
        outs[x][...] = ot_ref[:, block_rows(me ^ x, tok)].T.astype(BF16)


def backward_kernel(groups, cols, tok, n_after, place_ref, docs_ref, slope_ref, *refs):
    n_other = (cols - 1) * groups
    q_refs, refs = refs[:groups], refs[groups:]
    kv_refs, refs = refs[:groups], refs[groups:]
    other_refs, refs = refs[:n_other], refs[n_other:]
    grads, (ot_ref, lse_ref) = refs[:groups], refs[groups : groups + 2]
    refs = refs[groups + 2 + n_after :]
    dq_refs, own_ref, refs = refs[:groups], refs[groups], refs[groups + 1 :]
    if cols > 1:
        other_ref, refs = refs[0], refs[1:]
    q_s, k_s, v_s, kt_s, do_s, pos_s, start_s, rise_s, delta_s, dqt_s = refs
    me, col = place_ref[0], place_ref[1]
    slope = slope_ref[me]

    def store_query(z, piece):
        q_s[block_rows(z, tok)] = piece[...]

    def store_key(block, piece):
        k_s[block] = piece[0]
        v_s[block] = piece[1]
        kt_s[block] = piece[0].T

    natural_order(place_ref, groups, cols, q_refs, kv_refs, other_refs, store_query, store_key)
    column_setup(docs_ref, slope, groups, cols, col, tok, pos_s, start_s, rise_s)
    for x in range(groups):
        rows = block_rows(me ^ x, tok)
        grad = grads[x][...]
        do_s[rows] = grad
        delta_s[:, rows] = jnp.sum(grad.astype(F32).T * ot_ref[:, rows], axis=0, keepdims=True)
    dqt_s[...] = jnp.zeros_like(dqt_s)

    def store(kb, dk, dv):
        x, s = (kb // cols) ^ me, lax.rem(kb, cols) ^ col

        @pl.when(s == 0)
        def _():
            own_ref[x, 0] = dk
            own_ref[x, 1] = dv

        if cols > 1:

            @pl.when(s != 0)
            def _():
                other_ref[s - 1, x, 0] = dk.astype(BF16)
                other_ref[s - 1, x, 1] = dv.astype(BF16)

    def run(kb, base, width, masked):
        lanes = pl.ds(base, width)
        at = pos_s[:, lanes]
        row = slope * (kb * tok - at).astype(F32)
        query, grad = q_s[lanes], do_s[lanes]
        scores = mm(k_s[kb], query, NT) + widened(rise_s[...], width)
        probs = jnp.exp(scores - (lse_ref[:, lanes] - row))
        if masked:
            probs = jnp.where(allowed(kb, at, start_s[:, lanes], tok, width), probs, 0.0)
        dv = mm(probs.astype(BF16), grad)
        grad_scores = (probs * (mm(v_s[kb], grad, NT) - delta_s[:, lanes])).astype(BF16)
        dk = mm(grad_scores, query)
        dqt_s[:, lanes] += mm(kt_s[kb], grad_scores)
        store(kb, dk, dv)

    def none(kb):
        store(kb, jnp.zeros((tok, HD), F32), jnp.zeros((tok, HD), F32))

    over_key_blocks(docs_ref, groups, cols, col, tok, run, none)
    for x in range(groups):
        dq_refs[x][...] = (dqt_s[:, block_rows(me ^ x, tok)] * score_scale).T.astype(BF16)


SMEM = pl.BlockSpec(memory_space=pltpu.SMEM)
VMEM = pl.BlockSpec(memory_space=pltpu.VMEM)
ANY = pl.BlockSpec(memory_space=pl.ANY)
VMEM_BYTES = 66900000
COST = 1000
HOLD = 20 * 10**9
UP_HOLD = 5 * HOLD
LEAST_BYTES = 66900000
gelu_slope = (2.0 / 3.141592653589793) ** 0.5


def call(kernel, name, out_shape, specs, operands, scratch=(), after=(), room=8, flops=0, moved=0, exps=0):
    held = [*operands, *out_shape, *scratch]
    held = sum(math.prod(x.shape) * jnp.dtype(x.dtype).itemsize for x in held)
    limit = max(LEAST_BYTES, min(VMEM_BYTES, held * 9 // 8 + room * 2**20))
    results = pl.pallas_call(
        kernel,
        out_shape=out_shape,
        in_specs=list(specs) + [ANY] * len(after),
        out_specs=[VMEM] * len(out_shape),
        scratch_shapes=list(scratch),
        compiler_params=pltpu.CompilerParams(vmem_limit_bytes=limit),
        cost_estimate=pl.CostEstimate(flops=flops // COST, bytes_accessed=moved // COST, transcendentals=exps // COST),
        name=name,
    )(*operands, *after)
    return list(results)


def attend_forward(place, docs, slope, q, kv, others, groups, cols, tok, after):
    blocks = groups * cols
    operands = (place, docs, slope, *q, *kv, *others)
    out_shape = [jax.ShapeDtypeStruct((tok, HD), BF16)] * groups + [
        jax.ShapeDtypeStruct((HD, groups * tok), F32),
        jax.ShapeDtypeStruct((1, groups * tok), F32),
    ]
    results = call(
        functools.partial(forward_kernel, groups, cols, tok, len(after)),
        "attend_forward",
        out_shape,
        [SMEM] * 3 + [VMEM] * (len(operands) - 3),
        operands,
        [
            pltpu.VMEM((groups * tok, HD), BF16),
            pltpu.VMEM((blocks, tok, HD), BF16),
            pltpu.VMEM((blocks, HD, tok), BF16),
            pltpu.VMEM((1, groups * tok), jnp.int32),
            pltpu.VMEM((1, groups * tok), jnp.int32),
            pltpu.VMEM((tok, 128), F32),
            pltpu.VMEM((1, groups * tok), F32),
            pltpu.VMEM((1, groups * tok), F32),
        ],
        after,
        16,
        2 * blocks * groups * tok * tok * HD,
        2 * (groups + 2 * blocks) * tok * HD,
        blocks * groups * tok * tok // 2,
    )
    return results[:groups], results[groups], results[groups + 1]


def attend_backward(place, docs, slope, q, kv, others, grads, ot, lse, groups, cols, tok, after):
    blocks = groups * cols
    operands = (place, docs, slope, *q, *kv, *others, *grads, ot, lse)
    out_shape = [jax.ShapeDtypeStruct((tok, HD), BF16)] * groups + [
        jax.ShapeDtypeStruct((groups, 2, tok, HD), F32)
    ]
    if cols > 1:
        out_shape.append(jax.ShapeDtypeStruct((cols - 1, groups, 2, tok, HD), BF16))
    results = call(
        functools.partial(backward_kernel, groups, cols, tok, len(after)),
        "attend_backward",
        out_shape,
        [SMEM] * 3 + [VMEM] * (len(operands) - 3),
        operands,
        [
            pltpu.VMEM((groups * tok, HD), BF16),
            pltpu.VMEM((blocks, tok, HD), BF16),
            pltpu.VMEM((blocks, tok, HD), BF16),
            pltpu.VMEM((blocks, HD, tok), BF16),
            pltpu.VMEM((groups * tok, HD), BF16),
            pltpu.VMEM((1, groups * tok), jnp.int32),
            pltpu.VMEM((1, groups * tok), jnp.int32),
            pltpu.VMEM((tok, 128), F32),
            pltpu.VMEM((1, groups * tok), F32),
            pltpu.VMEM((HD, groups * tok), F32),
        ],
        after,
        24,
        14 * 10**9 * COST,
    )
    return results[:groups], results[groups], (results[groups + 1] if cols > 1 else None)


def rows_of(ref, part, size):
    return ref[pl.ds(pl.multiple_of(part * size, 16), size)]


def norm_rows(values):
    mean = jnp.mean(values, axis=-1, keepdims=True)
    centered = values - mean
    spread = jnp.mean(centered * centered, axis=-1, keepdims=True)
    return centered * lax.rsqrt(spread + norm_eps)


def mix_kernel(heads, n_after, place_ref, w_ref, *refs):
    pieces, out_ref, att_ref = refs[:heads], refs[heads + n_after], refs[heads + n_after + 1]
    for x in range(heads):
        head = place_ref[0] ^ x
        att_ref[:, pl.ds(pl.multiple_of(head * HD, HD), HD)] = pieces[x][...]
    out_ref[...] = mm(att_ref[...], w_ref[...]).astype(BF16)


def mix_heads(place, w_out, pieces, after):
    tok, heads = pieces[0].shape[0], len(pieces)
    return call(
        functools.partial(mix_kernel, heads, len(after)),
        "mix_heads",
        [jax.ShapeDtypeStruct((tok, D), BF16), jax.ShapeDtypeStruct((tok, heads * HD), BF16)],
        [SMEM] + [VMEM] * (heads + 1),
        (place, w_out, *pieces),
        after=after,
        flops=2 * tok * D * heads * HD,
        moved=2 * (tok * D + D * heads * HD),
    )


def unproject_kernel(heads, n_after, place_ref, w_ref, *refs):
    dq, dkv = refs[:heads], refs[heads : 2 * heads]
    out_ref, sum_ref, wide_s = refs[2 * heads + n_after :]
    for x in range(heads):
        head = place_ref[0] ^ x
        lanes = pl.ds(pl.multiple_of(head * HD, HD), HD)
        wide_s[0, :, lanes] = dq[x][...]
        wide_s[1, :, lanes] = dkv[x][0]
        wide_s[2, :, lanes] = dkv[x][1]
    total = mm(wide_s[0], w_ref[0], NT)
    for j in (1, 2):
        total = total + mm(wide_s[j], w_ref[j], NT)
    out_ref[...] = total.astype(BF16)
    sum_ref[0:1] = jnp.sum(wide_s[0].astype(F32), axis=0, keepdims=True)
    sum_ref[1:2] = jnp.sum(wide_s[2].astype(F32), axis=0, keepdims=True)


def unproject(place, w_qkv, dq, dkv, after):
    tok, heads = dq[0].shape[0], len(dq)
    return call(
        functools.partial(unproject_kernel, heads, len(after)),
        "unproject",
        [jax.ShapeDtypeStruct((tok, D), BF16), jax.ShapeDtypeStruct((2, heads * HD), F32)],
        [SMEM] + [VMEM] * (2 * heads + 1),
        (place, w_qkv, *dq, *dkv),
        [pltpu.VMEM((3, tok, heads * HD), BF16)],
        after=after,
        flops=6 * tok * D * heads * HD,
        moved=2 * (tok * D + 3 * D * heads * HD),
    )


def project_kernel(heads, place_ref, x_ref, gain_ref, shift_ref, w_ref, bias_ref, *refs):
    normed_ref, half_ref, q_refs, kv_refs = refs[0], refs[1], refs[2 : 2 + heads], refs[2 + heads : -1]
    out_s = refs[-1]
    normed = norm_rows(x_ref[...].astype(F32)) * gain_ref[0:1] + shift_ref[0:1]
    normed = normed.astype(BF16)
    normed_ref[...] = normed
    half_ref[...] = rows_of(normed_ref, place_ref[3], half_ref.shape[0])
    for j in range(3):
        product = mm(normed, w_ref[j])
        if j == 0:
            product = (product + bias_ref[0:1]) * score_scale
        if j == 2:
            product = product + bias_ref[1:2]
        product = product.astype(BF16)
        for h in range(heads):
            out_s[h, j] = product[:, h * HD : (h + 1) * HD]
    for x in range(heads):
        head = place_ref[0] ^ x
        q_refs[x][...] = out_s[head, 0]
        kv_refs[x][...] = out_s[head, 1:3]


def project(place, inputs, gain, shift, w_qkv, qv_bias):
    tok = inputs.shape[0]
    heads = w_qkv.shape[2] // HD
    out_shape = (
        [jax.ShapeDtypeStruct((tok, D), BF16), jax.ShapeDtypeStruct((tok // 2, D), BF16)]
        + [jax.ShapeDtypeStruct((tok, HD), BF16)] * heads
        + [jax.ShapeDtypeStruct((2, tok, HD), BF16)] * heads
    )
    results = call(
        functools.partial(project_kernel, heads),
        "project",
        out_shape,
        [SMEM] + [VMEM] * 5,
        (place, inputs, gain, shift, w_qkv, qv_bias),
        [pltpu.VMEM((heads, 3, tok, HD), BF16)],
    )
    return results[0], results[1], results[2 : 2 + heads], results[2 + heads :]


def middle_kernel(n_after, place_ref, x_ref, part_ref, other_ref, bias_ref, gain_ref, shift_ref, *refs):
    mixed_ref, normed_ref, half_ref = refs[n_after:]
    parts = part_ref[...].astype(F32) + other_ref[...].astype(F32)
    mixed = x_ref[...].astype(F32) + parts + bias_ref[0:1]
    mixed_ref[...] = mixed
    normed_ref[...] = (norm_rows(mixed) * gain_ref[1:2] + shift_ref[1:2]).astype(BF16)
    half_ref[...] = rows_of(normed_ref, place_ref[3], half_ref.shape[0])


def middle(place, inputs, part, other, out_bias, gain, shift, after=()):
    tok = inputs.shape[0]
    return call(
        functools.partial(middle_kernel, len(after)),
        "middle",
        [
            jax.ShapeDtypeStruct((tok, D), F32),
            jax.ShapeDtypeStruct((tok, D), BF16),
            jax.ShapeDtypeStruct((tok // 2, D), BF16),
        ],
        [SMEM] + [VMEM] * 6,
        (place, inputs, part, other, out_bias, gain, shift),
        after=after,
    )


def hidden_kernel(place_ref, normed_ref, half_ref, w_ref, bias_ref, grad_ref, *refs):
    act_sent, grad_sent, act_mine, grad_mine, back_ref, sum_ref = refs
    near, (tok, width) = place_ref[1] % 2, act_mine.shape
    grad_sent[tok:] = half_ref[...]
    total = None
    for act_ref, out_ref, side in ((act_sent, grad_sent, 1 - near), (act_mine, grad_mine, near)):
        cut = pl.ds(pl.multiple_of(side * width, 128), width)
        u = mm(normed_ref[...], w_ref[:, cut]) + bias_ref[:, cut]
        square = u * u
        bend = jnp.tanh(u * (gelu_slope + gelu_slope * 0.044715 * square))
        half = 0.5 + 0.5 * bend
        act_ref[...] = (u * half).astype(BF16)
        lean = u * (0.5 - 0.5 * bend * bend)
        rise = half + lean * (gelu_slope + (3 * 0.044715 * gelu_slope) * square)
        grad = (rise * grad_ref[:, cut]).astype(BF16)
        out_ref[:tok] = grad
        sum_ref[:, cut] = column_sum(grad.astype(F32))
        back = mm(grad, w_ref[:, cut], NT)
        total = back if total is None else total + back
    back_ref[...] = total.astype(BF16)


def hidden_units(place, normed, half, w_up, up_bias, grad_active, after=()):
    tok, total = normed.shape[0], w_up.shape[1]
    assert total // 2 == D
    act_sent, grad_sent, act_mine, grad_mine, back, sums = call(
        hidden_kernel,
        "hidden_units",
        [
            jax.ShapeDtypeStruct((tok, total // 2), BF16),
            jax.ShapeDtypeStruct((tok + tok // 2, total // 2), BF16),
            jax.ShapeDtypeStruct((tok, total // 2), BF16),
            jax.ShapeDtypeStruct((tok, total // 2), BF16),
            jax.ShapeDtypeStruct((tok, D), BF16),
            jax.ShapeDtypeStruct((1, total), F32),
        ],
        [SMEM] + [VMEM] * 5,
        (place, normed, half, w_up, up_bias, grad_active),
        room=16,
    )
    return act_mine, act_sent, grad_mine, grad_sent, back, sums


def column_sum(values):
    return jnp.sum(values, axis=0, keepdims=True)


def norm_back(values, grad, gain):
    mean = jnp.mean(values, axis=-1, keepdims=True)
    centered = values - mean
    scale = lax.rsqrt(jnp.mean(centered * centered, axis=-1, keepdims=True) + norm_eps)
    normed = centered * scale
    inner = grad * gain
    along = jnp.mean(inner * normed, axis=-1, keepdims=True)
    back = scale * (inner - jnp.mean(inner, axis=-1, keepdims=True) - normed * along)
    return back, column_sum(grad * normed), column_sum(grad)


def turn_kernel(heads, n_after, place_ref, mixed_ref, part_ref, other_ref, low_ref, gain_ref, w_ref, *refs):
    mid_ref, low_out_ref, sum_ref = refs[n_after : n_after + 3]
    pieces, head_s = refs[n_after + 3 : -1], refs[-1]
    grad = part_ref[...].astype(F32) + other_ref[...].astype(F32)
    back, gain_sum, shift_sum = norm_back(mixed_ref[...], grad, gain_ref[1:2])
    low_in = low_ref[...].astype(F32)
    mid = low_in + back
    mid_ref[...] = mid
    low = mid.astype(BF16)
    low_out_ref[...] = low
    sum_ref[0:1] = gain_sum
    sum_ref[1:2] = shift_sum
    sum_ref[2:3] = jnp.sum(low.astype(F32), axis=0, keepdims=True)
    sum_ref[3:4] = jnp.sum(low_in, axis=0, keepdims=True)
    product = mm(low, w_ref[...], NT).astype(BF16)
    for h in range(heads):
        head_s[h] = product[:, h * HD : (h + 1) * HD]
    for x in range(heads):
        pieces[x][...] = head_s[place_ref[0] ^ x]


def turn_back(place, mixed, part, other, cotangent, gain, w_out, after=()):
    tok, heads = mixed.shape[0], w_out.shape[0] // HD
    results = call(
        functools.partial(turn_kernel, heads, len(after)),
        "turn_back",
        [
            jax.ShapeDtypeStruct((tok, D), F32),
            jax.ShapeDtypeStruct((tok, D), BF16),
            jax.ShapeDtypeStruct((4, D), F32),
        ]
        + [jax.ShapeDtypeStruct((tok, HD), BF16)] * heads,
        [SMEM] + [VMEM] * 6,
        (place, mixed, part, other, cotangent, gain, w_out),
        [pltpu.VMEM((heads, tok, HD), BF16)],
        after=after,
    )
    return results[0], results[1], results[2], results[3:]


def last_kernel(n_after, x_ref, part_ref, other_ref, mid_ref, gain_ref, sums_ref, units_ref, heads_ref, *refs):
    out_ref, small_ref = refs[n_after:]
    grad = part_ref[...].astype(F32) + other_ref[...].astype(F32)
    back, gain_sum, shift_sum = norm_back(x_ref[...].astype(F32), grad, gain_ref[0:1])
    out_ref[...] = mid_ref[...] + back
    small_ref[0:4] = sums_ref[...]
    small_ref[4:5] = gain_sum
    small_ref[5:6] = shift_sum
    small_ref[6:7, : heads_ref.shape[1]] = heads_ref[0:1]
    small_ref[6:7, heads_ref.shape[1] :] = heads_ref[1:2]
    for k in range(units_ref.shape[1] // D):
        small_ref[7 + k : 8 + k] = units_ref[:, k * D : (k + 1) * D]


def last_rows(inputs, part, other, grad_mid, gain, sums, unit_sums, head_sums, after=()):
    tok = inputs.shape[0]
    return call(
        functools.partial(last_kernel, len(after)),
        "last_rows",
        [
            jax.ShapeDtypeStruct((tok, D), F32),
            jax.ShapeDtypeStruct((7 + unit_sums.shape[1] // D, D), F32),
        ],
        [VMEM] * 8,
        (inputs, part, other, grad_mid, gain, sums, unit_sums, head_sums),
        after=after,
    )


def feed_kernel(n_after, place_ref, mine_ref, sent_ref, w_ref, *refs):
    near, half = place_ref[1] % 2, mine_ref.shape[1]
    total = mm(mine_ref[...], rows_of(w_ref, near, half))
    total = total + mm(sent_ref[...], rows_of(w_ref, 1 - near, half))
    refs[n_after][...] = total.astype(BF16)


def feed(place, mine, sent, w_down, after):
    return call(
        functools.partial(feed_kernel, len(after)),
        "feed",
        [jax.ShapeDtypeStruct((mine.shape[0], D), BF16)],
        [SMEM] + [VMEM] * 3,
        (place, mine, sent, w_down),
        after=after,
    )[0]


def early_kernel(low_ref, w_ref, out_ref):
    out_ref[...] = mm(low_ref[...], w_ref[...], NT)


def early_grad(cotangent, w_down):
    return call(
        early_kernel,
        "early_grad",
        [jax.ShapeDtypeStruct((cotangent.shape[0], w_down.shape[0]), F32)],
        [VMEM] * 2,
        (cotangent, w_down),
    )[0]


def pair_grad_kernel(extra, halves, n_after, place_ref, rows_ref, units_ref, near_ref, *refs):
    near_rows, refs = refs[: 1 + halves], refs[1 + halves :]
    more, refs = refs[: 2 * extra], refs[2 * extra + n_after :]
    sent_ref, kept_ref, rows_s = refs
    dp, mp = place_ref[2], place_ref[3]
    tok, width = units_ref.shape
    if halves:
        half = near_rows[0].shape[0]
        for k in range(2):
            rows_s[pl.ds(pl.multiple_of((mp ^ k) * half, 16), half)] = near_rows[k][...]
    else:
        rows_s = near_rows[0]
    step = sent_ref.shape[0]
    for k, out_ref in ((1, sent_ref), (0, kept_ref)):
        cut = pl.ds(pl.multiple_of((dp ^ k) * step, 128), step)
        total = mm(rows_ref[:, cut], units_ref[...], TN) + mm(rows_s[:, cut], near_ref[:tok], TN)
        out_ref[:, :width] = total.astype(out_ref.dtype)
        if extra:
            out_ref[:, width:] = mm(more[0][:, cut], more[1][...], TN).astype(out_ref.dtype)


def pair_grad(place, rows, near_rows, units, near_units, more, after):
    tok, width = units.shape
    total = width + (more[1].shape[1] if more else 0)
    return call(
        functools.partial(pair_grad_kernel, int(bool(more)), len(near_rows) - 1, len(after)),
        "pair_grad",
        [jax.ShapeDtypeStruct((D // 2, total), BF16), jax.ShapeDtypeStruct((D // 2, total), F32)],
        [SMEM] + [VMEM] * (3 + len(near_rows) + len(more)),
        (place, rows, units, near_units, *near_rows, *more),
        [pltpu.VMEM((tok, D), BF16)],
        after=after,
    )


def head_grad_kernel(groups, n_after, place_ref, *refs):
    own_ref, mine, other = refs[0], refs[1:groups], refs[groups : 2 * groups - 1]
    dq, dkv = refs[2 * groups - 1 : 3 * groups - 1], refs[3 * groups - 1 : 4 * groups - 1]
    sent_ref, kept_ref, rows_s, grads_s = refs[4 * groups - 1 + n_after :]
    dp, mp = place_ref[2], place_ref[3]
    tok = own_ref.shape[0]
    half = tok // 2
    for x in range(groups):
        if x == 0:
            rows_s[0:tok] = own_ref[...]
        else:
            rows_s[pl.ds(pl.multiple_of(x * tok + mp * half, 16), half)] = mine[x - 1][...]
            rows_s[pl.ds(pl.multiple_of(x * tok + (1 - mp) * half, 16), half)] = other[x - 1][...]
        rows = slice(x * tok, (x + 1) * tok)
        grads_s[rows, :HD] = dq[x][...]
        grads_s[rows, HD : 2 * HD] = dkv[x][0]
        grads_s[rows, 2 * HD :] = dkv[x][1]
    step = sent_ref.shape[0]
    for k, out_ref in ((1, sent_ref), (0, kept_ref)):
        cut = pl.ds(pl.multiple_of((dp ^ k) * step, 128), step)
        out_ref[...] = mm(rows_s[:, cut], grads_s[...], TN).astype(out_ref.dtype)


def head_grad(place, own, mine, other, dq, dkv, after):
    tok, groups = own.shape[0], len(dq)
    return call(
        functools.partial(head_grad_kernel, groups, len(after)),
        "head_grad",
        [jax.ShapeDtypeStruct((D // 2, 3 * HD), BF16), jax.ShapeDtypeStruct((D // 2, 3 * HD), F32)],
        [SMEM] + [VMEM] * (4 * groups - 1),
        (place, own, *mine, *other, *dq, *dkv),
        [pltpu.VMEM((groups * tok, D), BF16), pltpu.VMEM((groups * tok, 3 * HD), BF16)],
        after=after,
        flops=2 * groups * tok * D * 3 * HD,
        moved=2 * groups * tok * (D + 3 * HD),
    )


def sum_kernel(groups, n_there, n_after, own_ref, *refs):
    there, outs = refs[:n_there], refs[n_there + n_after :]
    for x in range(groups):
        for j in range(2):
            total = own_ref[x, j]
            for ref in there:
                total = total + ref[0, x, j].astype(F32)
            outs[x][j] = total.astype(BF16)


def sum_columns(own, there, after):
    groups, _, tok, _ = own.shape
    return call(
        functools.partial(sum_kernel, groups, len(there), len(after)),
        "sum_columns",
        [jax.ShapeDtypeStruct((2, tok, HD), BF16)] * groups,
        [VMEM] * (1 + len(there)),
        (own, *there),
        after=after,
        moved=10 * own.size,
    )


def fold_kernel(outer, inner, n_after, now_ref, kept_ref, there_ref, *refs):
    mine_ref, sent_ref = refs[n_after:]
    for o in range(outer):
        for k, ref in ((0, mine_ref), (1, sent_ref)):
            at = pl.ds(pl.multiple_of((2 * o + (now_ref[0] ^ k)) * inner, 16), inner)
            total = kept_ref[at] + there_ref[at].astype(F32)
            ref[o * inner : (o + 1) * inner] = total.astype(ref.dtype)


def fold(now, kept, there, inner, after=()):
    rows, width = kept.shape
    return call(
        functools.partial(fold_kernel, rows // (2 * inner), inner, len(after)),
        "fold",
        [jax.ShapeDtypeStruct((rows // 2, width), F32), jax.ShapeDtypeStruct((rows // 2, width), BF16)],
        [SMEM, VMEM, VMEM],
        (now, kept, there),
        after=after,
        moved=9 * kept.size,
    )


def finish_small_kernel(width, mine_ref, there_ref, gain_ref, shift_ref, heads_ref, units_ref, bias_ref):
    total = mine_ref[...] + there_ref[...]
    gain_ref[0:1], gain_ref[1:2] = total[4:5], total[0:1]
    shift_ref[0:1], shift_ref[1:2] = total[5:6], total[1:2]
    heads_ref[0:1], heads_ref[1:2] = total[6:7, :width], total[6:7, width:]
    for k in range(units_ref.shape[1] // D):
        units_ref[:, k * D : (k + 1) * D] = total[7 + k : 8 + k]
    bias_ref[...] = total[2:4]


def finish_small(mine, there, width):
    shapes = [(2, D), (2, D), (2, width), (1, (mine.shape[0] - 7) * D), (2, D)]
    return call(
        functools.partial(finish_small_kernel, width),
        "finish_small",
        [jax.ShapeDtypeStruct(shape, F32) for shape in shapes],
        [VMEM, VMEM],
        (mine, there),
    )


def finish_units_kernel(n_after, place_ref, mine_ref, there_ref, *refs):
    up_ref, out_ref = refs[n_after:]
    near, half = place_ref[1] % 2, up_ref.shape[1] // 2
    up_ref[:, pl.ds(pl.multiple_of(near * half, 128), half)] = mine_ref[:, :half]
    there = there_ref[...].astype(F32)
    up_ref[:, pl.ds(pl.multiple_of((1 - near) * half, 128), half)] = there[:, :half]
    out_ref[...] = (mine_ref[:, half:] + there[:, half:]).T


def finish_units(place, mine, there, width, after):
    rows, total = mine.shape
    return call(
        functools.partial(finish_units_kernel, len(after)),
        "finish_units",
        [
            jax.ShapeDtypeStruct((rows, 2 * (total - width)), F32),
            jax.ShapeDtypeStruct((width, rows), F32),
        ],
        [SMEM, VMEM, VMEM],
        (place, mine, there),
        after=after,
    )


def pass_on(*refs):
    pass


def gate(x, *after, weight=0):
    return pl.pallas_call(
        pass_on,
        out_shape=jax.ShapeDtypeStruct(x.shape, x.dtype),
        in_specs=[ANY] * (1 + len(after)),
        out_specs=ANY,
        input_output_aliases={0: 0},
        cost_estimate=pl.CostEstimate(flops=weight, bytes_accessed=0, transcendentals=0),
        name="gate",
    )(x, *after)


def swap(x, axis, size, bit):
    return lax.ppermute(x, axis, [(i, i ^ bit) for i in range(size)])


def bits(size):
    return [1 << i for i in range(size.bit_length() - 1)]


def sum_over(vector, axes):
    for axis, size in axes:
        for bit in bits(size):
            vector = vector + swap(vector, axis, size, bit)
    return vector


def body(
    sizes,
    inputs,
    doc_lengths,
    slopes,
    norm_gain,
    norm_bias,
    w_qkv,
    qv_bias,
    w_out,
    w_up,
    up_bias,
    w_down,
    out_bias,
    cotangent,
):
    n_dp, groups, cols = sizes
    tok = inputs.shape[0]
    width = slopes.shape[0] * HD
    me, col = lax.axis_index("sg"), lax.axis_index("sr")
    mp, dp, near = lax.axis_index("mp"), lax.axis_index("dp"), lax.axis_index("sr") % 2
    place = jnp.stack([me, col, dp, mp]).astype(jnp.int32)

    def deal(pieces):
        return [pieces[x] if x == 0 else swap(pieces[x], "sg", groups, x) for x in range(groups)]

    def half_rows(x):
        return lax.dynamic_slice_in_dim(x, mp * (tok // 2), tok // 2, 0)

    normed_one, one_half, q, kv = project(place, inputs, norm_gain, norm_bias, w_qkv, qv_bias)
    grad_active = early_grad(cotangent, w_down)
    kv = deal(kv)
    others = [[swap(kv[0], "sr", cols, s)] for s in range(1, cols)]
    turn = (grad_active,)
    for x in range(1, groups):
        kv[x] = gate(kv[x], *turn, *[column[-1] for column in others])
        turn = ()
        for s in range(1, cols):
            others[s - 1].append(swap(kv[x], "sr", cols, s))
    others = [piece for column in others for piece in column]
    q = deal([q[0]] + [gate(piece, kv[groups - 1]) for piece in q[1:]])
    others[-1] = gate(others[-1], weight=5 * HOLD)
    outs, ot, lse = attend_forward(place, doc_lengths, slopes, q, kv, others, groups, cols, tok, [])
    low_near = swap(gate(cotangent, q[1]), "sr", cols, 1)
    low_near = gate(low_near, outs[0], weight=HOLD)
    outs = deal(outs)
    one_half = gate(one_half, outs[groups - 1])
    far = swap(one_half, "sg", groups, 2)
    attn_part, attended = mix_heads(place, w_out, outs, [low_near])
    mixed, normed_two, two_half = middle(
        place,
        inputs,
        attn_part,
        swap(attn_part, "mp", 2, 1),
        out_bias,
        norm_gain,
        norm_bias,
        [],
    )

    half_units = w_up.shape[1] // 2
    active, active_sent, grad_hidden, hidden_sent, back_two, unit_sums = hidden_units(
        place, normed_two, two_half, w_up, up_bias[None], grad_active
    )
    active_near = swap(active_sent, "sr", cols, 1)
    hidden_near = swap(hidden_sent, "sr", cols, 1)
    far = gate(far, back_two, weight=HOLD)
    grad_mid, grad_mid_low, row_sums, pieces = turn_back(
        place,
        mixed,
        back_two,
        swap(back_two, "mp", 2, 1),
        cotangent,
        norm_gain,
        w_out,
        [far],
    )
    grads = deal(pieces)

    down_sent, down_kept = pair_grad(
        place,
        cotangent,
        [low_near],
        active,
        active_near,
        (),
        [pieces[3]],
    )
    down_there = swap(down_sent, "dp", 2, 1)
    far = gate(far, down_sent, *grads[1:])
    last = swap(far, "sg", groups, 1)
    one_half = gate(one_half, far)
    beside = swap(one_half, "sg", groups, 1)
    dq, dkv, dkv_other = attend_backward(
        place,
        doc_lengths,
        slopes,
        q,
        kv,
        others,
        grads,
        ot,
        lse,
        groups,
        cols,
        tok,
        [down_sent, one_half],
    )
    dkv_there = [swap(dkv_other[s - 1 : s], "sr", cols, s) for s in range(1, cols)]
    beside = gate(beside, dq[0], weight=HOLD)
    last = gate(last, dq[0], weight=HOLD)
    hidden_near = gate(hidden_near, dq[0], weight=HOLD)
    dq_mine = [dq[0], gate(dq[1], beside), gate(dq[2], last), gate(dq[3], hidden_near)]
    dq = deal(dq_mine)
    two_near = hidden_near[tok:]
    two_near_mp = swap(two_near, "mp", 2, 1)

    rows_here = D // (2 * groups * cols)
    stages = [("sr", cols, 2 * bit) for bit in bits(cols // 2)]
    stages += [("sg", groups, bit) for bit in bits(groups)]

    def now(axis, bit):
        return ((lax.axis_index(axis) // bit) % 2).astype(jnp.int32).reshape(1)

    def stage(k, kept, there, *after):
        axis, size, bit = stages[k]
        kept, sent = fold(now(axis, bit), kept, there, 2 * rows_here, after)
        return kept, sent, swap(sent, axis, size, bit)

    last_turn = len(stages) - 1
    up_sent, up_kept = pair_grad(
        place,
        normed_two,
        [two_near, two_near_mp],
        grad_hidden,
        hidden_near,
        (grad_mid_low, attended),
        [dq_mine[3]],
    )
    down_there = gate(down_there, up_sent)
    for k in range(last_turn):
        down_kept, down_sent, down_there = stage(k, down_kept, down_there)
    up_there = swap(up_sent, "dp", 2, 1)
    dq = [dq[0]] + [gate(piece, down_sent, weight=HOLD) for piece in dq[1:]]
    dkv_there = [gate(piece, *dq[1:], weight=HOLD) for piece in dkv_there]
    rows_mine = [gate(piece, *dq[1:]) for piece in (beside, far, last)]
    rows_mp = [swap(piece, "mp", 2, 1) for piece in rows_mine]
    dkv_mine = sum_columns(dkv, dkv_there, rows_mine)
    dkv_mine = [dkv_mine[0]] + [gate(dkv_mine[x], rows_mp[x - 1]) for x in range(1, groups)]
    dkv = deal(dkv_mine)

    head_sent, head_kept = head_grad(
        place, normed_one, rows_mine, rows_mp, dq_mine, dkv_mine, []
    )
    ffn_part = feed(place, active, active_sent, w_down, [head_sent])
    down_there = gate(down_there, head_sent)
    down_kept, down_sent, down_there = stage(last_turn, down_kept, down_there)
    up_there = gate(up_there, down_sent, ffn_part)
    for k in range(last_turn):
        up_kept, up_sent, up_there = stage(k, up_kept, up_there)
    dkv = [dkv[0]] + [gate(piece, up_sent, weight=HOLD) for piece in dkv[1:]]
    head_there = swap(gate(head_sent, up_sent), "dp", 2, 1)
    back_part, head_sums = unproject(place, w_qkv, dq, dkv, [])
    back_there = swap(back_part, "mp", 2, 1)
    head_there = gate(head_there, back_part)
    down_there = gate(down_there, back_part)

    kept = (head_kept + head_there.astype(F32)).reshape(groups, cols // 2, 2 * rows_here, 3 * HD)
    for bit in bits(cols // 2):
        here = now("sr", 2 * bit)[0]
        view = kept.reshape(groups, -1, 2, 2 * rows_here, 3 * HD)
        sent = lax.dynamic_index_in_dim(view, 1 - here, 2, keepdims=False).astype(BF16)
        kept = lax.dynamic_index_in_dim(view, here, 2, keepdims=False)
        kept = kept + swap(sent, "sr", cols, 2 * bit).astype(F32)
    kept = kept.reshape(groups, 2, rows_here, 3 * HD)
    low = kept.astype(BF16)
    pieces = [lax.dynamic_index_in_dim(low, me ^ x, 0, keepdims=False) for x in range(groups)]
    pieces_sent = pieces
    pieces = deal(pieces)
    up_there = gate(up_there, pieces_sent[1], weight=HOLD)
    up_kept, up_sent, up_there = stage(last_turn, up_kept, up_there)
    grad_inputs, small = last_rows(
        inputs,
        back_part,
        gate(back_there, up_sent),
        grad_mid,
        norm_gain,
        row_sums,
        unit_sums,
        head_sums,
        [],
    )
    down = (down_kept + gate(down_there, small).astype(F32)).reshape(2, rows_here, -1)
    ffn_part = gate(ffn_part, small)
    small = sum_over(small, (("sr", cols), ("dp", n_dp)))
    ffn_other = gate(swap(ffn_part, "mp", 2, 1), small).astype(F32)
    outputs = (mixed + ffn_part.astype(F32) + ffn_other + out_bias[1]).astype(BF16)

    far_bits = bits(groups)
    small_there = swap(small, "sg", groups, far_bits[0])

    def with_near(x):
        sent = lax.dynamic_index_in_dim(x, 1 - near, 0, keepdims=False).astype(BF16)
        mine = lax.dynamic_index_in_dim(x, near, 0, keepdims=False)
        return sent, mine, swap(sent, "sr", cols, 1)

    def units_in_order(mine, there):
        return jnp.where(
            near == 0, jnp.concatenate([mine, there], 1), jnp.concatenate([there, mine], 1)
        )

    _, down_mine, down_there = with_near(down)
    pieces = [pieces[0]] + [gate(piece, up_sent) for piece in pieces[1:]]
    pieces[0] = lax.dynamic_index_in_dim(kept, me, 0, keepdims=False)
    heads_all = jnp.concatenate(
        [
            sum(jnp.where((me ^ x) == h, pieces[x].astype(F32), 0.0) for x in range(groups))
            for h in range(groups)
        ],
        2,
    )
    head_sent, mine, there = with_near(heads_all)
    grad_down = units_in_order(down_mine, gate(down_there, head_sent)).T
    up = up_kept + gate(up_there, grad_down).astype(F32)
    up_sent, up_mine, up_there = with_near(up.reshape(2, rows_here, -1))
    small = small + gate(small_there, up_sent)
    small_there = swap(small, "sg", groups, far_bits[1])
    there = gate(there, small)
    grad_qkv = (mine + there).reshape(rows_here, groups, 3, HD)
    grad_qkv = grad_qkv.transpose(2, 0, 1, 3).reshape(3, rows_here, width)
    for bit in far_bits[2:]:
        small = small + small_there
        small_there = swap(small, "sg", groups, bit)
    grad_gain, grad_shift, grad_qv_bias, grad_up_bias, grad_bias = finish_small(
        small, gate(small_there, grad_qkv), width
    )
    grad_up, grad_out = finish_units(place, up_mine, up_there, width, [grad_gain])

    return (
        outputs,
        grad_inputs,
        grad_gain,
        grad_shift,
        grad_qkv,
        grad_qv_bias,
        grad_out,
        grad_up,
        grad_up_bias.reshape(-1),
        grad_down,
        grad_bias,
    )


def solution(mesh):
    n_dp, n_seq, n_mp = mesh.shape["dp"], mesh.shape["seq"], mesh.shape["mp"]
    groups = 4
    cols = n_seq // groups
    inner = Mesh(mesh.devices.reshape(n_dp, groups, cols, n_mp), ("dp", "sg", "sr", "mp"))
    rows = ("dp", "sg", "sr")
    return jax.shard_map(
        functools.partial(body, (n_dp, groups, cols)),
        mesh=inner,
        in_specs=(
            P(rows, None),
            P("dp", None),
            P("mp"),
            P(),
            P(),
            P(None, None, "mp"),
            P(None, "mp"),
            P("mp", None),
            P(None, "mp"),
            P("mp"),
            P("mp", None),
            P(),
            P(rows, None),
        ),
        out_specs=(
            P(rows, None),
            P(rows, None),
            P(),
            P(),
            P(None, rows, "mp"),
            P(None, "mp"),
            P("mp", rows),
            P(rows, "mp"),
            P("mp"),
            P("mp", rows),
            P(),
        ),
        check_vma=False,
    )
```

```python
import functools
import math

import jax
import jax.numpy as jnp
from jax import lax
from jax.experimental import pallas as pl
from jax.experimental.pallas import tpu as pltpu
from jax.sharding import Mesh
from jax.sharding import PartitionSpec as P

D = 1024
HD = 128
BF16 = jnp.bfloat16
F32 = jnp.float32

norm_eps = 1e-05
masked_fill = -1e30
score_scale = HD ** (-0.5)

NT = (((1,), (1,)), ((), ()))
NN = (((1,), (0,)), ((), ()))
TN = (((0,), (0,)), ((), ()))


def mm(a, b, dims=NN):
    return lax.dot_general(a, b, dims, preferred_element_type=F32)


def doc_start(docs_ref, position):
    start = jnp.zeros_like(position)
    bound = jnp.int32(0)
    for d in range(docs_ref.shape[1]):
        bound = bound + docs_ref[0, d]
        start = jnp.where(position >= bound, bound, start)
    return start


def key_span(docs_ref, kb, z_count, cols, col, tok):
    z_key, col_key = kb // cols, lax.rem(kb, cols)
    first = z_key + (col_key > col).astype(jnp.int32)
    end = jnp.int32(0)
    barred = (col_key == col).astype(jnp.int32)
    for z in range(z_count):
        block = z * cols + col
        end = end + (doc_start(docs_ref, block * tok) < (kb + 1) * tok).astype(jnp.int32)
        late = (doc_start(docs_ref, block * tok + tok - 1) > kb * tok) & (block >= kb)
        barred = barred | late.astype(jnp.int32)
    return first, jnp.maximum(end - first, 0), barred


def column_setup(docs_ref, slope, groups, cols, col, tok, pos_s, start_s, rise_s):
    for z in range(groups):
        lanes = slice(z * tok, (z + 1) * tok)
        at = (z * cols + col) * tok + lax.broadcasted_iota(jnp.int32, (1, tok), 1)
        pos_s[:, lanes] = at
        start_s[:, lanes] = doc_start(docs_ref, at)
    rise_s[...] = slope * lax.broadcasted_iota(jnp.int32, (tok, 128), 0).astype(F32)


def widened(rise, width):
    return jnp.concatenate([rise] * (width // 128), axis=1)


def over_key_blocks(docs_ref, groups, cols, col, tok, run, none=None):
    blocks = groups * cols

    def step(i, carry):
        kb = blocks - 1 - i
        first, count, barred = key_span(docs_ref, kb, groups, cols, col, tok)
        for n in range(1, groups + 1):
            for masked in (True, False):

                @pl.when((count == n) & (barred == int(masked)))
                def _(n=n, masked=masked):
                    run(kb, pl.multiple_of(first * tok, 128), n * tok, masked)

        if none is not None:

            @pl.when(count == 0)
            def _():
                none(kb)

        return carry

    lax.fori_loop(0, blocks, step, 0)


def allowed(kb, at, start, tok, width):
    keys = kb * tok + lax.broadcasted_iota(jnp.int32, (tok, width), 0)
    return (keys <= at) & (keys >= start)


def natural_order(place_ref, n_groups, n_cols, q_refs, kv_refs, other_refs, store_query, store_key):
    me, col = place_ref[0], place_ref[1]
    for x in range(n_groups):
        z = me ^ x
        store_query(z, q_refs[x])
        store_key(z * n_cols + col, kv_refs[x])
        for s in range(1, n_cols):
            store_key(z * n_cols + (col ^ s), other_refs[(s - 1) * n_groups + x])


def block_rows(z, tok):
    return pl.ds(pl.multiple_of(z * tok, 128), tok)


def forward_kernel(groups, cols, tok, n_after, place_ref, docs_ref, slope_ref, *refs):
    n_other = (cols - 1) * groups
    q_refs, refs = refs[:groups], refs[groups:]
    kv_refs, refs = refs[:groups], refs[groups:]
    other_refs, refs = refs[:n_other], refs[n_other + n_after :]
    outs, (ot_ref, lse_ref), scratch = refs[:groups], refs[groups : groups + 2], refs[groups + 2 :]
    q_s, k_s, vt_s, pos_s, start_s, rise_s, top_s, total_s = scratch
    me, col = place_ref[0], place_ref[1]
    slope = slope_ref[me]

    def store_query(z, piece):
        q_s[block_rows(z, tok)] = piece[...]

    def store_key(block, piece):
        k_s[block] = piece[0]
        vt_s[block] = piece[1].T

    natural_order(place_ref, groups, cols, q_refs, kv_refs, other_refs, store_query, store_key)
    column_setup(docs_ref, slope, groups, cols, col, tok, pos_s, start_s, rise_s)
    top_s[...] = jnp.full(top_s.shape, masked_fill, F32)
    total_s[...] = jnp.zeros_like(total_s)
    ot_ref[...] = jnp.zeros_like(ot_ref)

    def run(kb, base, width, masked):
        lanes = pl.ds(base, width)
        at = pos_s[:, lanes]
        row = slope * (kb * tok - at).astype(F32)
        scores = mm(k_s[kb], q_s[lanes], NT) + widened(rise_s[...], width)
        if masked:
            scores = jnp.where(allowed(kb, at, start_s[:, lanes], tok, width), scores, masked_fill)
        top = jnp.maximum(top_s[:, lanes], jnp.max(scores, axis=0, keepdims=True) + row)
        weights = jnp.exp(scores - (top - row))
        rescale = jnp.exp(top_s[:, lanes] - top)
        top_s[:, lanes] = top
        total_s[:, lanes] = total_s[:, lanes] * rescale + jnp.sum(weights, axis=0, keepdims=True)
        ot_ref[:, lanes] = ot_ref[:, lanes] * rescale + mm(vt_s[kb], weights.astype(BF16))

    over_key_blocks(docs_ref, groups, cols, col, tok, run)
    total = total_s[...]
    ot_ref[...] = ot_ref[...] / total
    lse_ref[...] = top_s[...] + jnp.log(total)
    for x in range(groups):
        outs[x][...] = ot_ref[:, block_rows(me ^ x, tok)].T.astype(BF16)


def backward_kernel(groups, cols, tok, n_after, place_ref, docs_ref, slope_ref, *refs):
    n_other = (cols - 1) * groups
    q_refs, refs = refs[:groups], refs[groups:]
    kv_refs, refs = refs[:groups], refs[groups:]
    other_refs, refs = refs[:n_other], refs[n_other:]
    grads, (ot_ref, lse_ref) = refs[:groups], refs[groups : groups + 2]
    refs = refs[groups + 2 + n_after :]
    dq_refs, own_ref, refs = refs[:groups], refs[groups], refs[groups + 1 :]
    if cols > 1:
        other_ref, refs = refs[0], refs[1:]
    q_s, k_s, v_s, kt_s, do_s, pos_s, start_s, rise_s, delta_s, dqt_s = refs
    me, col = place_ref[0], place_ref[1]
    slope = slope_ref[me]

    def store_query(z, piece):
        q_s[block_rows(z, tok)] = piece[...]

    def store_key(block, piece):
        k_s[block] = piece[0]
        v_s[block] = piece[1]
        kt_s[block] = piece[0].T

    natural_order(place_ref, groups, cols, q_refs, kv_refs, other_refs, store_query, store_key)
    column_setup(docs_ref, slope, groups, cols, col, tok, pos_s, start_s, rise_s)
    for x in range(groups):
        rows = block_rows(me ^ x, tok)
        grad = grads[x][...]
        do_s[rows] = grad
        delta_s[:, rows] = jnp.sum(grad.astype(F32).T * ot_ref[:, rows], axis=0, keepdims=True)
    dqt_s[...] = jnp.zeros_like(dqt_s)

    def store(kb, dk, dv):
        x, s = (kb // cols) ^ me, lax.rem(kb, cols) ^ col

        @pl.when(s == 0)
        def _():
            own_ref[x, 0] = dk
            own_ref[x, 1] = dv

        if cols > 1:

            @pl.when(s != 0)
            def _():
                other_ref[s - 1, x, 0] = dk.astype(BF16)
                other_ref[s - 1, x, 1] = dv.astype(BF16)

    def run(kb, base, width, masked):
        lanes = pl.ds(base, width)
        at = pos_s[:, lanes]
        row = slope * (kb * tok - at).astype(F32)
        query, grad = q_s[lanes], do_s[lanes]
        scores = mm(k_s[kb], query, NT) + widened(rise_s[...], width)
        probs = jnp.exp(scores - (lse_ref[:, lanes] - row))
        if masked:
            probs = jnp.where(allowed(kb, at, start_s[:, lanes], tok, width), probs, 0.0)
        dv = mm(probs.astype(BF16), grad)
        grad_scores = (probs * (mm(v_s[kb], grad, NT) - delta_s[:, lanes])).astype(BF16)
        dk = mm(grad_scores, query)
        dqt_s[:, lanes] += mm(kt_s[kb], grad_scores)
        store(kb, dk, dv)

    def none(kb):
        store(kb, jnp.zeros((tok, HD), F32), jnp.zeros((tok, HD), F32))

    over_key_blocks(docs_ref, groups, cols, col, tok, run, none)
    for x in range(groups):
        dq_refs[x][...] = (dqt_s[:, block_rows(me ^ x, tok)] * score_scale).T.astype(BF16)


SMEM = pl.BlockSpec(memory_space=pltpu.SMEM)
VMEM = pl.BlockSpec(memory_space=pltpu.VMEM)
ANY = pl.BlockSpec(memory_space=pl.ANY)
VMEM_BYTES = 66900000
COST = 1000
HOLD = 20 * 10**9
UP_HOLD = 5 * HOLD
LEAST_BYTES = 66900000
gelu_slope = (2.0 / 3.141592653589793) ** 0.5


def call(kernel, name, out_shape, specs, operands, scratch=(), after=(), room=8, flops=0, moved=0, exps=0):
    held = [*operands, *out_shape, *scratch]
    held = sum(math.prod(x.shape) * jnp.dtype(x.dtype).itemsize for x in held)
    limit = max(LEAST_BYTES, min(VMEM_BYTES, held * 9 // 8 + room * 2**20))
    results = pl.pallas_call(
        kernel,
        out_shape=out_shape,
        in_specs=list(specs) + [ANY] * len(after),
        out_specs=[VMEM] * len(out_shape),
        scratch_shapes=list(scratch),
        compiler_params=pltpu.CompilerParams(vmem_limit_bytes=limit),
        cost_estimate=pl.CostEstimate(flops=flops // COST, bytes_accessed=moved // COST, transcendentals=exps // COST),
        name=name,
    )(*operands, *after)
    return list(results)


def attend_forward(place, docs, slope, q, kv, others, groups, cols, tok, after):
    blocks = groups * cols
    operands = (place, docs, slope, *q, *kv, *others)
    out_shape = [jax.ShapeDtypeStruct((tok, HD), BF16)] * groups + [
        jax.ShapeDtypeStruct((HD, groups * tok), F32),
        jax.ShapeDtypeStruct((1, groups * tok), F32),
    ]
    results = call(
        functools.partial(forward_kernel, groups, cols, tok, len(after)),
        "attend_forward",
        out_shape,
        [SMEM] * 3 + [VMEM] * (len(operands) - 3),
        operands,
        [
            pltpu.VMEM((groups * tok, HD), BF16),
            pltpu.VMEM((blocks, tok, HD), BF16),
            pltpu.VMEM((blocks, HD, tok), BF16),
            pltpu.VMEM((1, groups * tok), jnp.int32),
            pltpu.VMEM((1, groups * tok), jnp.int32),
            pltpu.VMEM((tok, 128), F32),
            pltpu.VMEM((1, groups * tok), F32),
            pltpu.VMEM((1, groups * tok), F32),
        ],
        after,
        16,
        2 * blocks * groups * tok * tok * HD,
        2 * (groups + 2 * blocks) * tok * HD,
        blocks * groups * tok * tok // 2,
    )
    return results[:groups], results[groups], results[groups + 1]


def attend_backward(place, docs, slope, q, kv, others, grads, ot, lse, groups, cols, tok, after):
    blocks = groups * cols
    operands = (place, docs, slope, *q, *kv, *others, *grads, ot, lse)
    out_shape = [jax.ShapeDtypeStruct((tok, HD), BF16)] * groups + [
        jax.ShapeDtypeStruct((groups, 2, tok, HD), F32)
    ]
    if cols > 1:
        out_shape.append(jax.ShapeDtypeStruct((cols - 1, groups, 2, tok, HD), BF16))
    results = call(
        functools.partial(backward_kernel, groups, cols, tok, len(after)),
        "attend_backward",
        out_shape,
        [SMEM] * 3 + [VMEM] * (len(operands) - 3),
        operands,
        [
            pltpu.VMEM((groups * tok, HD), BF16),
            pltpu.VMEM((blocks, tok, HD), BF16),
            pltpu.VMEM((blocks, tok, HD), BF16),
            pltpu.VMEM((blocks, HD, tok), BF16),
            pltpu.VMEM((groups * tok, HD), BF16),
            pltpu.VMEM((1, groups * tok), jnp.int32),
            pltpu.VMEM((1, groups * tok), jnp.int32),
            pltpu.VMEM((tok, 128), F32),
            pltpu.VMEM((1, groups * tok), F32),
            pltpu.VMEM((HD, groups * tok), F32),
        ],
        after,
        24,
        14 * 10**9 * COST,
    )
    return results[:groups], results[groups], (results[groups + 1] if cols > 1 else None)


def rows_of(ref, part, size):
    return ref[pl.ds(pl.multiple_of(part * size, 16), size)]


def norm_rows(values):
    mean = jnp.mean(values, axis=-1, keepdims=True)
    centered = values - mean
    spread = jnp.mean(centered * centered, axis=-1, keepdims=True)
    return centered * lax.rsqrt(spread + norm_eps)


def mix_kernel(heads, n_after, place_ref, w_ref, *refs):
    pieces, out_ref, att_ref = refs[:heads], refs[heads + n_after], refs[heads + n_after + 1]
    for x in range(heads):
        head = place_ref[0] ^ x
        att_ref[:, pl.ds(pl.multiple_of(head * HD, HD), HD)] = pieces[x][...]
    out_ref[...] = mm(att_ref[...], w_ref[...]).astype(BF16)


def mix_heads(place, w_out, pieces, after):
    tok, heads = pieces[0].shape[0], len(pieces)
    return call(
        functools.partial(mix_kernel, heads, len(after)),
        "mix_heads",
        [jax.ShapeDtypeStruct((tok, D), BF16), jax.ShapeDtypeStruct((tok, heads * HD), BF16)],
        [SMEM] + [VMEM] * (heads + 1),
        (place, w_out, *pieces),
        after=after,
        flops=2 * tok * D * heads * HD,
        moved=2 * (tok * D + D * heads * HD),
    )


def unproject_kernel(heads, n_after, place_ref, w_ref, *refs):
    dq, dkv = refs[:heads], refs[heads : 2 * heads]
    out_ref, sum_ref, wide_s = refs[2 * heads + n_after :]
    for x in range(heads):
        head = place_ref[0] ^ x
        lanes = pl.ds(pl.multiple_of(head * HD, HD), HD)
        wide_s[0, :, lanes] = dq[x][...]
        wide_s[1, :, lanes] = dkv[x][0]
        wide_s[2, :, lanes] = dkv[x][1]
    total = mm(wide_s[0], w_ref[0], NT)
    for j in (1, 2):
        total = total + mm(wide_s[j], w_ref[j], NT)
    out_ref[...] = total.astype(BF16)
    sum_ref[0:1] = jnp.sum(wide_s[0].astype(F32), axis=0, keepdims=True)
    sum_ref[1:2] = jnp.sum(wide_s[2].astype(F32), axis=0, keepdims=True)


def unproject(place, w_qkv, dq, dkv, after):
    tok, heads = dq[0].shape[0], len(dq)
    return call(
        functools.partial(unproject_kernel, heads, len(after)),
        "unproject",
        [jax.ShapeDtypeStruct((tok, D), BF16), jax.ShapeDtypeStruct((2, heads * HD), F32)],
        [SMEM] + [VMEM] * (2 * heads + 1),
        (place, w_qkv, *dq, *dkv),
        [pltpu.VMEM((3, tok, heads * HD), BF16)],
        after=after,
        flops=6 * tok * D * heads * HD,
        moved=2 * (tok * D + 3 * D * heads * HD),
    )


def project_kernel(heads, place_ref, x_ref, gain_ref, shift_ref, w_ref, bias_ref, *refs):
    normed_ref, half_ref, q_refs, kv_refs = refs[0], refs[1], refs[2 : 2 + heads], refs[2 + heads : -1]
    out_s = refs[-1]
    normed = norm_rows(x_ref[...].astype(F32)) * gain_ref[0:1] + shift_ref[0:1]
    normed = normed.astype(BF16)
    normed_ref[...] = normed
    half_ref[...] = rows_of(normed_ref, place_ref[3], half_ref.shape[0])
    for j in range(3):
        product = mm(normed, w_ref[j])
        if j == 0:
            product = (product + bias_ref[0:1]) * score_scale
        if j == 2:
            product = product + bias_ref[1:2]
        product = product.astype(BF16)
        for h in range(heads):
            out_s[h, j] = product[:, h * HD : (h + 1) * HD]
    for x in range(heads):
        head = place_ref[0] ^ x
        q_refs[x][...] = out_s[head, 0]
        kv_refs[x][...] = out_s[head, 1:3]


def project(place, inputs, gain, shift, w_qkv, qv_bias):
    tok = inputs.shape[0]
    heads = w_qkv.shape[2] // HD
    out_shape = (
        [jax.ShapeDtypeStruct((tok, D), BF16), jax.ShapeDtypeStruct((tok // 2, D), BF16)]
        + [jax.ShapeDtypeStruct((tok, HD), BF16)] * heads
        + [jax.ShapeDtypeStruct((2, tok, HD), BF16)] * heads
    )
    results = call(
        functools.partial(project_kernel, heads),
        "project",
        out_shape,
        [SMEM] + [VMEM] * 5,
        (place, inputs, gain, shift, w_qkv, qv_bias),
        [pltpu.VMEM((heads, 3, tok, HD), BF16)],
    )
    return results[0], results[1], results[2 : 2 + heads], results[2 + heads :]


def middle_kernel(n_after, place_ref, x_ref, part_ref, other_ref, bias_ref, gain_ref, shift_ref, *refs):
    mixed_ref, normed_ref, half_ref = refs[n_after:]
    parts = part_ref[...].astype(F32) + other_ref[...].astype(F32)
    mixed = x_ref[...].astype(F32) + parts + bias_ref[0:1]
    mixed_ref[...] = mixed
    normed_ref[...] = (norm_rows(mixed) * gain_ref[1:2] + shift_ref[1:2]).astype(BF16)
    half_ref[...] = rows_of(normed_ref, place_ref[3], half_ref.shape[0])


def middle(place, inputs, part, other, out_bias, gain, shift, after=()):
    tok = inputs.shape[0]
    return call(
        functools.partial(middle_kernel, len(after)),
        "middle",
        [
            jax.ShapeDtypeStruct((tok, D), F32),
            jax.ShapeDtypeStruct((tok, D), BF16),
            jax.ShapeDtypeStruct((tok // 2, D), BF16),
        ],
        [SMEM] + [VMEM] * 6,
        (place, inputs, part, other, out_bias, gain, shift),
        after=after,
    )


def hidden_kernel(place_ref, normed_ref, half_ref, w_ref, bias_ref, grad_ref, *refs):
    act_sent, grad_sent, act_mine, grad_mine, back_ref, sum_ref = refs
    near, (tok, width) = place_ref[1] % 2, act_mine.shape
    grad_sent[tok:] = half_ref[...]
    total = None
    for act_ref, out_ref, side in ((act_sent, grad_sent, 1 - near), (act_mine, grad_mine, near)):
        cut = pl.ds(pl.multiple_of(side * width, 128), width)
        u = mm(normed_ref[...], w_ref[:, cut]) + bias_ref[:, cut]
        square = u * u
        bend = jnp.tanh(u * (gelu_slope + gelu_slope * 0.044715 * square))
        half = 0.5 + 0.5 * bend
        act_ref[...] = (u * half).astype(BF16)
        lean = u * (0.5 - 0.5 * bend * bend)
        rise = half + lean * (gelu_slope + (3 * 0.044715 * gelu_slope) * square)
        grad = (rise * grad_ref[:, cut]).astype(BF16)
        out_ref[:tok] = grad
        sum_ref[:, cut] = column_sum(grad.astype(F32))
        back = mm(grad, w_ref[:, cut], NT)
        total = back if total is None else total + back
    back_ref[...] = total.astype(BF16)


def hidden_units(place, normed, half, w_up, up_bias, grad_active, after=()):
    tok, total = normed.shape[0], w_up.shape[1]
    assert total // 2 == D
    act_sent, grad_sent, act_mine, grad_mine, back, sums = call(
        hidden_kernel,
        "hidden_units",
        [
            jax.ShapeDtypeStruct((tok, total // 2), BF16),
            jax.ShapeDtypeStruct((tok + tok // 2, total // 2), BF16),
            jax.ShapeDtypeStruct((tok, total // 2), BF16),
            jax.ShapeDtypeStruct((tok, total // 2), BF16),
            jax.ShapeDtypeStruct((tok, D), BF16),
            jax.ShapeDtypeStruct((1, total), F32),
        ],
        [SMEM] + [VMEM] * 5,
        (place, normed, half, w_up, up_bias, grad_active),
        room=16,
    )
    return act_mine, act_sent, grad_mine, grad_sent, back, sums


def column_sum(values):
    return jnp.sum(values, axis=0, keepdims=True)


def norm_back(values, grad, gain):
    mean = jnp.mean(values, axis=-1, keepdims=True)
    centered = values - mean
    scale = lax.rsqrt(jnp.mean(centered * centered, axis=-1, keepdims=True) + norm_eps)
    normed = centered * scale
    inner = grad * gain
    along = jnp.mean(inner * normed, axis=-1, keepdims=True)
    back = scale * (inner - jnp.mean(inner, axis=-1, keepdims=True) - normed * along)
    return back, column_sum(grad * normed), column_sum(grad)


def turn_kernel(heads, n_after, place_ref, mixed_ref, part_ref, other_ref, low_ref, gain_ref, w_ref, *refs):
    mid_ref, low_out_ref, sum_ref = refs[n_after : n_after + 3]
    pieces, head_s = refs[n_after + 3 : -1], refs[-1]
    grad = part_ref[...].astype(F32) + other_ref[...].astype(F32)
    back, gain_sum, shift_sum = norm_back(mixed_ref[...], grad, gain_ref[1:2])
    low_in = low_ref[...].astype(F32)
    mid = low_in + back
    mid_ref[...] = mid
    low = mid.astype(BF16)
    low_out_ref[...] = low
    sum_ref[0:1] = gain_sum
    sum_ref[1:2] = shift_sum
    sum_ref[2:3] = jnp.sum(low.astype(F32), axis=0, keepdims=True)
    sum_ref[3:4] = jnp.sum(low_in, axis=0, keepdims=True)
    product = mm(low, w_ref[...], NT).astype(BF16)
    for h in range(heads):
        head_s[h] = product[:, h * HD : (h + 1) * HD]
    for x in range(heads):
        pieces[x][...] = head_s[place_ref[0] ^ x]


def turn_back(place, mixed, part, other, cotangent, gain, w_out, after=()):
    tok, heads = mixed.shape[0], w_out.shape[0] // HD
    results = call(
        functools.partial(turn_kernel, heads, len(after)),
        "turn_back",
        [
            jax.ShapeDtypeStruct((tok, D), F32),
            jax.ShapeDtypeStruct((tok, D), BF16),
            jax.ShapeDtypeStruct((4, D), F32),
        ]
        + [jax.ShapeDtypeStruct((tok, HD), BF16)] * heads,
        [SMEM] + [VMEM] * 6,
        (place, mixed, part, other, cotangent, gain, w_out),
        [pltpu.VMEM((heads, tok, HD), BF16)],
        after=after,
    )
    return results[0], results[1], results[2], results[3:]


def last_kernel(n_after, x_ref, part_ref, other_ref, mid_ref, gain_ref, sums_ref, units_ref, heads_ref, *refs):
    out_ref, small_ref = refs[n_after:]
    grad = part_ref[...].astype(F32) + other_ref[...].astype(F32)
    back, gain_sum, shift_sum = norm_back(x_ref[...].astype(F32), grad, gain_ref[0:1])
    out_ref[...] = mid_ref[...] + back
    small_ref[0:4] = sums_ref[...]
    small_ref[4:5] = gain_sum
    small_ref[5:6] = shift_sum
    small_ref[6:7, : heads_ref.shape[1]] = heads_ref[0:1]
    small_ref[6:7, heads_ref.shape[1] :] = heads_ref[1:2]
    for k in range(units_ref.shape[1] // D):
        small_ref[7 + k : 8 + k] = units_ref[:, k * D : (k + 1) * D]


def last_rows(inputs, part, other, grad_mid, gain, sums, unit_sums, head_sums, after=()):
    tok = inputs.shape[0]
    return call(
        functools.partial(last_kernel, len(after)),
        "last_rows",
        [
            jax.ShapeDtypeStruct((tok, D), F32),
            jax.ShapeDtypeStruct((7 + unit_sums.shape[1] // D, D), F32),
        ],
        [VMEM] * 8,
        (inputs, part, other, grad_mid, gain, sums, unit_sums, head_sums),
        after=after,
    )


def feed_kernel(n_after, place_ref, mine_ref, sent_ref, w_ref, *refs):
    near, half = place_ref[1] % 2, mine_ref.shape[1]
    total = mm(mine_ref[...], rows_of(w_ref, near, half))
    total = total + mm(sent_ref[...], rows_of(w_ref, 1 - near, half))
    refs[n_after][...] = total.astype(BF16)


def feed(place, mine, sent, w_down, after):
    return call(
        functools.partial(feed_kernel, len(after)),
        "feed",
        [jax.ShapeDtypeStruct((mine.shape[0], D), BF16)],
        [SMEM] + [VMEM] * 3,
        (place, mine, sent, w_down),
        after=after,
    )[0]


def early_kernel(low_ref, w_ref, out_ref):
    out_ref[...] = mm(low_ref[...], w_ref[...], NT)


def early_grad(cotangent, w_down):
    return call(
        early_kernel,
        "early_grad",
        [jax.ShapeDtypeStruct((cotangent.shape[0], w_down.shape[0]), F32)],
        [VMEM] * 2,
        (cotangent, w_down),
    )[0]


def pair_grad_kernel(extra, halves, n_after, place_ref, rows_ref, units_ref, near_ref, *refs):
    near_rows, refs = refs[: 1 + halves], refs[1 + halves :]
    more, refs = refs[: 2 * extra], refs[2 * extra + n_after :]
    sent_ref, kept_ref, rows_s = refs
    dp, mp = place_ref[2], place_ref[3]
    tok, width = units_ref.shape
    if halves:
        half = near_rows[0].shape[0]
        for k in range(2):
            rows_s[pl.ds(pl.multiple_of((mp ^ k) * half, 16), half)] = near_rows[k][...]
    else:
        rows_s = near_rows[0]
    step = sent_ref.shape[0]
    for k, out_ref in ((1, sent_ref), (0, kept_ref)):
        cut = pl.ds(pl.multiple_of((dp ^ k) * step, 128), step)
        total = mm(rows_ref[:, cut], units_ref[...], TN) + mm(rows_s[:, cut], near_ref[:tok], TN)
        out_ref[:, :width] = total.astype(out_ref.dtype)
        if extra:
            out_ref[:, width:] = mm(more[0][:, cut], more[1][...], TN).astype(out_ref.dtype)


def pair_grad(place, rows, near_rows, units, near_units, more, after):
    tok, width = units.shape
    total = width + (more[1].shape[1] if more else 0)
    return call(
        functools.partial(pair_grad_kernel, int(bool(more)), len(near_rows) - 1, len(after)),
        "pair_grad",
        [jax.ShapeDtypeStruct((D // 2, total), BF16), jax.ShapeDtypeStruct((D // 2, total), F32)],
        [SMEM] + [VMEM] * (3 + len(near_rows) + len(more)),
        (place, rows, units, near_units, *near_rows, *more),
        [pltpu.VMEM((tok, D), BF16)],
        after=after,
    )


def head_grad_kernel(groups, n_after, place_ref, *refs):
    own_ref, mine, other = refs[0], refs[1:groups], refs[groups : 2 * groups - 1]
    dq, dkv = refs[2 * groups - 1 : 3 * groups - 1], refs[3 * groups - 1 : 4 * groups - 1]
    sent_ref, kept_ref, rows_s, grads_s = refs[4 * groups - 1 + n_after :]
    dp, mp = place_ref[2], place_ref[3]
    tok = own_ref.shape[0]
    half = tok // 2
    for x in range(groups):
        if x == 0:
            rows_s[0:tok] = own_ref[...]
        else:
            rows_s[pl.ds(pl.multiple_of(x * tok + mp * half, 16), half)] = mine[x - 1][...]
            rows_s[pl.ds(pl.multiple_of(x * tok + (1 - mp) * half, 16), half)] = other[x - 1][...]
        rows = slice(x * tok, (x + 1) * tok)
        grads_s[rows, :HD] = dq[x][...]
        grads_s[rows, HD : 2 * HD] = dkv[x][0]
        grads_s[rows, 2 * HD :] = dkv[x][1]
    step = sent_ref.shape[0]
    for k, out_ref in ((1, sent_ref), (0, kept_ref)):
        cut = pl.ds(pl.multiple_of((dp ^ k) * step, 128), step)
        out_ref[...] = mm(rows_s[:, cut], grads_s[...], TN).astype(out_ref.dtype)


def head_grad(place, own, mine, other, dq, dkv, after):
    tok, groups = own.shape[0], len(dq)
    return call(
        functools.partial(head_grad_kernel, groups, len(after)),
        "head_grad",
        [jax.ShapeDtypeStruct((D // 2, 3 * HD), BF16), jax.ShapeDtypeStruct((D // 2, 3 * HD), F32)],
        [SMEM] + [VMEM] * (4 * groups - 1),
        (place, own, *mine, *other, *dq, *dkv),
        [pltpu.VMEM((groups * tok, D), BF16), pltpu.VMEM((groups * tok, 3 * HD), BF16)],
        after=after,
        flops=2 * groups * tok * D * 3 * HD,
        moved=2 * groups * tok * (D + 3 * HD),
    )


def sum_kernel(groups, n_there, n_after, own_ref, *refs):
    there, outs = refs[:n_there], refs[n_there + n_after :]
    for x in range(groups):
        for j in range(2):
            total = own_ref[x, j]
            for ref in there:
                total = total + ref[0, x, j].astype(F32)
            outs[x][j] = total.astype(BF16)


def sum_columns(own, there, after):
    groups, _, tok, _ = own.shape
    return call(
        functools.partial(sum_kernel, groups, len(there), len(after)),
        "sum_columns",
        [jax.ShapeDtypeStruct((2, tok, HD), BF16)] * groups,
        [VMEM] * (1 + len(there)),
        (own, *there),
        after=after,
        moved=10 * own.size,
    )


def fold_kernel(outer, inner, n_after, now_ref, kept_ref, there_ref, *refs):
    mine_ref, sent_ref = refs[n_after:]
    for o in range(outer):
        for k, ref in ((0, mine_ref), (1, sent_ref)):
            at = pl.ds(pl.multiple_of((2 * o + (now_ref[0] ^ k)) * inner, 16), inner)
            total = kept_ref[at] + there_ref[at].astype(F32)
            ref[o * inner : (o + 1) * inner] = total.astype(ref.dtype)


def fold(now, kept, there, inner, after=()):
    rows, width = kept.shape
    return call(
        functools.partial(fold_kernel, rows // (2 * inner), inner, len(after)),
        "fold",
        [jax.ShapeDtypeStruct((rows // 2, width), F32), jax.ShapeDtypeStruct((rows // 2, width), BF16)],
        [SMEM, VMEM, VMEM],
        (now, kept, there),
        after=after,
        moved=9 * kept.size,
    )


def both_halves(near, mine, there, out_ref, half):
    out_ref[:, pl.ds(pl.multiple_of(near * half, 128), half)] = mine
    out_ref[:, pl.ds(pl.multiple_of((1 - near) * half, 128), half)] = there


def finish_kernel(width, n_after, place_ref, mine_ref, there_ref, h_ref, h_there_ref, d_ref, d_there_ref, *refs):
    gain_ref, shift_ref, heads_ref, units_ref, bias_ref, qkv_ref, down_ref = refs[n_after:]
    total = mine_ref[...] + there_ref[...]
    gain_ref[0:1], gain_ref[1:2] = total[4:5], total[0:1]
    shift_ref[0:1], shift_ref[1:2] = total[5:6], total[1:2]
    heads_ref[0:1], heads_ref[1:2] = total[6:7, :width], total[6:7, width:]
    for k in range(units_ref.shape[1] // D):
        units_ref[:, k * D : (k + 1) * D] = total[7 + k : 8 + k]
    bias_ref[...] = total[2:4]
    rows = h_ref[...] + h_there_ref[...].astype(F32)
    for h in range(width // HD):
        for j in range(3):
            at = (3 * h + j) * HD
            qkv_ref[j, :, h * HD : (h + 1) * HD] = rows[:, at : at + HD]
    both_halves(place_ref[1] % 2, d_ref[...], d_there_ref[...].astype(F32), down_ref, d_ref.shape[1])


def finish(place, small, small_there, heads, heads_there, down, down_there, width, after):
    rows = heads.shape[0]
    shapes = [(2, D), (2, D), (2, width), (1, (small.shape[0] - 7) * D), (2, D)]
    shapes += [(3, rows, width), (rows, 2 * down.shape[1])]
    return call(
        functools.partial(finish_kernel, width, len(after)),
        "finish",
        [jax.ShapeDtypeStruct(shape, F32) for shape in shapes],
        [SMEM] + [VMEM] * 6,
        (place, small, small_there, heads, heads_there, down, down_there),
        after=after,
    )


def finish_units_kernel(n_after, place_ref, mine_ref, there_ref, *refs):
    up_ref, out_ref = refs[n_after:]
    half = up_ref.shape[1] // 2
    there = there_ref[...].astype(F32)
    both_halves(place_ref[1] % 2, mine_ref[:, :half], there[:, :half], up_ref, half)
    out_ref[...] = mine_ref[:, half:] + there[:, half:]


def finish_units(place, mine, there, width, after):
    rows, total = mine.shape
    return call(
        functools.partial(finish_units_kernel, len(after)),
        "finish_units",
        [
            jax.ShapeDtypeStruct((rows, 2 * (total - width)), F32),
            jax.ShapeDtypeStruct((rows, width), F32),
        ],
        [SMEM, VMEM, VMEM],
        (place, mine, there),
        after=after,
    )


def pass_on(*refs):
    pass


def gate(x, *after, weight=0):
    return pl.pallas_call(
        pass_on,
        out_shape=jax.ShapeDtypeStruct(x.shape, x.dtype),
        in_specs=[ANY] * (1 + len(after)),
        out_specs=ANY,
        input_output_aliases={0: 0},
        cost_estimate=pl.CostEstimate(flops=weight, bytes_accessed=0, transcendentals=0),
        name="gate",
    )(x, *after)


def swap(x, axis, size, bit):
    return lax.ppermute(x, axis, [(i, i ^ bit) for i in range(size)])


def bits(size):
    return [1 << i for i in range(size.bit_length() - 1)]


def sum_over(vector, axes):
    for axis, size in axes:
        for bit in bits(size):
            vector = vector + swap(vector, axis, size, bit)
    return vector


def body(
    sizes,
    inputs,
    doc_lengths,
    slopes,
    norm_gain,
    norm_bias,
    w_qkv,
    qv_bias,
    w_out,
    w_up,
    up_bias,
    w_down,
    out_bias,
    cotangent,
):
    n_dp, groups, cols = sizes
    tok = inputs.shape[0]
    width = slopes.shape[0] * HD
    me, col = lax.axis_index("sg"), lax.axis_index("sr")
    mp, dp, near = lax.axis_index("mp"), lax.axis_index("dp"), lax.axis_index("sr") % 2
    place = jnp.stack([me, col, dp, mp]).astype(jnp.int32)

    def deal(pieces):
        return [pieces[x] if x == 0 else swap(pieces[x], "sg", groups, x) for x in range(groups)]

    def half_rows(x):
        return lax.dynamic_slice_in_dim(x, mp * (tok // 2), tok // 2, 0)

    normed_one, one_half, q, kv = project(place, inputs, norm_gain, norm_bias, w_qkv, qv_bias)
    grad_active = early_grad(cotangent, w_down)
    kv = deal(kv)
    others = [[swap(kv[0], "sr", cols, s)] for s in range(1, cols)]
    turn = (grad_active,)
    for x in range(1, groups):
        kv[x] = gate(kv[x], *turn, *[column[-1] for column in others])
        turn = ()
        for s in range(1, cols):
            others[s - 1].append(swap(kv[x], "sr", cols, s))
    others = [piece for column in others for piece in column]
    q = deal([q[0]] + [gate(piece, kv[groups - 2]) for piece in q[1:]])
    others[-1] = gate(others[-1], weight=5 * HOLD)
    outs, ot, lse = attend_forward(place, doc_lengths, slopes, q, kv, others, groups, cols, tok, [])
    low_near = swap(gate(cotangent, q[1]), "sr", cols, 1)
    low_near = gate(low_near, outs[0], weight=HOLD)
    outs = deal(outs)
    one_half = gate(one_half, outs[groups - 1])
    far = swap(one_half, "sg", groups, 2)
    attn_part, attended = mix_heads(place, w_out, outs, [low_near])
    mixed, normed_two, two_half = middle(
        place,
        inputs,
        attn_part,
        swap(attn_part, "mp", 2, 1),
        out_bias,
        norm_gain,
        norm_bias,
        [],
    )

    half_units = w_up.shape[1] // 2
    active, active_sent, grad_hidden, hidden_sent, back_two, unit_sums = hidden_units(
        place, normed_two, two_half, w_up, up_bias[None], grad_active
    )
    active_near = swap(active_sent, "sr", cols, 1)
    hidden_near = swap(hidden_sent, "sr", cols, 1)
    far = gate(far, back_two, weight=HOLD)
    grad_mid, grad_mid_low, row_sums, pieces = turn_back(
        place,
        mixed,
        back_two,
        swap(back_two, "mp", 2, 1),
        cotangent,
        norm_gain,
        w_out,
        [far],
    )
    grads = deal(pieces)

    down_sent, down_kept = pair_grad(
        place,
        cotangent,
        [low_near],
        active,
        active_near,
        (),
        [pieces[3]],
    )
    down_there = swap(down_sent, "dp", 2, 1)
    far = gate(far, down_sent, *grads[1:])
    last = swap(far, "sg", groups, 1)
    one_half = gate(one_half, far)
    beside = swap(one_half, "sg", groups, 1)
    dq, dkv, dkv_other = attend_backward(
        place,
        doc_lengths,
        slopes,
        q,
        kv,
        others,
        grads,
        ot,
        lse,
        groups,
        cols,
        tok,
        [down_sent, one_half],
    )
    dkv_there = [swap(dkv_other[s - 1 : s], "sr", cols, s) for s in range(1, cols)]
    beside = gate(beside, dq[0], weight=HOLD)
    last = gate(last, dq[0], weight=HOLD)
    hidden_near = gate(hidden_near, dq[0], weight=HOLD)
    dq_mine = [dq[0], gate(dq[1], beside), gate(dq[2], last), gate(dq[3], hidden_near)]
    dq = deal(dq_mine)
    two_near = hidden_near[tok:]
    two_near_mp = swap(two_near, "mp", 2, 1)

    rows_here = D // (2 * groups * cols)
    stages = [("sr", cols, 2 * bit) for bit in bits(cols // 2)]
    stages += [("sg", groups, bit) for bit in bits(groups)]

    def now(axis, bit):
        return ((lax.axis_index(axis) // bit) % 2).astype(jnp.int32).reshape(1)

    def stage(k, kept, there, *after):
        axis, size, bit = stages[k]
        kept, sent = fold(now(axis, bit), kept, there, 2 * rows_here, after)
        return kept, sent, swap(sent, axis, size, bit)

    last_turn = len(stages) - 1
    up_sent, up_kept = pair_grad(
        place,
        normed_two,
        [two_near, two_near_mp],
        grad_hidden,
        hidden_near,
        (grad_mid_low, attended),
        [dq_mine[3]],
    )
    down_there = gate(down_there, up_sent)
    for k in range(last_turn):
        down_kept, down_sent, down_there = stage(k, down_kept, down_there)
    up_there = swap(up_sent, "dp", 2, 1)
    dq = [dq[0]] + [gate(piece, down_sent, weight=HOLD) for piece in dq[1:]]
    dkv_there = [gate(piece, *dq[1:], weight=HOLD) for piece in dkv_there]
    rows_mine = [gate(piece, *dq[1:]) for piece in (beside, far, last)]
    rows_mp = [swap(piece, "mp", 2, 1) for piece in rows_mine]
    dkv_mine = sum_columns(dkv, dkv_there, rows_mine)
    dkv_mine = [dkv_mine[0]] + [gate(dkv_mine[x], rows_mp[x - 1]) for x in range(1, groups)]
    dkv = deal(dkv_mine)

    head_sent, head_kept = head_grad(
        place, normed_one, rows_mine, rows_mp, dq_mine, dkv_mine, []
    )
    ffn_part = feed(place, active, active_sent, w_down, [head_sent])
    down_there = gate(down_there, head_sent)
    down_kept, down_sent, down_there = stage(last_turn, down_kept, down_there)
    up_there = gate(up_there, down_sent, ffn_part)
    for k in range(last_turn):
        up_kept, up_sent, up_there = stage(k, up_kept, up_there)
    dkv = [dkv[0]] + [gate(piece, up_sent, weight=HOLD) for piece in dkv[1:]]
    head_there = swap(gate(head_sent, up_sent), "dp", 2, 1)
    back_part, head_sums = unproject(place, w_qkv, dq, dkv, [])
    back_there = swap(back_part, "mp", 2, 1)
    head_there = gate(head_there, back_part)
    down_there = gate(down_there, back_part)

    kept = (head_kept + head_there.astype(F32)).reshape(groups, cols // 2, 2 * rows_here, 3 * HD)
    for bit in bits(cols // 2):
        here = now("sr", 2 * bit)[0]
        view = kept.reshape(groups, -1, 2, 2 * rows_here, 3 * HD)
        sent = lax.dynamic_index_in_dim(view, 1 - here, 2, keepdims=False).astype(BF16)
        kept = lax.dynamic_index_in_dim(view, here, 2, keepdims=False)
        kept = kept + swap(sent, "sr", cols, 2 * bit).astype(F32)
    kept = kept.reshape(groups, 2, rows_here, 3 * HD)
    low = kept.astype(BF16)
    pieces = [lax.dynamic_index_in_dim(low, me ^ x, 0, keepdims=False) for x in range(groups)]
    pieces_sent = pieces
    pieces = deal(pieces)
    up_there = gate(up_there, pieces_sent[1], weight=HOLD)
    up_kept, up_sent, up_there = stage(last_turn, up_kept, up_there)
    grad_inputs, small = last_rows(
        inputs,
        back_part,
        gate(back_there, up_sent),
        grad_mid,
        norm_gain,
        row_sums,
        unit_sums,
        head_sums,
        [],
    )

    def with_near(x):
        sent = lax.dynamic_index_in_dim(x, 1 - near, 0, keepdims=False).astype(BF16)
        mine = lax.dynamic_index_in_dim(x, near, 0, keepdims=False)
        return sent, mine, swap(sent, "sr", cols, 1)

    def add_with_near(kept, there):
        if rows_here % 16:
            return with_near((kept + there.astype(F32)).reshape(2, rows_here, -1))
        mine, sent = fold(now("sr", 1), kept, there, rows_here)
        return sent, mine, swap(sent, "sr", cols, 1)

    _, down_mine, down_there = add_with_near(down_kept, gate(down_there, small))
    ffn_part = gate(ffn_part, small)
    small = sum_over(small, (("sr", cols), ("dp", n_dp)))
    ffn_other = gate(swap(ffn_part, "mp", 2, 1), small).astype(F32)
    outputs = (mixed + ffn_part.astype(F32) + ffn_other + out_bias[1]).astype(BF16)

    far_bits = bits(groups)
    small_there = swap(small, "sg", groups, far_bits[0])

    pieces = [pieces[0]] + [gate(piece, up_sent) for piece in pieces[1:]]
    pieces[0] = lax.dynamic_index_in_dim(kept, me, 0, keepdims=False)
    heads_all = jnp.concatenate(
        [
            sum(jnp.where((me ^ x) == h, pieces[x].astype(F32), 0.0) for x in range(groups))
            for h in range(groups)
        ],
        2,
    )
    head_sent, head_mine, head_near = with_near(heads_all)
    up_sent, up_mine, up_there = add_with_near(up_kept, gate(up_there, head_sent))
    for bit in far_bits[1:]:
        small = small + gate(small_there, up_sent)
        small_there = swap(small, "sg", groups, bit)
    grad_gain, grad_shift, grad_qv_bias, grad_up_bias, grad_bias, grad_qkv, grad_down = finish(
        place,
        small,
        small_there,
        head_mine,
        head_near,
        down_mine,
        down_there,
        width,
        [outputs],
    )
    grad_up, grad_out = finish_units(place, up_mine, up_there, width, [grad_gain])

    return (
        outputs,
        grad_inputs,
        grad_gain,
        grad_shift,
        grad_qkv,
        grad_qv_bias,
        grad_out.T,
        grad_up,
        grad_up_bias.reshape(-1),
        grad_down.T,
        grad_bias,
    )


def solution(mesh):
    n_dp, n_seq, n_mp = mesh.shape["dp"], mesh.shape["seq"], mesh.shape["mp"]
    groups = 4
    cols = n_seq // groups
    inner = Mesh(mesh.devices.reshape(n_dp, groups, cols, n_mp), ("dp", "sg", "sr", "mp"))
    rows = ("dp", "sg", "sr")
    return jax.shard_map(
        functools.partial(body, (n_dp, groups, cols)),
        mesh=inner,
        in_specs=(
            P(rows, None),
            P("dp", None),
            P("mp"),
            P(),
            P(),
            P(None, None, "mp"),
            P(None, "mp"),
            P("mp", None),
            P(None, "mp"),
            P("mp"),
            P("mp", None),
            P(),
            P(rows, None),
        ),
        out_specs=(
            P(rows, None),
            P(rows, None),
            P(),
            P(),
            P(None, rows, "mp"),
            P(None, "mp"),
            P("mp", rows),
            P(rows, "mp"),
            P("mp"),
            P("mp", rows),
            P(),
        ),
        check_vma=False,
    )
```

```python
import functools

import jax
import jax.numpy as jnp
from jax import lax
from jax.experimental import pallas as pl
from jax.experimental.pallas import tpu as pltpu
from jax.sharding import Mesh
from jax.sharding import PartitionSpec as P

D = 1024
HD = 128
BF16 = jnp.bfloat16
F32 = jnp.float32

norm_eps = 1e-05
masked_fill = -1e30
score_scale = HD ** (-0.5)

NT = (((1,), (1,)), ((), ()))
NN = (((1,), (0,)), ((), ()))
TN = (((0,), (0,)), ((), ()))


def mm(a, b, dims=NN):
    return lax.dot_general(a, b, dims, preferred_element_type=F32)


def doc_start(docs_ref, position):
    start = jnp.zeros_like(position)
    bound = jnp.int32(0)
    for d in range(docs_ref.shape[1]):
        bound = bound + docs_ref[0, d]
        start = jnp.where(position >= bound, bound, start)
    return start


def key_span(docs_ref, kb, z_count, cols, col, tok):
    z_key, col_key = kb // cols, lax.rem(kb, cols)
    first = z_key + (col_key > col).astype(jnp.int32)
    end = jnp.int32(0)
    barred = (col_key == col).astype(jnp.int32)
    for z in range(z_count):
        block = z * cols + col
        end = end + (doc_start(docs_ref, block * tok) < (kb + 1) * tok).astype(jnp.int32)
        late = (doc_start(docs_ref, block * tok + tok - 1) > kb * tok) & (block >= kb)
        barred = barred | late.astype(jnp.int32)
    return first, jnp.maximum(end - first, 0), barred


def column_setup(docs_ref, slope, groups, cols, col, tok, pos_s, start_s, rise_s):
    for z in range(groups):
        lanes = slice(z * tok, (z + 1) * tok)
        at = (z * cols + col) * tok + lax.broadcasted_iota(jnp.int32, (1, tok), 1)
        pos_s[:, lanes] = at
        start_s[:, lanes] = doc_start(docs_ref, at)
    rise_s[...] = slope * lax.broadcasted_iota(jnp.int32, (tok, 128), 0).astype(F32)


def widened(rise, width):
    return jnp.concatenate([rise] * (width // 128), axis=1)


def over_key_blocks(docs_ref, groups, cols, col, tok, run, none=None):
    blocks = groups * cols

    def step(i, carry):
        kb = blocks - 1 - i
        first, count, barred = key_span(docs_ref, kb, groups, cols, col, tok)
        for n in range(1, groups + 1):
            for masked in (True, False):

                @pl.when((count == n) & (barred == int(masked)))
                def _(n=n, masked=masked):
                    run(kb, pl.multiple_of(first * tok, 128), n * tok, masked)

        if none is not None:

            @pl.when(count == 0)
            def _():
                none(kb)

        return carry

    lax.fori_loop(0, blocks, step, 0)


def allowed(kb, at, start, tok, width):
    keys = kb * tok + lax.broadcasted_iota(jnp.int32, (tok, width), 0)
    return (keys <= at) & (keys >= start)


def natural_order(place_ref, n_groups, n_cols, q_refs, kv_refs, other_refs, store_query, store_key):
    me, col = place_ref[0], place_ref[1]
    for x in range(n_groups):
        z = me ^ x
        store_query(z, q_refs[x])
        store_key(z * n_cols + col, kv_refs[x])
        for s in range(1, n_cols):
            store_key(z * n_cols + (col ^ s), other_refs[(s - 1) * n_groups + x])


def block_rows(z, tok):
    return pl.ds(pl.multiple_of(z * tok, 128), tok)


def forward_kernel(groups, cols, tok, n_after, place_ref, docs_ref, slope_ref, *refs):
    n_other = (cols - 1) * groups
    q_refs, refs = refs[:groups], refs[groups:]
    kv_refs, refs = refs[:groups], refs[groups:]
    other_refs, refs = refs[:n_other], refs[n_other + n_after :]
    outs, (ot_ref, lse_ref), scratch = refs[:groups], refs[groups : groups + 2], refs[groups + 2 :]
    q_s, k_s, vt_s, pos_s, start_s, rise_s, top_s, total_s = scratch
    me, col = place_ref[0], place_ref[1]
    slope = slope_ref[me]

    def store_query(z, piece):
        q_s[block_rows(z, tok)] = piece[...]

    def store_key(block, piece):
        k_s[block] = piece[0]
        vt_s[block] = piece[1].T

    natural_order(place_ref, groups, cols, q_refs, kv_refs, other_refs, store_query, store_key)
    column_setup(docs_ref, slope, groups, cols, col, tok, pos_s, start_s, rise_s)
    top_s[...] = jnp.full(top_s.shape, masked_fill, F32)
    total_s[...] = jnp.zeros_like(total_s)
    ot_ref[...] = jnp.zeros_like(ot_ref)

    def run(kb, base, width, masked):
        lanes = pl.ds(base, width)
        at = pos_s[:, lanes]
        row = slope * (kb * tok - at).astype(F32)
        scores = mm(k_s[kb], q_s[lanes], NT) + widened(rise_s[...], width)
        if masked:
            scores = jnp.where(allowed(kb, at, start_s[:, lanes], tok, width), scores, masked_fill)
        top = jnp.maximum(top_s[:, lanes], jnp.max(scores, axis=0, keepdims=True) + row)
        weights = jnp.exp(scores - (top - row))
        rescale = jnp.exp(top_s[:, lanes] - top)
        top_s[:, lanes] = top
        total_s[:, lanes] = total_s[:, lanes] * rescale + jnp.sum(weights, axis=0, keepdims=True)
        ot_ref[:, lanes] = ot_ref[:, lanes] * rescale + mm(vt_s[kb], weights.astype(BF16))

    over_key_blocks(docs_ref, groups, cols, col, tok, run)
    total = total_s[...]
    ot_ref[...] = ot_ref[...] / total
    lse_ref[...] = top_s[...] + jnp.log(total)
    for x in range(groups):
        outs[x][...] = ot_ref[:, block_rows(me ^ x, tok)].T.astype(BF16)


def backward_kernel(groups, cols, tok, n_after, place_ref, docs_ref, slope_ref, *refs):
    n_other = (cols - 1) * groups
    q_refs, refs = refs[:groups], refs[groups:]
    kv_refs, refs = refs[:groups], refs[groups:]
    other_refs, refs = refs[:n_other], refs[n_other:]
    grads, (ot_ref, lse_ref) = refs[:groups], refs[groups : groups + 2]
    refs = refs[groups + 2 + n_after :]
    dq_refs, own_ref, refs = refs[:groups], refs[groups], refs[groups + 1 :]
    if cols > 1:
        other_ref, refs = refs[0], refs[1:]
    q_s, k_s, v_s, kt_s, do_s, pos_s, start_s, rise_s, delta_s, dqt_s = refs
    me, col = place_ref[0], place_ref[1]
    slope = slope_ref[me]

    def store_query(z, piece):
        q_s[block_rows(z, tok)] = piece[...]

    def store_key(block, piece):
        k_s[block] = piece[0]
        v_s[block] = piece[1]
        kt_s[block] = piece[0].T

    natural_order(place_ref, groups, cols, q_refs, kv_refs, other_refs, store_query, store_key)
    column_setup(docs_ref, slope, groups, cols, col, tok, pos_s, start_s, rise_s)
    for x in range(groups):
        rows = block_rows(me ^ x, tok)
        grad = grads[x][...]
        do_s[rows] = grad
        delta_s[:, rows] = jnp.sum(grad.astype(F32).T * ot_ref[:, rows], axis=0, keepdims=True)
    dqt_s[...] = jnp.zeros_like(dqt_s)

    def store(kb, dk, dv):
        x, s = (kb // cols) ^ me, lax.rem(kb, cols) ^ col

        @pl.when(s == 0)
        def _():
            own_ref[x, 0] = dk
            own_ref[x, 1] = dv

        if cols > 1:

            @pl.when(s != 0)
            def _():
                other_ref[s - 1, x, 0] = dk.astype(BF16)
                other_ref[s - 1, x, 1] = dv.astype(BF16)

    def run(kb, base, width, masked):
        lanes = pl.ds(base, width)
        at = pos_s[:, lanes]
        row = slope * (kb * tok - at).astype(F32)
        query, grad = q_s[lanes], do_s[lanes]
        scores = mm(k_s[kb], query, NT) + widened(rise_s[...], width)
        probs = jnp.exp(scores - (lse_ref[:, lanes] - row))
        if masked:
            probs = jnp.where(allowed(kb, at, start_s[:, lanes], tok, width), probs, 0.0)
        dv = mm(probs.astype(BF16), grad)
        grad_scores = (probs * (mm(v_s[kb], grad, NT) - delta_s[:, lanes])).astype(BF16)
        dk = mm(grad_scores, query)
        dqt_s[:, lanes] += mm(kt_s[kb], grad_scores)
        store(kb, dk, dv)

    def none(kb):
        store(kb, jnp.zeros((tok, HD), F32), jnp.zeros((tok, HD), F32))

    over_key_blocks(docs_ref, groups, cols, col, tok, run, none)
    for x in range(groups):
        dq_refs[x][...] = (dqt_s[:, block_rows(me ^ x, tok)] * score_scale).T.astype(BF16)


SMEM = pl.BlockSpec(memory_space=pltpu.SMEM)
VMEM = pl.BlockSpec(memory_space=pltpu.VMEM)
ANY = pl.BlockSpec(memory_space=pl.ANY)
VMEM_BYTES = 66900000
COST = 1000
HOLD = 20 * 10**9
UP_HOLD = 5 * HOLD
gelu_slope = (2.0 / 3.141592653589793) ** 0.5


def call(kernel, name, out_shape, specs, operands, scratch=(), after=(), room=8, flops=0, moved=0, exps=0):
    limit = VMEM_BYTES
    results = pl.pallas_call(
        kernel,
        out_shape=out_shape,
        in_specs=list(specs) + [ANY] * len(after),
        out_specs=[VMEM] * len(out_shape),
        scratch_shapes=list(scratch),
        compiler_params=pltpu.CompilerParams(vmem_limit_bytes=limit),
        cost_estimate=pl.CostEstimate(flops=flops // COST, bytes_accessed=moved // COST, transcendentals=exps // COST),
        name=name,
    )(*operands, *after)
    return list(results)


def attend_forward(place, docs, slope, q, kv, others, groups, cols, tok, after):
    blocks = groups * cols
    operands = (place, docs, slope, *q, *kv, *others)
    out_shape = [jax.ShapeDtypeStruct((tok, HD), BF16)] * groups + [
        jax.ShapeDtypeStruct((HD, groups * tok), F32),
        jax.ShapeDtypeStruct((1, groups * tok), F32),
    ]
    results = call(
        functools.partial(forward_kernel, groups, cols, tok, len(after)),
        "attend_forward",
        out_shape,
        [SMEM] * 3 + [VMEM] * (len(operands) - 3),
        operands,
        [
            pltpu.VMEM((groups * tok, HD), BF16),
            pltpu.VMEM((blocks, tok, HD), BF16),
            pltpu.VMEM((blocks, HD, tok), BF16),
            pltpu.VMEM((1, groups * tok), jnp.int32),
            pltpu.VMEM((1, groups * tok), jnp.int32),
            pltpu.VMEM((tok, 128), F32),
            pltpu.VMEM((1, groups * tok), F32),
            pltpu.VMEM((1, groups * tok), F32),
        ],
        after,
        16,
        2 * blocks * groups * tok * tok * HD,
        2 * (groups + 2 * blocks) * tok * HD,
        blocks * groups * tok * tok // 2,
    )
    return results[:groups], results[groups], results[groups + 1]


def attend_backward(place, docs, slope, q, kv, others, grads, ot, lse, groups, cols, tok, after):
    blocks = groups * cols
    operands = (place, docs, slope, *q, *kv, *others, *grads, ot, lse)
    out_shape = [jax.ShapeDtypeStruct((tok, HD), BF16)] * groups + [
        jax.ShapeDtypeStruct((groups, 2, tok, HD), F32)
    ]
    if cols > 1:
        out_shape.append(jax.ShapeDtypeStruct((cols - 1, groups, 2, tok, HD), BF16))
    results = call(
        functools.partial(backward_kernel, groups, cols, tok, len(after)),
        "attend_backward",
        out_shape,
        [SMEM] * 3 + [VMEM] * (len(operands) - 3),
        operands,
        [
            pltpu.VMEM((groups * tok, HD), BF16),
            pltpu.VMEM((blocks, tok, HD), BF16),
            pltpu.VMEM((blocks, tok, HD), BF16),
            pltpu.VMEM((blocks, HD, tok), BF16),
            pltpu.VMEM((groups * tok, HD), BF16),
            pltpu.VMEM((1, groups * tok), jnp.int32),
            pltpu.VMEM((1, groups * tok), jnp.int32),
            pltpu.VMEM((tok, 128), F32),
            pltpu.VMEM((1, groups * tok), F32),
            pltpu.VMEM((HD, groups * tok), F32),
        ],
        after,
        24,
        14 * 10**9 * COST,
    )
    return results[:groups], results[groups], (results[groups + 1] if cols > 1 else None)


def rows_of(ref, part, size):
    return ref[pl.ds(pl.multiple_of(part * size, 16), size)]


def norm_rows(values):
    mean = jnp.mean(values, axis=-1, keepdims=True)
    centered = values - mean
    spread = jnp.mean(centered * centered, axis=-1, keepdims=True)
    return centered * lax.rsqrt(spread + norm_eps)


def mix_kernel(heads, n_after, place_ref, w_ref, *refs):
    pieces, out_ref, att_ref = refs[:heads], refs[heads + n_after], refs[heads + n_after + 1]
    for x in range(heads):
        head = place_ref[0] ^ x
        att_ref[:, pl.ds(pl.multiple_of(head * HD, HD), HD)] = pieces[x][...]
    out_ref[...] = mm(att_ref[...], w_ref[...]).astype(BF16)


def mix_heads(place, w_out, pieces, after):
    tok, heads = pieces[0].shape[0], len(pieces)
    return call(
        functools.partial(mix_kernel, heads, len(after)),
        "mix_heads",
        [jax.ShapeDtypeStruct((tok, D), BF16), jax.ShapeDtypeStruct((tok, heads * HD), BF16)],
        [SMEM] + [VMEM] * (heads + 1),
        (place, w_out, *pieces),
        after=after,
        flops=2 * tok * D * heads * HD,
        moved=2 * (tok * D + D * heads * HD),
    )


def unproject_kernel(heads, n_after, place_ref, w_ref, *refs):
    dq, dkv = refs[:heads], refs[heads : 2 * heads]
    out_ref, sum_ref, wide_s = refs[2 * heads + n_after :]
    for x in range(heads):
        head = place_ref[0] ^ x
        lanes = pl.ds(pl.multiple_of(head * HD, HD), HD)
        wide_s[0, :, lanes] = dq[x][...]
        wide_s[1, :, lanes] = dkv[x][0]
        wide_s[2, :, lanes] = dkv[x][1]
    total = mm(wide_s[0], w_ref[0], NT)
    for j in (1, 2):
        total = total + mm(wide_s[j], w_ref[j], NT)
    out_ref[...] = total.astype(BF16)
    sum_ref[0:1] = jnp.sum(wide_s[0].astype(F32), axis=0, keepdims=True)
    sum_ref[1:2] = jnp.sum(wide_s[2].astype(F32), axis=0, keepdims=True)


def unproject(place, w_qkv, dq, dkv, after):
    tok, heads = dq[0].shape[0], len(dq)
    return call(
        functools.partial(unproject_kernel, heads, len(after)),
        "unproject",
        [jax.ShapeDtypeStruct((tok, D), BF16), jax.ShapeDtypeStruct((2, heads * HD), F32)],
        [SMEM] + [VMEM] * (2 * heads + 1),
        (place, w_qkv, *dq, *dkv),
        [pltpu.VMEM((3, tok, heads * HD), BF16)],
        after=after,
        flops=6 * tok * D * heads * HD,
        moved=2 * (tok * D + 3 * D * heads * HD),
    )


def project_kernel(heads, place_ref, x_ref, gain_ref, shift_ref, w_ref, bias_ref, *refs):
    normed_ref, half_ref, q_refs, kv_refs = refs[0], refs[1], refs[2 : 2 + heads], refs[2 + heads : -1]
    out_s = refs[-1]
    normed = norm_rows(x_ref[...].astype(F32)) * gain_ref[0:1] + shift_ref[0:1]
    normed = normed.astype(BF16)
    normed_ref[...] = normed
    half_ref[...] = rows_of(normed_ref, place_ref[3], half_ref.shape[0])
    for j in range(3):
        product = mm(normed, w_ref[j])
        if j == 0:
            product = (product + bias_ref[0:1]) * score_scale
        if j == 2:
            product = product + bias_ref[1:2]
        product = product.astype(BF16)
        for h in range(heads):
            out_s[h, j] = product[:, h * HD : (h + 1) * HD]
    for x in range(heads):
        head = place_ref[0] ^ x
        q_refs[x][...] = out_s[head, 0]
        kv_refs[x][...] = out_s[head, 1:3]


def project(place, inputs, gain, shift, w_qkv, qv_bias):
    tok = inputs.shape[0]
    heads = w_qkv.shape[2] // HD
    out_shape = (
        [jax.ShapeDtypeStruct((tok, D), BF16), jax.ShapeDtypeStruct((tok // 2, D), BF16)]
        + [jax.ShapeDtypeStruct((tok, HD), BF16)] * heads
        + [jax.ShapeDtypeStruct((2, tok, HD), BF16)] * heads
    )
    results = call(
        functools.partial(project_kernel, heads),
        "project",
        out_shape,
        [SMEM] + [VMEM] * 5,
        (place, inputs, gain, shift, w_qkv, qv_bias),
        [pltpu.VMEM((heads, 3, tok, HD), BF16)],
    )
    return results[0], results[1], results[2 : 2 + heads], results[2 + heads :]


def middle_kernel(n_after, place_ref, x_ref, part_ref, other_ref, bias_ref, gain_ref, shift_ref, *refs):
    mixed_ref, normed_ref, half_ref = refs[n_after:]
    parts = part_ref[...].astype(F32) + other_ref[...].astype(F32)
    mixed = x_ref[...].astype(F32) + parts + bias_ref[0:1]
    mixed_ref[...] = mixed
    normed_ref[...] = (norm_rows(mixed) * gain_ref[1:2] + shift_ref[1:2]).astype(BF16)
    half_ref[...] = rows_of(normed_ref, place_ref[3], half_ref.shape[0])


def middle(place, inputs, part, other, out_bias, gain, shift, after=()):
    tok = inputs.shape[0]
    return call(
        functools.partial(middle_kernel, len(after)),
        "middle",
        [
            jax.ShapeDtypeStruct((tok, D), F32),
            jax.ShapeDtypeStruct((tok, D), BF16),
            jax.ShapeDtypeStruct((tok // 2, D), BF16),
        ],
        [SMEM] + [VMEM] * 6,
        (place, inputs, part, other, out_bias, gain, shift),
        after=after,
    )


def hidden_kernel(place_ref, normed_ref, half_ref, w_ref, bias_ref, grad_ref, *refs):
    act_sent, grad_sent, act_mine, grad_mine, back_ref, sum_ref = refs
    near, (tok, width) = place_ref[1] % 2, act_mine.shape
    grad_sent[tok:] = half_ref[...]
    total = None
    for act_ref, out_ref, side in ((act_sent, grad_sent, 1 - near), (act_mine, grad_mine, near)):
        cut = pl.ds(pl.multiple_of(side * width, 128), width)
        u = mm(normed_ref[...], w_ref[:, cut]) + bias_ref[:, cut]
        square = u * u
        bend = jnp.tanh(u * (gelu_slope + gelu_slope * 0.044715 * square))
        half = 0.5 + 0.5 * bend
        act_ref[...] = (u * half).astype(BF16)
        lean = u * (0.5 - 0.5 * bend * bend)
        rise = half + lean * (gelu_slope + (3 * 0.044715 * gelu_slope) * square)
        grad = (rise * grad_ref[:, cut]).astype(BF16)
        out_ref[:tok] = grad
        sum_ref[:, cut] = column_sum(grad.astype(F32))
        back = mm(grad, w_ref[:, cut], NT)
        total = back if total is None else total + back
    back_ref[...] = total.astype(BF16)


def hidden_units(place, normed, half, w_up, up_bias, grad_active, after=()):
    tok, total = normed.shape[0], w_up.shape[1]
    assert total // 2 == D
    act_sent, grad_sent, act_mine, grad_mine, back, sums = call(
        hidden_kernel,
        "hidden_units",
        [
            jax.ShapeDtypeStruct((tok, total // 2), BF16),
            jax.ShapeDtypeStruct((tok + tok // 2, total // 2), BF16),
            jax.ShapeDtypeStruct((tok, total // 2), BF16),
            jax.ShapeDtypeStruct((tok, total // 2), BF16),
            jax.ShapeDtypeStruct((tok, D), BF16),
            jax.ShapeDtypeStruct((1, total), F32),
        ],
        [SMEM] + [VMEM] * 5,
        (place, normed, half, w_up, up_bias, grad_active),
        room=16,
    )
    return act_mine, act_sent, grad_mine, grad_sent, back, sums


def column_sum(values):
    return jnp.sum(values, axis=0, keepdims=True)


def norm_back(values, grad, gain):
    mean = jnp.mean(values, axis=-1, keepdims=True)
    centered = values - mean
    scale = lax.rsqrt(jnp.mean(centered * centered, axis=-1, keepdims=True) + norm_eps)
    normed = centered * scale
    inner = grad * gain
    along = jnp.mean(inner * normed, axis=-1, keepdims=True)
    back = scale * (inner - jnp.mean(inner, axis=-1, keepdims=True) - normed * along)
    return back, column_sum(grad * normed), column_sum(grad)


def turn_kernel(heads, n_after, place_ref, mixed_ref, part_ref, other_ref, low_ref, gain_ref, w_ref, *refs):
    mid_ref, low_out_ref, sum_ref = refs[n_after : n_after + 3]
    pieces, head_s = refs[n_after + 3 : -1], refs[-1]
    grad = part_ref[...].astype(F32) + other_ref[...].astype(F32)
    back, gain_sum, shift_sum = norm_back(mixed_ref[...], grad, gain_ref[1:2])
    low_in = low_ref[...].astype(F32)
    mid = low_in + back
    mid_ref[...] = mid
    low = mid.astype(BF16)
    low_out_ref[...] = low
    sum_ref[0:1] = gain_sum
    sum_ref[1:2] = shift_sum
    sum_ref[2:3] = jnp.sum(low.astype(F32), axis=0, keepdims=True)
    sum_ref[3:4] = jnp.sum(low_in, axis=0, keepdims=True)
    product = mm(low, w_ref[...], NT).astype(BF16)
    for h in range(heads):
        head_s[h] = product[:, h * HD : (h + 1) * HD]
    for x in range(heads):
        pieces[x][...] = head_s[place_ref[0] ^ x]


def turn_back(place, mixed, part, other, cotangent, gain, w_out, after=()):
    tok, heads = mixed.shape[0], w_out.shape[0] // HD
    results = call(
        functools.partial(turn_kernel, heads, len(after)),
        "turn_back",
        [
            jax.ShapeDtypeStruct((tok, D), F32),
            jax.ShapeDtypeStruct((tok, D), BF16),
            jax.ShapeDtypeStruct((4, D), F32),
        ]
        + [jax.ShapeDtypeStruct((tok, HD), BF16)] * heads,
        [SMEM] + [VMEM] * 6,
        (place, mixed, part, other, cotangent, gain, w_out),
        [pltpu.VMEM((heads, tok, HD), BF16)],
        after=after,
    )
    return results[0], results[1], results[2], results[3:]


def last_kernel(n_after, x_ref, part_ref, other_ref, mid_ref, gain_ref, sums_ref, units_ref, heads_ref, *refs):
    out_ref, small_ref = refs[n_after:]
    grad = part_ref[...].astype(F32) + other_ref[...].astype(F32)
    back, gain_sum, shift_sum = norm_back(x_ref[...].astype(F32), grad, gain_ref[0:1])
    out_ref[...] = mid_ref[...] + back
    small_ref[0:4] = sums_ref[...]
    small_ref[4:5] = gain_sum
    small_ref[5:6] = shift_sum
    small_ref[6:7, : heads_ref.shape[1]] = heads_ref[0:1]
    small_ref[6:7, heads_ref.shape[1] :] = heads_ref[1:2]
    for k in range(units_ref.shape[1] // D):
        small_ref[7 + k : 8 + k] = units_ref[:, k * D : (k + 1) * D]


def last_rows(inputs, part, other, grad_mid, gain, sums, unit_sums, head_sums, after=()):
    tok = inputs.shape[0]
    return call(
        functools.partial(last_kernel, len(after)),
        "last_rows",
        [
            jax.ShapeDtypeStruct((tok, D), F32),
            jax.ShapeDtypeStruct((7 + unit_sums.shape[1] // D, D), F32),
        ],
        [VMEM] * 8,
        (inputs, part, other, grad_mid, gain, sums, unit_sums, head_sums),
        after=after,
    )


def feed_kernel(n_after, place_ref, mine_ref, sent_ref, w_ref, *refs):
    near, half = place_ref[1] % 2, mine_ref.shape[1]
    total = mm(mine_ref[...], rows_of(w_ref, near, half))
    total = total + mm(sent_ref[...], rows_of(w_ref, 1 - near, half))
    refs[n_after][...] = total.astype(BF16)


def feed(place, mine, sent, w_down, after):
    return call(
        functools.partial(feed_kernel, len(after)),
        "feed",
        [jax.ShapeDtypeStruct((mine.shape[0], D), BF16)],
        [SMEM] + [VMEM] * 3,
        (place, mine, sent, w_down),
        after=after,
    )[0]


def early_kernel(low_ref, w_ref, out_ref):
    out_ref[...] = mm(low_ref[...], w_ref[...], NT)


def early_grad(cotangent, w_down):
    return call(
        early_kernel,
        "early_grad",
        [jax.ShapeDtypeStruct((cotangent.shape[0], w_down.shape[0]), F32)],
        [VMEM] * 2,
        (cotangent, w_down),
    )[0]


def pair_grad_kernel(extra, halves, n_after, place_ref, rows_ref, units_ref, near_ref, *refs):
    near_rows, refs = refs[: 1 + halves], refs[1 + halves :]
    more, refs = refs[: 2 * extra], refs[2 * extra + n_after :]
    sent_ref, kept_ref, rows_s = refs
    dp, mp = place_ref[2], place_ref[3]
    tok, width = units_ref.shape
    if halves:
        half = near_rows[0].shape[0]
        for k in range(2):
            rows_s[pl.ds(pl.multiple_of((mp ^ k) * half, 16), half)] = near_rows[k][...]
    else:
        rows_s = near_rows[0]
    step = sent_ref.shape[0]
    for k, out_ref in ((1, sent_ref), (0, kept_ref)):
        cut = pl.ds(pl.multiple_of((dp ^ k) * step, 128), step)
        total = mm(rows_ref[:, cut], units_ref[...], TN) + mm(rows_s[:, cut], near_ref[:tok], TN)
        out_ref[:, :width] = total.astype(out_ref.dtype)
        if extra:
            out_ref[:, width:] = mm(more[0][:, cut], more[1][...], TN).astype(out_ref.dtype)


def pair_grad(place, rows, near_rows, units, near_units, more, after):
    tok, width = units.shape
    total = width + (more[1].shape[1] if more else 0)
    return call(
        functools.partial(pair_grad_kernel, int(bool(more)), len(near_rows) - 1, len(after)),
        "pair_grad",
        [jax.ShapeDtypeStruct((D // 2, total), BF16), jax.ShapeDtypeStruct((D // 2, total), F32)],
        [SMEM] + [VMEM] * (3 + len(near_rows) + len(more)),
        (place, rows, units, near_units, *near_rows, *more),
        [pltpu.VMEM((tok, D), BF16)],
        after=after,
    )


def head_grad_kernel(groups, n_after, place_ref, *refs):
    own_ref, mine, other = refs[0], refs[1:groups], refs[groups : 2 * groups - 1]
    dq, dkv = refs[2 * groups - 1 : 3 * groups - 1], refs[3 * groups - 1 : 4 * groups - 1]
    sent_ref, kept_ref, rows_s, grads_s = refs[4 * groups - 1 + n_after :]
    dp, mp = place_ref[2], place_ref[3]
    tok = own_ref.shape[0]
    half = tok // 2
    for x in range(groups):
        if x == 0:
            rows_s[0:tok] = own_ref[...]
        else:
            rows_s[pl.ds(pl.multiple_of(x * tok + mp * half, 16), half)] = mine[x - 1][...]
            rows_s[pl.ds(pl.multiple_of(x * tok + (1 - mp) * half, 16), half)] = other[x - 1][...]
        rows = slice(x * tok, (x + 1) * tok)
        grads_s[rows, :HD] = dq[x][...]
        grads_s[rows, HD : 2 * HD] = dkv[x][0]
        grads_s[rows, 2 * HD :] = dkv[x][1]
    step = sent_ref.shape[0]
    for k, out_ref in ((1, sent_ref), (0, kept_ref)):
        cut = pl.ds(pl.multiple_of((dp ^ k) * step, 128), step)
        out_ref[...] = mm(rows_s[:, cut], grads_s[...], TN).astype(out_ref.dtype)


def head_grad(place, own, mine, other, dq, dkv, after):
    tok, groups = own.shape[0], len(dq)
    return call(
        functools.partial(head_grad_kernel, groups, len(after)),
        "head_grad",
        [jax.ShapeDtypeStruct((D // 2, 3 * HD), BF16), jax.ShapeDtypeStruct((D // 2, 3 * HD), F32)],
        [SMEM] + [VMEM] * (4 * groups - 1),
        (place, own, *mine, *other, *dq, *dkv),
        [pltpu.VMEM((groups * tok, D), BF16), pltpu.VMEM((groups * tok, 3 * HD), BF16)],
        after=after,
        flops=2 * groups * tok * D * 3 * HD,
        moved=2 * groups * tok * (D + 3 * HD),
    )


def sum_kernel(groups, n_there, n_after, own_ref, *refs):
    there, outs = refs[:n_there], refs[n_there + n_after :]
    for x in range(groups):
        for j in range(2):
            total = own_ref[x, j]
            for ref in there:
                total = total + ref[0, x, j].astype(F32)
            outs[x][j] = total.astype(BF16)


def sum_columns(own, there, after):
    groups, _, tok, _ = own.shape
    return call(
        functools.partial(sum_kernel, groups, len(there), len(after)),
        "sum_columns",
        [jax.ShapeDtypeStruct((2, tok, HD), BF16)] * groups,
        [VMEM] * (1 + len(there)),
        (own, *there),
        after=after,
        moved=10 * own.size,
    )


def fold_kernel(outer, inner, n_after, now_ref, kept_ref, there_ref, *refs):
    mine_ref, sent_ref = refs[n_after:]
    for o in range(outer):
        for k, ref in ((0, mine_ref), (1, sent_ref)):
            at = pl.ds(pl.multiple_of((2 * o + (now_ref[0] ^ k)) * inner, 16), inner)
            total = kept_ref[at] + there_ref[at].astype(F32)
            ref[o * inner : (o + 1) * inner] = total.astype(ref.dtype)


def fold(now, kept, there, inner, after=()):
    rows, width = kept.shape
    return call(
        functools.partial(fold_kernel, rows // (2 * inner), inner, len(after)),
        "fold",
        [jax.ShapeDtypeStruct((rows // 2, width), F32), jax.ShapeDtypeStruct((rows // 2, width), BF16)],
        [SMEM, VMEM, VMEM],
        (now, kept, there),
        after=after,
        moved=9 * kept.size,
    )


def both_halves(near, mine, there, out_ref, half):
    out_ref[:, pl.ds(pl.multiple_of(near * half, 128), half)] = mine
    out_ref[:, pl.ds(pl.multiple_of((1 - near) * half, 128), half)] = there


def finish_kernel(width, n_after, place_ref, mine_ref, there_ref, h_ref, h_there_ref, d_ref, d_there_ref, *refs):
    u_ref, u_there_ref, refs = refs[0], refs[1], refs[2 + n_after :]
    gain_ref, shift_ref, heads_ref, units_ref, bias_ref, qkv_ref, down_ref, up_ref, out_ref = refs
    total = mine_ref[...] + there_ref[...]
    gain_ref[0:1], gain_ref[1:2] = total[4:5], total[0:1]
    shift_ref[0:1], shift_ref[1:2] = total[5:6], total[1:2]
    heads_ref[0:1], heads_ref[1:2] = total[6:7, :width], total[6:7, width:]
    for k in range(units_ref.shape[1] // D):
        units_ref[:, k * D : (k + 1) * D] = total[7 + k : 8 + k]
    bias_ref[...] = total[2:4]
    rows = h_ref[...] + h_there_ref[...].astype(F32)
    for h in range(width // HD):
        for j in range(3):
            at = (3 * h + j) * HD
            qkv_ref[j, :, h * HD : (h + 1) * HD] = rows[:, at : at + HD]
    near, half = place_ref[1] % 2, d_ref.shape[1]
    both_halves(near, d_ref[...], d_there_ref[...].astype(F32), down_ref, half)
    there = u_there_ref[...].astype(F32)
    both_halves(near, u_ref[:, :half], there[:, :half], up_ref, half)
    out_ref[...] = u_ref[:, half:] + there[:, half:]


def five_and_rest(arrays):
    return [arrays[:5], *arrays[5:]]


def finish(place, small, small_there, heads, heads_there, down, down_there, up, up_there, width, after):
    rows = heads.shape[0]
    shapes = [(2, D), (2, D), (2, width), (1, (small.shape[0] - 7) * D), (2, D)]
    shapes += [(3, rows, width), (rows, 2 * down.shape[1]), (rows, 2 * down.shape[1]), (rows, width)]
    return call(
        functools.partial(finish_kernel, width, len(after)),
        "finish",
        [jax.ShapeDtypeStruct(shape, F32) for shape in shapes],
        [SMEM] + [VMEM] * 8,
        (place, small, small_there, heads, heads_there, down, down_there, up, up_there),
        after=after,
    )


def pass_on(*refs):
    pass


def gate(x, *after, weight=0):
    return pl.pallas_call(
        pass_on,
        out_shape=jax.ShapeDtypeStruct(x.shape, x.dtype),
        in_specs=[ANY] * (1 + len(after)),
        out_specs=ANY,
        input_output_aliases={0: 0},
        cost_estimate=pl.CostEstimate(flops=weight, bytes_accessed=0, transcendentals=0),
        name="gate",
    )(x, *after)


def swap(x, axis, size, bit):
    return lax.ppermute(x, axis, [(i, i ^ bit) for i in range(size)])


def bits(size):
    return [1 << i for i in range(size.bit_length() - 1)]


def sum_over(vector, axes):
    for axis, size in axes:
        for bit in bits(size):
            vector = vector + swap(vector, axis, size, bit)
    return vector


def body(
    sizes,
    inputs,
    doc_lengths,
    slopes,
    norm_gain,
    norm_bias,
    w_qkv,
    qv_bias,
    w_out,
    w_up,
    up_bias,
    w_down,
    out_bias,
    cotangent,
):
    n_dp, groups, cols = sizes
    tok = inputs.shape[0]
    width = slopes.shape[0] * HD
    me, col = lax.axis_index("sg"), lax.axis_index("sr")
    mp, dp, near = lax.axis_index("mp"), lax.axis_index("dp"), lax.axis_index("sr") % 2
    place = jnp.stack([me, col, dp, mp]).astype(jnp.int32)

    def deal(pieces):
        return [pieces[x] if x == 0 else swap(pieces[x], "sg", groups, x) for x in range(groups)]

    def half_rows(x):
        return lax.dynamic_slice_in_dim(x, mp * (tok // 2), tok // 2, 0)

    normed_one, one_half, q, kv = project(place, inputs, norm_gain, norm_bias, w_qkv, qv_bias)
    grad_active = early_grad(cotangent, w_down)
    kv = deal(kv)
    others = [[swap(kv[0], "sr", cols, s)] for s in range(1, cols)]
    turn = (grad_active,)
    for x in range(1, groups):
        kv[x] = gate(kv[x], *turn, *[column[-1] for column in others])
        turn = ()
        for s in range(1, cols):
            others[s - 1].append(swap(kv[x], "sr", cols, s))
    others = [piece for column in others for piece in column]
    q = deal([q[0]] + [gate(piece, kv[groups - 2]) for piece in q[1:]])
    others[-1] = gate(others[-1], weight=5 * HOLD)
    outs, ot, lse = attend_forward(place, doc_lengths, slopes, q, kv, others, groups, cols, tok, [])
    low_near = swap(gate(cotangent, q[1]), "sr", cols, 1)
    low_near = gate(low_near, outs[0], weight=HOLD)
    outs = deal(outs)
    one_half = gate(one_half, outs[groups - 1])
    far = swap(one_half, "sg", groups, 2)
    attn_part, attended = mix_heads(place, w_out, outs, [low_near])
    mixed, normed_two, two_half = middle(
        place,
        inputs,
        attn_part,
        swap(attn_part, "mp", 2, 1),
        out_bias,
        norm_gain,
        norm_bias,
        [],
    )

    half_units = w_up.shape[1] // 2
    active, active_sent, grad_hidden, hidden_sent, back_two, unit_sums = hidden_units(
        place, normed_two, two_half, w_up, up_bias[None], grad_active
    )
    active_near = swap(active_sent, "sr", cols, 1)
    hidden_near = swap(hidden_sent, "sr", cols, 1)
    far = gate(far, back_two, weight=HOLD)
    grad_mid, grad_mid_low, row_sums, pieces = turn_back(
        place,
        mixed,
        back_two,
        swap(back_two, "mp", 2, 1),
        cotangent,
        norm_gain,
        w_out,
        [far],
    )
    grads = deal(pieces)

    down_sent, down_kept = pair_grad(
        place,
        cotangent,
        [low_near],
        active,
        active_near,
        (),
        [pieces[3]],
    )
    down_there = swap(down_sent, "dp", 2, 1)
    far = gate(far, down_sent, *grads[1:])
    last = swap(far, "sg", groups, 1)
    one_half = gate(one_half, far)
    beside = swap(one_half, "sg", groups, 1)
    dq, dkv, dkv_other = attend_backward(
        place,
        doc_lengths,
        slopes,
        q,
        kv,
        others,
        grads,
        ot,
        lse,
        groups,
        cols,
        tok,
        [down_sent, one_half],
    )
    dkv_there = [swap(dkv_other[s - 1 : s], "sr", cols, s) for s in range(1, cols)]
    beside = gate(beside, dq[0], weight=HOLD)
    last = gate(last, dq[0], weight=HOLD)
    hidden_near = gate(hidden_near, dq[0], weight=HOLD)
    dq_mine = [dq[0], gate(dq[1], beside), gate(dq[2], last), gate(dq[3], hidden_near)]
    dq = deal(dq_mine)
    two_near = hidden_near[tok:]
    two_near_mp = swap(two_near, "mp", 2, 1)

    rows_here = D // (2 * groups * cols)
    stages = [("sr", cols, 2 * bit) for bit in bits(cols // 2)]
    stages += [("sg", groups, bit) for bit in bits(groups)]

    def now(axis, bit):
        return ((lax.axis_index(axis) // bit) % 2).astype(jnp.int32).reshape(1)

    def stage(k, kept, there, *after):
        axis, size, bit = stages[k]
        kept, sent = fold(now(axis, bit), kept, there, 2 * rows_here, after)
        return kept, sent, swap(sent, axis, size, bit)

    last_turn = len(stages) - 1
    up_sent, up_kept = pair_grad(
        place,
        normed_two,
        [two_near, two_near_mp],
        grad_hidden,
        hidden_near,
        (grad_mid_low, attended),
        [dq_mine[3]],
    )
    down_there = gate(down_there, up_sent)
    for k in range(last_turn):
        down_kept, down_sent, down_there = stage(k, down_kept, down_there)
    up_there = swap(up_sent, "dp", 2, 1)
    dq = [dq[0]] + [gate(piece, down_sent, weight=HOLD) for piece in dq[1:]]
    dkv_there = [gate(piece, *dq[1:], weight=HOLD) for piece in dkv_there]
    rows_mine = [gate(piece, *dq[1:]) for piece in (beside, far, last)]
    rows_mp = [swap(piece, "mp", 2, 1) for piece in rows_mine]
    dkv_mine = sum_columns(dkv, dkv_there, rows_mine)
    dkv_mine = [dkv_mine[0]] + [gate(dkv_mine[x], rows_mp[x - 1]) for x in range(1, groups)]
    dkv = deal(dkv_mine)

    head_sent, head_kept = head_grad(
        place, normed_one, rows_mine, rows_mp, dq_mine, dkv_mine, []
    )
    ffn_part = feed(place, active, active_sent, w_down, [head_sent])
    down_there = gate(down_there, head_sent)
    down_kept, down_sent, down_there = stage(last_turn, down_kept, down_there)
    up_there = gate(up_there, down_sent, ffn_part)
    for k in range(last_turn):
        up_kept, up_sent, up_there = stage(k, up_kept, up_there)
    dkv = [dkv[0]] + [gate(piece, up_sent, weight=HOLD) for piece in dkv[1:]]
    head_there = swap(gate(head_sent, up_sent), "dp", 2, 1)
    back_part, head_sums = unproject(place, w_qkv, dq, dkv, [])
    back_there = swap(back_part, "mp", 2, 1)
    head_there = gate(head_there, back_part)
    down_there = gate(down_there, back_part)

    kept = (head_kept + head_there.astype(F32)).reshape(groups, cols // 2, 2 * rows_here, 3 * HD)
    for bit in bits(cols // 2):
        here = now("sr", 2 * bit)[0]
        view = kept.reshape(groups, -1, 2, 2 * rows_here, 3 * HD)
        sent = lax.dynamic_index_in_dim(view, 1 - here, 2, keepdims=False).astype(BF16)
        kept = lax.dynamic_index_in_dim(view, here, 2, keepdims=False)
        kept = kept + swap(sent, "sr", cols, 2 * bit).astype(F32)
    kept = kept.reshape(groups, 2, rows_here, 3 * HD)
    low = kept.astype(BF16)
    pieces = [lax.dynamic_index_in_dim(low, me ^ x, 0, keepdims=False) for x in range(groups)]
    pieces_sent = pieces
    pieces = deal(pieces)
    up_there = gate(up_there, pieces_sent[1], weight=HOLD)
    up_kept, up_sent, up_there = stage(last_turn, up_kept, up_there)
    grad_inputs, small = last_rows(
        inputs,
        back_part,
        gate(back_there, up_sent),
        grad_mid,
        norm_gain,
        row_sums,
        unit_sums,
        head_sums,
        [],
    )

    def with_near(x):
        sent = lax.dynamic_index_in_dim(x, 1 - near, 0, keepdims=False).astype(BF16)
        mine = lax.dynamic_index_in_dim(x, near, 0, keepdims=False)
        return sent, mine, swap(sent, "sr", cols, 1)

    def add_with_near(kept, there):
        if rows_here % 16:
            return with_near((kept + there.astype(F32)).reshape(2, rows_here, -1))
        mine, sent = fold(now("sr", 1), kept, there, rows_here)
        return sent, mine, swap(sent, "sr", cols, 1)

    _, down_mine, down_there = add_with_near(down_kept, gate(down_there, small))
    ffn_part = gate(ffn_part, small)
    small = sum_over(small, (("sr", cols), ("dp", n_dp)))
    ffn_other = gate(swap(ffn_part, "mp", 2, 1), small).astype(F32)
    outputs = (mixed + ffn_part.astype(F32) + ffn_other + out_bias[1]).astype(BF16)

    far_bits = bits(groups)
    small_there = swap(small, "sg", groups, far_bits[0])

    pieces = [pieces[0]] + [gate(piece, up_sent) for piece in pieces[1:]]
    pieces[0] = lax.dynamic_index_in_dim(kept, me, 0, keepdims=False)
    heads_all = jnp.concatenate(
        [
            sum(jnp.where((me ^ x) == h, pieces[x].astype(F32), 0.0) for x in range(groups))
            for h in range(groups)
        ],
        2,
    )
    head_sent, head_mine, head_near = with_near(heads_all)
    up_sent, up_mine, up_there = add_with_near(up_kept, gate(up_there, head_sent))
    for bit in far_bits[1:]:
        small = small + gate(small_there, up_sent)
        small_there = swap(small, "sg", groups, bit)
    sums, grad_qkv, grad_down, grad_up, grad_out = five_and_rest(
        finish(
            place,
            small,
            small_there,
            head_mine,
            head_near,
            down_mine,
            down_there,
            up_mine,
            up_there,
            width,
            [outputs],
        )
    )
    grad_gain, grad_shift, grad_qv_bias, grad_up_bias, grad_bias = sums

    return (
        outputs,
        grad_inputs,
        grad_gain,
        grad_shift,
        grad_qkv,
        grad_qv_bias,
        grad_out.T,
        grad_up,
        grad_up_bias.reshape(-1),
        grad_down.T,
        grad_bias,
    )


def solution(mesh):
    n_dp, n_seq, n_mp = mesh.shape["dp"], mesh.shape["seq"], mesh.shape["mp"]
    groups = 4
    cols = n_seq // groups
    inner = Mesh(mesh.devices.reshape(n_dp, groups, cols, n_mp), ("dp", "sg", "sr", "mp"))
    rows = ("dp", "sg", "sr")
    return jax.shard_map(
        functools.partial(body, (n_dp, groups, cols)),
        mesh=inner,
        in_specs=(
            P(rows, None),
            P("dp", None),
            P("mp"),
            P(),
            P(),
            P(None, None, "mp"),
            P(None, "mp"),
            P("mp", None),
            P(None, "mp"),
            P("mp"),
            P("mp", None),
            P(),
            P(rows, None),
        ),
        out_specs=(
            P(rows, None),
            P(rows, None),
            P(),
            P(),
            P(None, rows, "mp"),
            P(None, "mp"),
            P("mp", rows),
            P(rows, "mp"),
            P("mp"),
            P("mp", rows),
            P(),
        ),
        check_vma=False,
    )
```

```python
import functools

import jax
import jax.numpy as jnp
from jax import lax
from jax.experimental import pallas as pl
from jax.experimental.pallas import tpu as pltpu
from jax.sharding import Mesh
from jax.sharding import PartitionSpec as P

D = 1024
HD = 128
BF16 = jnp.bfloat16
F32 = jnp.float32

norm_eps = 1e-05
masked_fill = -1e30
score_scale = HD ** (-0.5)

NT = (((1,), (1,)), ((), ()))
NN = (((1,), (0,)), ((), ()))
TN = (((0,), (0,)), ((), ()))


def mm(a, b, dims=NN):
    return lax.dot_general(a, b, dims, preferred_element_type=F32)


def doc_start(docs_ref, position):
    start = jnp.zeros_like(position)
    bound = jnp.int32(0)
    for d in range(docs_ref.shape[1]):
        bound = bound + docs_ref[0, d]
        start = jnp.where(position >= bound, bound, start)
    return start


def key_span(docs_ref, kb, z_count, cols, col, tok):
    z_key, col_key = kb // cols, lax.rem(kb, cols)
    first = z_key + (col_key > col).astype(jnp.int32)
    end = jnp.int32(0)
    barred = (col_key == col).astype(jnp.int32)
    for z in range(z_count):
        block = z * cols + col
        end = end + (doc_start(docs_ref, block * tok) < (kb + 1) * tok).astype(jnp.int32)
        late = (doc_start(docs_ref, block * tok + tok - 1) > kb * tok) & (block >= kb)
        barred = barred | late.astype(jnp.int32)
    return first, jnp.maximum(end - first, 0), barred


def column_setup(docs_ref, slope, groups, cols, col, tok, pos_s, start_s, rise_s):
    for z in range(groups):
        lanes = slice(z * tok, (z + 1) * tok)
        at = (z * cols + col) * tok + lax.broadcasted_iota(jnp.int32, (1, tok), 1)
        pos_s[:, lanes] = at
        start_s[:, lanes] = doc_start(docs_ref, at)
    rise_s[...] = slope * lax.broadcasted_iota(jnp.int32, (tok, 128), 0).astype(F32)


def widened(rise, width):
    return jnp.concatenate([rise] * (width // 128), axis=1)


def over_key_blocks(docs_ref, groups, cols, col, tok, run, none=None):
    blocks = groups * cols

    def step(i, carry):
        kb = blocks - 1 - i
        first, count, barred = key_span(docs_ref, kb, groups, cols, col, tok)
        for n in range(1, groups + 1):
            for masked in (True, False):

                @pl.when((count == n) & (barred == int(masked)))
                def _(n=n, masked=masked):
                    run(kb, pl.multiple_of(first * tok, 128), n * tok, masked)

        if none is not None:

            @pl.when(count == 0)
            def _():
                none(kb)

        return carry

    lax.fori_loop(0, blocks, step, 0)


def allowed(kb, at, start, tok, width):
    keys = kb * tok + lax.broadcasted_iota(jnp.int32, (tok, width), 0)
    return (keys <= at) & (keys >= start)


def natural_order(place_ref, n_groups, n_cols, q_refs, kv_refs, other_refs, store_query, store_key):
    me, col = place_ref[0], place_ref[1]
    for x in range(n_groups):
        z = me ^ x
        store_query(z, q_refs[x])
        store_key(z * n_cols + col, kv_refs[x])
        for s in range(1, n_cols):
            store_key(z * n_cols + (col ^ s), other_refs[(s - 1) * n_groups + x])


def block_rows(z, tok):
    return pl.ds(pl.multiple_of(z * tok, 128), tok)


def forward_kernel(groups, cols, tok, n_after, place_ref, docs_ref, slope_ref, *refs):
    n_other = (cols - 1) * groups
    q_refs, refs = refs[:groups], refs[groups:]
    kv_refs, refs = refs[:groups], refs[groups:]
    other_refs, refs = refs[:n_other], refs[n_other + n_after :]
    outs, (ot_ref, lse_ref), scratch = refs[:groups], refs[groups : groups + 2], refs[groups + 2 :]
    q_s, k_s, vt_s, pos_s, start_s, rise_s, top_s, total_s = scratch
    me, col = place_ref[0], place_ref[1]
    slope = slope_ref[me]

    def store_query(z, piece):
        q_s[block_rows(z, tok)] = piece[...]

    def store_key(block, piece):
        k_s[block] = piece[0]
        vt_s[block] = piece[1].T

    natural_order(place_ref, groups, cols, q_refs, kv_refs, other_refs, store_query, store_key)
    column_setup(docs_ref, slope, groups, cols, col, tok, pos_s, start_s, rise_s)
    top_s[...] = jnp.full(top_s.shape, masked_fill, F32)
    total_s[...] = jnp.zeros_like(total_s)
    ot_ref[...] = jnp.zeros_like(ot_ref)

    def run(kb, base, width, masked):
        lanes = pl.ds(base, width)
        at = pos_s[:, lanes]
        row = slope * (kb * tok - at).astype(F32)
        scores = mm(k_s[kb], q_s[lanes], NT) + widened(rise_s[...], width)
        if masked:
            scores = jnp.where(allowed(kb, at, start_s[:, lanes], tok, width), scores, masked_fill)
        top = jnp.maximum(top_s[:, lanes], jnp.max(scores, axis=0, keepdims=True) + row)
        weights = jnp.exp(scores - (top - row))
        rescale = jnp.exp(top_s[:, lanes] - top)
        top_s[:, lanes] = top
        total_s[:, lanes] = total_s[:, lanes] * rescale + jnp.sum(weights, axis=0, keepdims=True)
        ot_ref[:, lanes] = ot_ref[:, lanes] * rescale + mm(vt_s[kb], weights.astype(BF16))

    over_key_blocks(docs_ref, groups, cols, col, tok, run)
    total = total_s[...]
    ot_ref[...] = ot_ref[...] / total
    lse_ref[...] = top_s[...] + jnp.log(total)
    for x in range(groups):
        outs[x][...] = ot_ref[:, block_rows(me ^ x, tok)].T.astype(BF16)


def backward_kernel(groups, cols, tok, n_after, place_ref, docs_ref, slope_ref, *refs):
    n_other = (cols - 1) * groups
    q_refs, refs = refs[:groups], refs[groups:]
    kv_refs, refs = refs[:groups], refs[groups:]
    other_refs, refs = refs[:n_other], refs[n_other:]
    grads, (ot_ref, lse_ref) = refs[:groups], refs[groups : groups + 2]
    refs = refs[groups + 2 + n_after :]
    dq_refs, own_ref, refs = refs[:groups], refs[groups], refs[groups + 1 :]
    if cols > 1:
        other_ref, refs = refs[0], refs[1:]
    q_s, k_s, v_s, kt_s, do_s, pos_s, start_s, rise_s, delta_s, dqt_s = refs
    me, col = place_ref[0], place_ref[1]
    slope = slope_ref[me]

    def store_query(z, piece):
        q_s[block_rows(z, tok)] = piece[...]

    def store_key(block, piece):
        k_s[block] = piece[0]
        v_s[block] = piece[1]
        kt_s[block] = piece[0].T

    natural_order(place_ref, groups, cols, q_refs, kv_refs, other_refs, store_query, store_key)
    column_setup(docs_ref, slope, groups, cols, col, tok, pos_s, start_s, rise_s)
    for x in range(groups):
        rows = block_rows(me ^ x, tok)
        grad = grads[x][...]
        do_s[rows] = grad
        delta_s[:, rows] = jnp.sum(grad.astype(F32).T * ot_ref[:, rows], axis=0, keepdims=True)
    dqt_s[...] = jnp.zeros_like(dqt_s)

    def store(kb, dk, dv):
        x, s = (kb // cols) ^ me, lax.rem(kb, cols) ^ col

        @pl.when(s == 0)
        def _():
            own_ref[x, 0] = dk
            own_ref[x, 1] = dv

        if cols > 1:

            @pl.when(s != 0)
            def _():
                other_ref[s - 1, x, 0] = dk.astype(BF16)
                other_ref[s - 1, x, 1] = dv.astype(BF16)

    def run(kb, base, width, masked):
        lanes = pl.ds(base, width)
        at = pos_s[:, lanes]
        row = slope * (kb * tok - at).astype(F32)
        query, grad = q_s[lanes], do_s[lanes]
        scores = mm(k_s[kb], query, NT) + widened(rise_s[...], width)
        probs = jnp.exp(scores - (lse_ref[:, lanes] - row))
        if masked:
            probs = jnp.where(allowed(kb, at, start_s[:, lanes], tok, width), probs, 0.0)
        dv = mm(probs.astype(BF16), grad)
        grad_scores = (probs * (mm(v_s[kb], grad, NT) - delta_s[:, lanes])).astype(BF16)
        dk = mm(grad_scores, query)
        dqt_s[:, lanes] += mm(kt_s[kb], grad_scores)
        store(kb, dk, dv)

    def none(kb):
        store(kb, jnp.zeros((tok, HD), F32), jnp.zeros((tok, HD), F32))

    over_key_blocks(docs_ref, groups, cols, col, tok, run, none)
    for x in range(groups):
        dq_refs[x][...] = (dqt_s[:, block_rows(me ^ x, tok)] * score_scale).T.astype(BF16)


SMEM = pl.BlockSpec(memory_space=pltpu.SMEM)
VMEM = pl.BlockSpec(memory_space=pltpu.VMEM)
ANY = pl.BlockSpec(memory_space=pl.ANY)
VMEM_BYTES = 66900000
COST = 1000
HOLD = 40 * 10**9
UP_HOLD = 5 * HOLD
gelu_slope = (2.0 / 3.141592653589793) ** 0.5


def call(kernel, name, out_shape, specs, operands, scratch=(), after=(), room=8, flops=0, moved=0, exps=0):
    limit = VMEM_BYTES
    results = pl.pallas_call(
        kernel,
        out_shape=out_shape,
        in_specs=list(specs) + [ANY] * len(after),
        out_specs=[VMEM] * len(out_shape),
        scratch_shapes=list(scratch),
        compiler_params=pltpu.CompilerParams(vmem_limit_bytes=limit),
        cost_estimate=pl.CostEstimate(flops=flops // COST, bytes_accessed=moved // COST, transcendentals=exps // COST),
        name=name,
    )(*operands, *after)
    return list(results)


def attend_forward(place, docs, slope, q, kv, others, groups, cols, tok, after):
    blocks = groups * cols
    operands = (place, docs, slope, *q, *kv, *others)
    out_shape = [jax.ShapeDtypeStruct((tok, HD), BF16)] * groups + [
        jax.ShapeDtypeStruct((HD, groups * tok), F32),
        jax.ShapeDtypeStruct((1, groups * tok), F32),
    ]
    results = call(
        functools.partial(forward_kernel, groups, cols, tok, len(after)),
        "attend_forward",
        out_shape,
        [SMEM] * 3 + [VMEM] * (len(operands) - 3),
        operands,
        [
            pltpu.VMEM((groups * tok, HD), BF16),
            pltpu.VMEM((blocks, tok, HD), BF16),
            pltpu.VMEM((blocks, HD, tok), BF16),
            pltpu.VMEM((1, groups * tok), jnp.int32),
            pltpu.VMEM((1, groups * tok), jnp.int32),
            pltpu.VMEM((tok, 128), F32),
            pltpu.VMEM((1, groups * tok), F32),
            pltpu.VMEM((1, groups * tok), F32),
        ],
        after,
        16,
        2 * blocks * groups * tok * tok * HD,
        2 * (groups + 2 * blocks) * tok * HD,
        blocks * groups * tok * tok // 2,
    )
    return results[:groups], results[groups], results[groups + 1]


def attend_backward(place, docs, slope, q, kv, others, grads, ot, lse, groups, cols, tok, after):
    blocks = groups * cols
    operands = (place, docs, slope, *q, *kv, *others, *grads, ot, lse)
    out_shape = [jax.ShapeDtypeStruct((tok, HD), BF16)] * groups + [
        jax.ShapeDtypeStruct((groups, 2, tok, HD), F32)
    ]
    if cols > 1:
        out_shape.append(jax.ShapeDtypeStruct((cols - 1, groups, 2, tok, HD), BF16))
    results = call(
        functools.partial(backward_kernel, groups, cols, tok, len(after)),
        "attend_backward",
        out_shape,
        [SMEM] * 3 + [VMEM] * (len(operands) - 3),
        operands,
        [
            pltpu.VMEM((groups * tok, HD), BF16),
            pltpu.VMEM((blocks, tok, HD), BF16),
            pltpu.VMEM((blocks, tok, HD), BF16),
            pltpu.VMEM((blocks, HD, tok), BF16),
            pltpu.VMEM((groups * tok, HD), BF16),
            pltpu.VMEM((1, groups * tok), jnp.int32),
            pltpu.VMEM((1, groups * tok), jnp.int32),
            pltpu.VMEM((tok, 128), F32),
            pltpu.VMEM((1, groups * tok), F32),
            pltpu.VMEM((HD, groups * tok), F32),
        ],
        after,
        24,
        14 * 10**9 * COST,
    )
    return results[:groups], results[groups], (results[groups + 1] if cols > 1 else None)


def rows_of(ref, part, size):
    return ref[pl.ds(pl.multiple_of(part * size, 16), size)]


def norm_rows(values):
    mean = jnp.mean(values, axis=-1, keepdims=True)
    centered = values - mean
    spread = jnp.mean(centered * centered, axis=-1, keepdims=True)
    return centered * lax.rsqrt(spread + norm_eps)


def mix_kernel(heads, n_after, place_ref, w_ref, *refs):
    pieces, out_ref, att_ref = refs[:heads], refs[heads + n_after], refs[heads + n_after + 1]
    for x in range(heads):
        head = place_ref[0] ^ x
        att_ref[:, pl.ds(pl.multiple_of(head * HD, HD), HD)] = pieces[x][...]
    out_ref[...] = mm(att_ref[...], w_ref[...]).astype(BF16)


def mix_heads(place, w_out, pieces, after):
    tok, heads = pieces[0].shape[0], len(pieces)
    return call(
        functools.partial(mix_kernel, heads, len(after)),
        "mix_heads",
        [jax.ShapeDtypeStruct((tok, D), BF16), jax.ShapeDtypeStruct((tok, heads * HD), BF16)],
        [SMEM] + [VMEM] * (heads + 1),
        (place, w_out, *pieces),
        after=after,
        flops=2 * tok * D * heads * HD,
        moved=2 * (tok * D + D * heads * HD),
    )


def unproject_kernel(heads, n_after, place_ref, w_ref, *refs):
    dq, dkv = refs[:heads], refs[heads : 2 * heads]
    out_ref, sum_ref, wide_s = refs[2 * heads + n_after :]
    for x in range(heads):
        head = place_ref[0] ^ x
        lanes = pl.ds(pl.multiple_of(head * HD, HD), HD)
        wide_s[0, :, lanes] = dq[x][...]
        wide_s[1, :, lanes] = dkv[x][0]
        wide_s[2, :, lanes] = dkv[x][1]
    total = mm(wide_s[0], w_ref[0], NT)
    for j in (1, 2):
        total = total + mm(wide_s[j], w_ref[j], NT)
    out_ref[...] = total.astype(BF16)
    sum_ref[0:1] = jnp.sum(wide_s[0].astype(F32), axis=0, keepdims=True)
    sum_ref[1:2] = jnp.sum(wide_s[2].astype(F32), axis=0, keepdims=True)


def unproject(place, w_qkv, dq, dkv, after):
    tok, heads = dq[0].shape[0], len(dq)
    return call(
        functools.partial(unproject_kernel, heads, len(after)),
        "unproject",
        [jax.ShapeDtypeStruct((tok, D), BF16), jax.ShapeDtypeStruct((2, heads * HD), F32)],
        [SMEM] + [VMEM] * (2 * heads + 1),
        (place, w_qkv, *dq, *dkv),
        [pltpu.VMEM((3, tok, heads * HD), BF16)],
        after=after,
        flops=6 * tok * D * heads * HD,
        moved=2 * (tok * D + 3 * D * heads * HD),
    )


def project_kernel(heads, place_ref, x_ref, gain_ref, shift_ref, w_ref, bias_ref, *refs):
    normed_ref, half_ref, q_refs, kv_refs = refs[0], refs[1], refs[2 : 2 + heads], refs[2 + heads : -1]
    out_s = refs[-1]
    normed = norm_rows(x_ref[...].astype(F32)) * gain_ref[0:1] + shift_ref[0:1]
    normed = normed.astype(BF16)
    normed_ref[...] = normed
    half_ref[...] = rows_of(normed_ref, place_ref[3], half_ref.shape[0])
    for j in range(3):
        product = mm(normed, w_ref[j])
        if j == 0:
            product = (product + bias_ref[0:1]) * score_scale
        if j == 2:
            product = product + bias_ref[1:2]
        product = product.astype(BF16)
        for h in range(heads):
            out_s[h, j] = product[:, h * HD : (h + 1) * HD]
    for x in range(heads):
        head = place_ref[0] ^ x
        q_refs[x][...] = out_s[head, 0]
        kv_refs[x][...] = out_s[head, 1:3]


def project(place, inputs, gain, shift, w_qkv, qv_bias):
    tok = inputs.shape[0]
    heads = w_qkv.shape[2] // HD
    out_shape = (
        [jax.ShapeDtypeStruct((tok, D), BF16), jax.ShapeDtypeStruct((tok // 2, D), BF16)]
        + [jax.ShapeDtypeStruct((tok, HD), BF16)] * heads
        + [jax.ShapeDtypeStruct((2, tok, HD), BF16)] * heads
    )
    results = call(
        functools.partial(project_kernel, heads),
        "project",
        out_shape,
        [SMEM] + [VMEM] * 5,
        (place, inputs, gain, shift, w_qkv, qv_bias),
        [pltpu.VMEM((heads, 3, tok, HD), BF16)],
    )
    return results[0], results[1], results[2 : 2 + heads], results[2 + heads :]


def middle_kernel(n_after, place_ref, x_ref, part_ref, other_ref, bias_ref, gain_ref, shift_ref, *refs):
    mixed_ref, normed_ref, half_ref = refs[n_after:]
    parts = part_ref[...].astype(F32) + other_ref[...].astype(F32)
    mixed = x_ref[...].astype(F32) + parts + bias_ref[0:1]
    mixed_ref[...] = mixed
    normed_ref[...] = (norm_rows(mixed) * gain_ref[1:2] + shift_ref[1:2]).astype(BF16)
    half_ref[...] = rows_of(normed_ref, place_ref[3], half_ref.shape[0])


def middle(place, inputs, part, other, out_bias, gain, shift, after=()):
    tok = inputs.shape[0]
    return call(
        functools.partial(middle_kernel, len(after)),
        "middle",
        [
            jax.ShapeDtypeStruct((tok, D), F32),
            jax.ShapeDtypeStruct((tok, D), BF16),
            jax.ShapeDtypeStruct((tok // 2, D), BF16),
        ],
        [SMEM] + [VMEM] * 6,
        (place, inputs, part, other, out_bias, gain, shift),
        after=after,
    )


def hidden_kernel(place_ref, normed_ref, half_ref, w_ref, bias_ref, grad_ref, *refs):
    act_sent, grad_sent, act_mine, grad_mine, back_ref, sum_ref = refs
    near, (tok, width) = place_ref[1] % 2, act_mine.shape
    grad_sent[tok:] = half_ref[...]
    total = None
    for act_ref, out_ref, side in ((act_sent, grad_sent, 1 - near), (act_mine, grad_mine, near)):
        cut = pl.ds(pl.multiple_of(side * width, 128), width)
        u = mm(normed_ref[...], w_ref[:, cut]) + bias_ref[:, cut]
        square = u * u
        bend = jnp.tanh(u * (gelu_slope + gelu_slope * 0.044715 * square))
        half = 0.5 + 0.5 * bend
        act_ref[...] = (u * half).astype(BF16)
        lean = u * (0.5 - 0.5 * bend * bend)
        rise = half + lean * (gelu_slope + (3 * 0.044715 * gelu_slope) * square)
        grad = (rise * grad_ref[:, cut]).astype(BF16)
        out_ref[:tok] = grad
        sum_ref[:, cut] = column_sum(grad.astype(F32))
        back = mm(grad, w_ref[:, cut], NT)
        total = back if total is None else total + back
    back_ref[...] = total.astype(BF16)


def hidden_units(place, normed, half, w_up, up_bias, grad_active, after=()):
    tok, total = normed.shape[0], w_up.shape[1]
    assert total // 2 == D
    act_sent, grad_sent, act_mine, grad_mine, back, sums = call(
        hidden_kernel,
        "hidden_units",
        [
            jax.ShapeDtypeStruct((tok, total // 2), BF16),
            jax.ShapeDtypeStruct((tok + tok // 2, total // 2), BF16),
            jax.ShapeDtypeStruct((tok, total // 2), BF16),
            jax.ShapeDtypeStruct((tok, total // 2), BF16),
            jax.ShapeDtypeStruct((tok, D), BF16),
            jax.ShapeDtypeStruct((1, total), F32),
        ],
        [SMEM] + [VMEM] * 5,
        (place, normed, half, w_up, up_bias, grad_active),
        room=16,
    )
    return act_mine, act_sent, grad_mine, grad_sent, back, sums


def column_sum(values):
    return jnp.sum(values, axis=0, keepdims=True)


def norm_back(values, grad, gain):
    mean = jnp.mean(values, axis=-1, keepdims=True)
    centered = values - mean
    scale = lax.rsqrt(jnp.mean(centered * centered, axis=-1, keepdims=True) + norm_eps)
    normed = centered * scale
    inner = grad * gain
    along = jnp.mean(inner * normed, axis=-1, keepdims=True)
    back = scale * (inner - jnp.mean(inner, axis=-1, keepdims=True) - normed * along)
    return back, column_sum(grad * normed), column_sum(grad)


def turn_kernel(heads, n_after, place_ref, mixed_ref, part_ref, other_ref, low_ref, gain_ref, w_ref, *refs):
    mid_ref, low_out_ref, sum_ref = refs[n_after : n_after + 3]
    pieces, head_s = refs[n_after + 3 : -1], refs[-1]
    grad = part_ref[...].astype(F32) + other_ref[...].astype(F32)
    back, gain_sum, shift_sum = norm_back(mixed_ref[...], grad, gain_ref[1:2])
    low_in = low_ref[...].astype(F32)
    mid = low_in + back
    mid_ref[...] = mid
    low = mid.astype(BF16)
    low_out_ref[...] = low
    sum_ref[0:1] = gain_sum
    sum_ref[1:2] = shift_sum
    sum_ref[2:3] = jnp.sum(low.astype(F32), axis=0, keepdims=True)
    sum_ref[3:4] = jnp.sum(low_in, axis=0, keepdims=True)
    product = mm(low, w_ref[...], NT).astype(BF16)
    for h in range(heads):
        head_s[h] = product[:, h * HD : (h + 1) * HD]
    for x in range(heads):
        pieces[x][...] = head_s[place_ref[0] ^ x]


def turn_back(place, mixed, part, other, cotangent, gain, w_out, after=()):
    tok, heads = mixed.shape[0], w_out.shape[0] // HD
    results = call(
        functools.partial(turn_kernel, heads, len(after)),
        "turn_back",
        [
            jax.ShapeDtypeStruct((tok, D), F32),
            jax.ShapeDtypeStruct((tok, D), BF16),
            jax.ShapeDtypeStruct((4, D), F32),
        ]
        + [jax.ShapeDtypeStruct((tok, HD), BF16)] * heads,
        [SMEM] + [VMEM] * 6,
        (place, mixed, part, other, cotangent, gain, w_out),
        [pltpu.VMEM((heads, tok, HD), BF16)],
        after=after,
    )
    return results[0], results[1], results[2], results[3:]


def last_kernel(n_after, x_ref, part_ref, other_ref, mid_ref, gain_ref, sums_ref, units_ref, heads_ref, *refs):
    out_ref, small_ref = refs[n_after:]
    grad = part_ref[...].astype(F32) + other_ref[...].astype(F32)
    back, gain_sum, shift_sum = norm_back(x_ref[...].astype(F32), grad, gain_ref[0:1])
    out_ref[...] = mid_ref[...] + back
    small_ref[0:4] = sums_ref[...]
    small_ref[4:5] = gain_sum
    small_ref[5:6] = shift_sum
    small_ref[6:7, : heads_ref.shape[1]] = heads_ref[0:1]
    small_ref[6:7, heads_ref.shape[1] :] = heads_ref[1:2]
    for k in range(units_ref.shape[1] // D):
        small_ref[7 + k : 8 + k] = units_ref[:, k * D : (k + 1) * D]


def last_rows(inputs, part, other, grad_mid, gain, sums, unit_sums, head_sums, after=()):
    tok = inputs.shape[0]
    return call(
        functools.partial(last_kernel, len(after)),
        "last_rows",
        [
            jax.ShapeDtypeStruct((tok, D), F32),
            jax.ShapeDtypeStruct((7 + unit_sums.shape[1] // D, D), F32),
        ],
        [VMEM] * 8,
        (inputs, part, other, grad_mid, gain, sums, unit_sums, head_sums),
        after=after,
    )


def feed_kernel(n_after, place_ref, mine_ref, sent_ref, w_ref, *refs):
    near, half = place_ref[1] % 2, mine_ref.shape[1]
    total = mm(mine_ref[...], rows_of(w_ref, near, half))
    total = total + mm(sent_ref[...], rows_of(w_ref, 1 - near, half))
    refs[n_after][...] = total.astype(BF16)


def feed(place, mine, sent, w_down, after):
    return call(
        functools.partial(feed_kernel, len(after)),
        "feed",
        [jax.ShapeDtypeStruct((mine.shape[0], D), BF16)],
        [SMEM] + [VMEM] * 3,
        (place, mine, sent, w_down),
        after=after,
    )[0]


def early_kernel(low_ref, w_ref, out_ref):
    out_ref[...] = mm(low_ref[...], w_ref[...], NT)


def early_grad(cotangent, w_down):
    return call(
        early_kernel,
        "early_grad",
        [jax.ShapeDtypeStruct((cotangent.shape[0], w_down.shape[0]), F32)],
        [VMEM] * 2,
        (cotangent, w_down),
    )[0]


def pair_grad_kernel(extra, halves, n_after, place_ref, rows_ref, units_ref, near_ref, *refs):
    near_rows, refs = refs[: 1 + halves], refs[1 + halves :]
    more, refs = refs[: 2 * extra], refs[2 * extra + n_after :]
    sent_ref, kept_ref, rows_s = refs
    dp, mp = place_ref[2], place_ref[3]
    tok, width = units_ref.shape
    if halves:
        half = near_rows[0].shape[0]
        for k in range(2):
            rows_s[pl.ds(pl.multiple_of((mp ^ k) * half, 16), half)] = near_rows[k][...]
    else:
        rows_s = near_rows[0]
    step = sent_ref.shape[0]
    for k, out_ref in ((1, sent_ref), (0, kept_ref)):
        cut = pl.ds(pl.multiple_of((dp ^ k) * step, 128), step)
        total = mm(rows_ref[:, cut], units_ref[...], TN) + mm(rows_s[:, cut], near_ref[:tok], TN)
        out_ref[:, :width] = total.astype(out_ref.dtype)
        if extra:
            out_ref[:, width:] = mm(more[0][:, cut], more[1][...], TN).astype(out_ref.dtype)


def pair_grad(place, rows, near_rows, units, near_units, more, after):
    tok, width = units.shape
    total = width + (more[1].shape[1] if more else 0)
    return call(
        functools.partial(pair_grad_kernel, int(bool(more)), len(near_rows) - 1, len(after)),
        "pair_grad",
        [jax.ShapeDtypeStruct((D // 2, total), BF16), jax.ShapeDtypeStruct((D // 2, total), F32)],
        [SMEM] + [VMEM] * (3 + len(near_rows) + len(more)),
        (place, rows, units, near_units, *near_rows, *more),
        [pltpu.VMEM((tok, D), BF16)],
        after=after,
    )


def head_grad_kernel(groups, n_after, place_ref, *refs):
    own_ref, mine, other = refs[0], refs[1:groups], refs[groups : 2 * groups - 1]
    dq, dkv = refs[2 * groups - 1 : 3 * groups - 1], refs[3 * groups - 1 : 4 * groups - 1]
    sent_ref, kept_ref, rows_s, grads_s = refs[4 * groups - 1 + n_after :]
    dp, mp = place_ref[2], place_ref[3]
    tok = own_ref.shape[0]
    half = tok // 2
    for x in range(groups):
        if x == 0:
            rows_s[0:tok] = own_ref[...]
        else:
            rows_s[pl.ds(pl.multiple_of(x * tok + mp * half, 16), half)] = mine[x - 1][...]
            rows_s[pl.ds(pl.multiple_of(x * tok + (1 - mp) * half, 16), half)] = other[x - 1][...]
        rows = slice(x * tok, (x + 1) * tok)
        grads_s[rows, :HD] = dq[x][...]
        grads_s[rows, HD : 2 * HD] = dkv[x][0]
        grads_s[rows, 2 * HD :] = dkv[x][1]
    step = sent_ref.shape[0]
    for k, out_ref in ((1, sent_ref), (0, kept_ref)):
        cut = pl.ds(pl.multiple_of((dp ^ k) * step, 128), step)
        out_ref[...] = mm(rows_s[:, cut], grads_s[...], TN).astype(out_ref.dtype)


def head_grad(place, own, mine, other, dq, dkv, after):
    tok, groups = own.shape[0], len(dq)
    return call(
        functools.partial(head_grad_kernel, groups, len(after)),
        "head_grad",
        [jax.ShapeDtypeStruct((D // 2, 3 * HD), BF16), jax.ShapeDtypeStruct((D // 2, 3 * HD), F32)],
        [SMEM] + [VMEM] * (4 * groups - 1),
        (place, own, *mine, *other, *dq, *dkv),
        [pltpu.VMEM((groups * tok, D), BF16), pltpu.VMEM((groups * tok, 3 * HD), BF16)],
        after=after,
        flops=2 * groups * tok * D * 3 * HD,
        moved=2 * groups * tok * (D + 3 * HD),
    )


def sum_kernel(groups, n_there, n_after, own_ref, *refs):
    there, outs = refs[:n_there], refs[n_there + n_after :]
    for x in range(groups):
        for j in range(2):
            total = own_ref[x, j]
            for ref in there:
                total = total + ref[0, x, j].astype(F32)
            outs[x][j] = total.astype(BF16)


def sum_columns(own, there, after):
    groups, _, tok, _ = own.shape
    return call(
        functools.partial(sum_kernel, groups, len(there), len(after)),
        "sum_columns",
        [jax.ShapeDtypeStruct((2, tok, HD), BF16)] * groups,
        [VMEM] * (1 + len(there)),
        (own, *there),
        after=after,
        moved=10 * own.size,
    )


def fold_kernel(outer, inner, n_after, now_ref, kept_ref, there_ref, *refs):
    mine_ref, sent_ref = refs[n_after:]
    for o in range(outer):
        for k, ref in ((0, mine_ref), (1, sent_ref)):
            at = pl.ds(pl.multiple_of((2 * o + (now_ref[0] ^ k)) * inner, 16), inner)
            total = kept_ref[at] + there_ref[at].astype(F32)
            ref[o * inner : (o + 1) * inner] = total.astype(ref.dtype)


def fold(now, kept, there, inner, after=()):
    rows, width = kept.shape
    return call(
        functools.partial(fold_kernel, rows // (2 * inner), inner, len(after)),
        "fold",
        [jax.ShapeDtypeStruct((rows // 2, width), F32), jax.ShapeDtypeStruct((rows // 2, width), BF16)],
        [SMEM, VMEM, VMEM],
        (now, kept, there),
        after=after,
        moved=9 * kept.size,
    )


def both_halves(near, mine, there, out_ref, half):
    out_ref[:, pl.ds(pl.multiple_of(near * half, 128), half)] = mine
    out_ref[:, pl.ds(pl.multiple_of((1 - near) * half, 128), half)] = there


def finish_kernel(width, n_after, place_ref, mine_ref, there_ref, h_ref, h_there_ref, d_ref, d_there_ref, *refs):
    u_ref, u_there_ref, refs = refs[0], refs[1], refs[2 + n_after :]
    gain_ref, shift_ref, heads_ref, units_ref, bias_ref, qkv_ref, down_ref, up_ref, out_ref = refs
    total = mine_ref[...] + there_ref[...]
    gain_ref[0:1], gain_ref[1:2] = total[4:5], total[0:1]
    shift_ref[0:1], shift_ref[1:2] = total[5:6], total[1:2]
    heads_ref[0:1], heads_ref[1:2] = total[6:7, :width], total[6:7, width:]
    for k in range(units_ref.shape[1] // D):
        units_ref[:, k * D : (k + 1) * D] = total[7 + k : 8 + k]
    bias_ref[...] = total[2:4]
    rows = h_ref[...] + h_there_ref[...].astype(F32)
    for h in range(width // HD):
        for j in range(3):
            at = (3 * h + j) * HD
            qkv_ref[j, :, h * HD : (h + 1) * HD] = rows[:, at : at + HD]
    near, half = place_ref[1] % 2, d_ref.shape[1]
    both_halves(near, d_ref[...], d_there_ref[...].astype(F32), down_ref, half)
    there = u_there_ref[...].astype(F32)
    both_halves(near, u_ref[:, :half], there[:, :half], up_ref, half)
    out_ref[...] = u_ref[:, half:] + there[:, half:]


def five_and_rest(arrays):
    return [arrays[:5], *arrays[5:]]


def finish(place, small, small_there, heads, heads_there, down, down_there, up, up_there, width, after):
    rows = heads.shape[0]
    shapes = [(2, D), (2, D), (2, width), (1, (small.shape[0] - 7) * D), (2, D)]
    shapes += [(3, rows, width), (rows, 2 * down.shape[1]), (rows, 2 * down.shape[1]), (rows, width)]
    return call(
        functools.partial(finish_kernel, width, len(after)),
        "finish",
        [jax.ShapeDtypeStruct(shape, F32) for shape in shapes],
        [SMEM] + [VMEM] * 8,
        (place, small, small_there, heads, heads_there, down, down_there, up, up_there),
        after=after,
    )


def pass_on(*refs):
    pass


def gate(x, *after, weight=0):
    return pl.pallas_call(
        pass_on,
        out_shape=jax.ShapeDtypeStruct(x.shape, x.dtype),
        in_specs=[ANY] * (1 + len(after)),
        out_specs=ANY,
        input_output_aliases={0: 0},
        cost_estimate=pl.CostEstimate(flops=weight, bytes_accessed=0, transcendentals=0),
        name="gate",
    )(x, *after)


def swap(x, axis, size, bit):
    return lax.ppermute(x, axis, [(i, i ^ bit) for i in range(size)])


def bits(size):
    return [1 << i for i in range(size.bit_length() - 1)]


def sum_over(vector, axes):
    for axis, size in axes:
        for bit in bits(size):
            vector = vector + swap(vector, axis, size, bit)
    return vector


def body(
    sizes,
    inputs,
    doc_lengths,
    slopes,
    norm_gain,
    norm_bias,
    w_qkv,
    qv_bias,
    w_out,
    w_up,
    up_bias,
    w_down,
    out_bias,
    cotangent,
):
    n_dp, groups, cols = sizes
    tok = inputs.shape[0]
    width = slopes.shape[0] * HD
    me, col = lax.axis_index("sg"), lax.axis_index("sr")
    mp, dp, near = lax.axis_index("mp"), lax.axis_index("dp"), lax.axis_index("sr") % 2
    place = jnp.stack([me, col, dp, mp]).astype(jnp.int32)

    def deal(pieces):
        return [pieces[x] if x == 0 else swap(pieces[x], "sg", groups, x) for x in range(groups)]

    def half_rows(x):
        return lax.dynamic_slice_in_dim(x, mp * (tok // 2), tok // 2, 0)

    normed_one, one_half, q, kv = project(place, inputs, norm_gain, norm_bias, w_qkv, qv_bias)
    grad_active = early_grad(cotangent, w_down)
    kv = deal(kv)
    others = [[swap(kv[0], "sr", cols, s)] for s in range(1, cols)]
    turn = (grad_active,)
    for x in range(1, groups):
        kv[x] = gate(kv[x], *turn, *[column[-1] for column in others])
        turn = ()
        for s in range(1, cols):
            others[s - 1].append(swap(kv[x], "sr", cols, s))
    others = [piece for column in others for piece in column]
    q = deal([q[0]] + [gate(piece, kv[groups - 2]) for piece in q[1:]])
    others[-1] = gate(others[-1], weight=5 * HOLD)
    outs, ot, lse = attend_forward(place, doc_lengths, slopes, q, kv, others, groups, cols, tok, [])
    low_near = swap(gate(cotangent, q[1]), "sr", cols, 1)
    low_near = gate(low_near, outs[0], weight=HOLD)
    outs = deal(outs)
    one_half = gate(one_half, outs[groups - 1])
    far = swap(one_half, "sg", groups, 2)
    attn_part, attended = mix_heads(place, w_out, outs, [low_near])
    mixed, normed_two, two_half = middle(
        place,
        inputs,
        attn_part,
        swap(attn_part, "mp", 2, 1),
        out_bias,
        norm_gain,
        norm_bias,
        [],
    )

    half_units = w_up.shape[1] // 2
    active, active_sent, grad_hidden, hidden_sent, back_two, unit_sums = hidden_units(
        place, normed_two, two_half, w_up, up_bias[None], grad_active
    )
    active_near = swap(active_sent, "sr", cols, 1)
    hidden_near = swap(hidden_sent, "sr", cols, 1)
    far = gate(far, back_two, weight=HOLD)
    grad_mid, grad_mid_low, row_sums, pieces = turn_back(
        place,
        mixed,
        back_two,
        swap(back_two, "mp", 2, 1),
        cotangent,
        norm_gain,
        w_out,
        [far],
    )
    grads = deal(pieces)

    down_sent, down_kept = pair_grad(
        place,
        cotangent,
        [low_near],
        active,
        active_near,
        (),
        [pieces[3]],
    )
    down_there = swap(down_sent, "dp", 2, 1)
    far = gate(far, down_sent, *grads[1:])
    last = swap(far, "sg", groups, 1)
    one_half = gate(one_half, far)
    beside = swap(one_half, "sg", groups, 1)
    dq, dkv, dkv_other = attend_backward(
        place,
        doc_lengths,
        slopes,
        q,
        kv,
        others,
        grads,
        ot,
        lse,
        groups,
        cols,
        tok,
        [down_sent, one_half],
    )
    dkv_there = [swap(dkv_other[s - 1 : s], "sr", cols, s) for s in range(1, cols)]
    beside = gate(beside, dq[0], weight=HOLD)
    last = gate(last, dq[0], weight=HOLD)
    hidden_near = gate(hidden_near, dq[0], weight=HOLD)
    dq_mine = [dq[0], gate(dq[1], beside), gate(dq[2], last), gate(dq[3], hidden_near)]
    dq = deal(dq_mine)
    two_near = hidden_near[tok:]
    two_near_mp = swap(two_near, "mp", 2, 1)

    rows_here = D // (2 * groups * cols)
    stages = [("sr", cols, 2 * bit) for bit in bits(cols // 2)]
    stages += [("sg", groups, bit) for bit in bits(groups)]

    def now(axis, bit):
        return ((lax.axis_index(axis) // bit) % 2).astype(jnp.int32).reshape(1)

    def stage(k, kept, there, *after):
        axis, size, bit = stages[k]
        kept, sent = fold(now(axis, bit), kept, there, 2 * rows_here, after)
        return kept, sent, swap(sent, axis, size, bit)

    last_turn = len(stages) - 1
    up_sent, up_kept = pair_grad(
        place,
        normed_two,
        [two_near, two_near_mp],
        grad_hidden,
        hidden_near,
        (grad_mid_low, attended),
        [dq_mine[3]],
    )
    down_there = gate(down_there, up_sent)
    for k in range(last_turn):
        down_kept, down_sent, down_there = stage(k, down_kept, down_there)
    up_there = swap(up_sent, "dp", 2, 1)
    dq = [dq[0]] + [gate(piece, down_sent, weight=HOLD) for piece in dq[1:]]
    dkv_there = [gate(piece, *dq[1:], weight=HOLD) for piece in dkv_there]
    rows_mine = [gate(piece, *dq[1:]) for piece in (beside, far, last)]
    rows_mp = [swap(piece, "mp", 2, 1) for piece in rows_mine]
    dkv_mine = sum_columns(dkv, dkv_there, rows_mine)
    dkv_mine = [dkv_mine[0]] + [gate(dkv_mine[x], rows_mp[x - 1]) for x in range(1, groups)]
    dkv = deal(dkv_mine)

    head_sent, head_kept = head_grad(
        place, normed_one, rows_mine, rows_mp, dq_mine, dkv_mine, []
    )
    ffn_part = feed(place, active, active_sent, w_down, [head_sent])
    down_there = gate(down_there, head_sent)
    down_kept, down_sent, down_there = stage(last_turn, down_kept, down_there)
    up_there = gate(up_there, down_sent, ffn_part)
    for k in range(last_turn):
        up_kept, up_sent, up_there = stage(k, up_kept, up_there)
    dkv = [dkv[0]] + [gate(piece, up_sent, weight=HOLD) for piece in dkv[1:]]
    head_there = swap(gate(head_sent, up_sent), "dp", 2, 1)
    back_part, head_sums = unproject(place, w_qkv, dq, dkv, [])
    back_there = swap(back_part, "mp", 2, 1)
    head_there = gate(head_there, back_part)
    down_there = gate(down_there, back_part)

    kept = (head_kept + head_there.astype(F32)).reshape(groups, cols // 2, 2 * rows_here, 3 * HD)
    for bit in bits(cols // 2):
        here = now("sr", 2 * bit)[0]
        view = kept.reshape(groups, -1, 2, 2 * rows_here, 3 * HD)
        sent = lax.dynamic_index_in_dim(view, 1 - here, 2, keepdims=False).astype(BF16)
        kept = lax.dynamic_index_in_dim(view, here, 2, keepdims=False)
        kept = kept + swap(sent, "sr", cols, 2 * bit).astype(F32)
    kept = kept.reshape(groups, 2, rows_here, 3 * HD)
    low = kept.astype(BF16)
    pieces = [lax.dynamic_index_in_dim(low, me ^ x, 0, keepdims=False) for x in range(groups)]
    pieces_sent = pieces
    pieces = deal(pieces)
    up_there = gate(up_there, pieces_sent[1], weight=HOLD)
    up_kept, up_sent, up_there = stage(last_turn, up_kept, up_there)
    grad_inputs, small = last_rows(
        inputs,
        back_part,
        gate(back_there, up_sent),
        grad_mid,
        norm_gain,
        row_sums,
        unit_sums,
        head_sums,
        [],
    )

    def with_near(x):
        sent = lax.dynamic_index_in_dim(x, 1 - near, 0, keepdims=False).astype(BF16)
        mine = lax.dynamic_index_in_dim(x, near, 0, keepdims=False)
        return sent, mine, swap(sent, "sr", cols, 1)

    def add_with_near(kept, there):
        if rows_here % 16:
            return with_near((kept + there.astype(F32)).reshape(2, rows_here, -1))
        mine, sent = fold(now("sr", 1), kept, there, rows_here)
        return sent, mine, swap(sent, "sr", cols, 1)

    _, down_mine, down_there = add_with_near(down_kept, gate(down_there, small))
    ffn_part = gate(ffn_part, small)
    small = sum_over(small, (("sr", cols), ("dp", n_dp)))
    ffn_other = gate(swap(ffn_part, "mp", 2, 1), small).astype(F32)
    outputs = (mixed + ffn_part.astype(F32) + ffn_other + out_bias[1]).astype(BF16)

    far_bits = bits(groups)
    small_there = swap(small, "sg", groups, far_bits[0])

    pieces = [pieces[0]] + [gate(piece, up_sent) for piece in pieces[1:]]
    pieces[0] = lax.dynamic_index_in_dim(kept, me, 0, keepdims=False)
    heads_all = jnp.concatenate(
        [
            sum(jnp.where((me ^ x) == h, pieces[x].astype(F32), 0.0) for x in range(groups))
            for h in range(groups)
        ],
        2,
    )
    head_sent, head_mine, head_near = with_near(heads_all)
    up_sent, up_mine, up_there = add_with_near(up_kept, gate(up_there, head_sent))
    for bit in far_bits[1:]:
        small = small + gate(small_there, up_sent)
        small_there = swap(small, "sg", groups, bit)
    sums, grad_qkv, grad_down, grad_up, grad_out = five_and_rest(
        finish(
            place,
            small,
            small_there,
            head_mine,
            head_near,
            down_mine,
            down_there,
            up_mine,
            up_there,
            width,
            [outputs],
        )
    )
    grad_gain, grad_shift, grad_qv_bias, grad_up_bias, grad_bias = sums

    return (
        outputs,
        grad_inputs,
        grad_gain,
        grad_shift,
        grad_qkv,
        grad_qv_bias,
        grad_out.T,
        grad_up,
        grad_up_bias.reshape(-1),
        grad_down.T,
        grad_bias,
    )


def solution(mesh):
    n_dp, n_seq, n_mp = mesh.shape["dp"], mesh.shape["seq"], mesh.shape["mp"]
    groups = 4
    cols = n_seq // groups
    inner = Mesh(mesh.devices.reshape(n_dp, groups, cols, n_mp), ("dp", "sg", "sr", "mp"))
    rows = ("dp", "sg", "sr")
    return jax.shard_map(
        functools.partial(body, (n_dp, groups, cols)),
        mesh=inner,
        in_specs=(
            P(rows, None),
            P("dp", None),
            P("mp"),
            P(),
            P(),
            P(None, None, "mp"),
            P(None, "mp"),
            P("mp", None),
            P(None, "mp"),
            P("mp"),
            P("mp", None),
            P(),
            P(rows, None),
        ),
        out_specs=(
            P(rows, None),
            P(rows, None),
            P(),
            P(),
            P(None, rows, "mp"),
            P(None, "mp"),
            P("mp", rows),
            P(rows, "mp"),
            P("mp"),
            P("mp", rows),
            P(),
        ),
        check_vma=False,
    )
```
